32 devices in a mesh: groups: 2 (over y), row: 4 (over z), col: 2 (over x), depth: 2 (over core).
Axes of the slice: x: 2, y: 2, z: 4, core: 2. Of those that a mesh axis runs over, the one named last changes fastest.
Arguments:
- environment: bfloat16 [4, 2, 2048, 2048], P(('groups', 'depth'), None, 'row', 'col'), parts along dimension 0, may hold values from -6 to 6
- site_tensor: bfloat16 [4, 2048, 2, 2048], P('groups', 'row', None, 'col'), parts along dimension 0, may hold values from -0.09375 to 0.09375
- mpo: float32 [4, 2, 2, 2], P('groups'), parts along dimension 0, may hold values from -3 to 3
Outputs:
- new_environment: float32 [4, 2, 2048, 2048], P('groups', None, 'row', ('col', 'depth')), parts along dimension 0
The draws below stay inside these ranges and needn't reach their ends.
There are 2 independent parts, one for each index of `groups`. The reference program is written for one: setup_inputs(seed, part) draws one part's arguments, and reference() takes and returns one part's arrays. A program takes and returns all parts, laid end to end along the dimension named above; each array names one. Nothing has to cross between parts.
All inputs are finite; a program needn't handle non-finite values.
Results may differ from the reference program's by a relative error of at most 0.003.
Values may be sent and summed in bfloat16 or wider, within the bound.
No kernel may reach another device: no remote copies, remote signals or barrier semaphores. Data moves between devices by JAX's collectives and lax.ppermute only.
A program may use at most 128 MiB of HBM per device.

```python
from functools import partial
import jax
import jax.numpy as jnp
from jax import lax

BOND = 2048
PHYS = 2
MPO = 2


def levels(own_key, dims, pieces, smallest, high):
    gain = 1.0
    for position, shards_of in pieces:
        heights = jax.random.uniform(jax.random.fold_in(jax.random.fold_in(own_key, 6), position), (shards_of,), jnp.float32, smallest / len(pieces), high / len(pieces))
        gain = gain * jnp.repeat(jnp.exp(heights), dims[position] // shards_of).reshape((-1,) + (1,) * (len(dims) - 1 - position))
    return gain


def centred(stream_key, extent, width, limit, shards=(), held_as=jnp.bfloat16):
    values = width * jax.random.normal(stream_key, extent, jnp.float32)
    if shards:
        values = values * levels(stream_key, extent, shards, -0.22, 0.18)
    return jnp.clip(values, -limit, limit).astype(held_as)


def setup_inputs(seed: int = 0, part: int = 0) -> dict:
    keys = jax.random.split(jax.random.key(seed), 4)
    part_splits = jax.random.split(jax.random.fold_in(keys[3], part), 4)
    return {
        "environment": centred(part_splits[0], (MPO, 2, BOND, BOND), 1.0, 6.0, ((0, 2), (2, 4), (3, 2))),
        "site_tensor": centred(part_splits[1], (PHYS, BOND, 2, BOND), (2 * BOND) ** -0.5, 0.09375, ((1, 4), (3, 2))),
        "mpo": centred(part_splits[2], (MPO, MPO, PHYS, PHYS), (MPO * PHYS) ** -0.5, 3.0, (), jnp.float32),
    }


def reference(environment, site_tensor, mpo):
    highest = lax.Precision.HIGHEST
    env_full = environment.astype(jnp.float32)
    site_full = site_tensor.astype(jnp.float32)
    site_real = site_full[:, :, 0, :]
    site_imag = site_full[:, :, 1, :]
    env_real = env_full[:, 0]
    env_imag = env_full[:, 1]
    first_mult = partial(jnp.einsum, "sxa,wac->wsxc", precision=highest)
    g_real = first_mult(site_real, env_real) + first_mult(site_imag, env_imag)
    g_imag = first_mult(site_real, env_imag) - first_mult(site_imag, env_real)
    stacked = jnp.stack([g_real, g_imag], axis=2)
    mixed = jnp.einsum("wvst,wspxc->vtpxc", mpo.astype(jnp.float32), stacked, precision=highest)
    mixed_low = lax.optimization_barrier(mixed.astype(jnp.bfloat16))
    mixed_wide = mixed_low.astype(jnp.float32)
    q_real = mixed_wide[:, :, 0]
    q_imag = mixed_wide[:, :, 1]
    second_mult = partial(jnp.einsum, "vtxc,tyc->vxy", precision=highest)
    out_real = second_mult(q_real, site_real) - second_mult(q_imag, site_imag)
    out_imag = second_mult(q_real, site_imag) + second_mult(q_imag, site_real)
    return jnp.stack([out_real, out_imag], axis=1)
```

```python
from functools import partial
import jax
import jax.numpy as jnp
from jax import lax
from jax.experimental import pallas as pl
from jax.experimental.pallas import tpu as pltpu
from jax.sharding import PartitionSpec as P

F32 = jnp.float32
BF16 = jnp.bfloat16
VMEM_BYTES = 48 * 1024 * 1024


def params(steps):
    return pltpu.CompilerParams(
        dimension_semantics=("arbitrary",) * steps, vmem_limit_bytes=VMEM_BYTES
    )


def mul(left, right):
    return jnp.dot(left, right, preferred_element_type=F32)


def mul_t(left, right):
    return lax.dot_general(left, right, (((1,), (1,)), ((), ())), preferred_element_type=F32)


def first_kernel(site_ref, own_ref, sib_ref, *rest):
    out_ref = rest[-1]
    real, imag = site_ref[0, 0], site_ref[0, 1]
    for which, env_ref in enumerate((own_ref, sib_ref)):
        env_real, env_imag = env_ref[0, 0], env_ref[0, 1]
        g_real = mul(real, env_real) + mul(imag, env_imag)
        g_imag = mul(real, env_imag) - mul(imag, env_real)
        if len(rest) == 2:
            g_real = g_real + rest[0][which, 0, 0, 0]
            g_imag = g_imag + rest[0][which, 0, 0, 1]
        out_ref[which, 0, 0, 0] = g_real
        out_ref[which, 0, 0, 1] = g_imag


def first_product(site, own, sib, total):
    phys, _, rows, depth = site.shape
    w_local, _, _, cols = own.shape
    total_spec = pl.BlockSpec((2, 1, 1, 2, rows, cols), lambda s, w: (0, w, s, 0, 0, 0))
    env_spec = pl.BlockSpec((1, 2, depth, cols), lambda s, w: (w, 0, 0, 0))
    args = (site, own, sib) + (() if total is None else (total,))
    shape = (2, w_local, phys, 2, rows, cols)
    return pl.pallas_call(
        first_kernel,
        grid=(phys, w_local),
        in_specs=[pl.BlockSpec((1, 2, rows, depth), lambda s, w: (s, 0, 0, 0)), env_spec, env_spec]
        + ([] if total is None else [total_spec]),
        out_specs=total_spec,
        out_shape=jax.ShapeDtypeStruct(shape, F32),
        input_output_aliases={} if total is None else {3: 0},
        compiler_params=params(2),
        cost_estimate=pl.CostEstimate(
            flops=16 * w_local * phys * rows * depth * cols,
            bytes_accessed=32 * w_local * phys * rows * cols,
            transcendentals=0,
        ),
        name="first_product",
    )(*args)


def mix_kernel(mpo_ref, g_ref, q_ref):
    _, w_local, phys = g_ref.shape[:3]
    mpo_count = q_ref.shape[0]
    for v in range(mpo_count):
        for t in range(phys):
            total = None
            for which in range(2):
                for w in range(w_local):
                    for s in range(phys):
                        term = mpo_ref[which * w_local + w, v, s, t] * g_ref[which, w, s, 0]
                        total = term if total is None else total + term
            q_ref[v, t, 0] = total.astype(BF16)


def mix(mpo, g):
    _, w_local, phys, _, rows, cols = g.shape
    mpo_count = mpo.shape[1]
    tile = min(rows, 64)
    return pl.pallas_call(
        mix_kernel,
        grid=(2, rows // tile),
        in_specs=[
            pl.BlockSpec(memory_space=pltpu.SMEM),
            pl.BlockSpec((2, w_local, phys, 1, tile, cols), lambda p, i: (0, 0, 0, p, i, 0)),
        ],
        out_specs=pl.BlockSpec((mpo_count, phys, 1, tile, cols), lambda p, i: (0, 0, p, i, 0)),
        out_shape=jax.ShapeDtypeStruct((mpo_count, phys, 2, rows, cols), BF16),
        compiler_params=params(2),
        cost_estimate=pl.CostEstimate(
            flops=4 * w_local * phys * phys * mpo_count * 2 * rows * cols,
            bytes_accessed=g.size * 4 + mpo_count * phys * 4 * rows * cols,
            transcendentals=0,
        ),
        name="mix",
    )(mpo, g)


def second_kernel(q_ref, site_ref, wide_ref, low_ref):
    out_real, out_imag = 0.0, 0.0
    for t in range(q_ref.shape[1]):
        q_real, q_imag = q_ref[0, t, 0], q_ref[0, t, 1]
        real, imag = site_ref[t, 0], site_ref[t, 1]
        out_real += mul_t(q_real, real) - mul_t(q_imag, imag)
        out_imag += mul_t(q_real, imag) + mul_t(q_imag, real)
    wide_ref[0, 0] = out_real
    wide_ref[0, 1] = out_imag
    low_ref[0, 0] = out_real.astype(BF16)
    low_ref[0, 1] = out_imag.astype(BF16)


def second_product(q, site):
    mpo_count, phys, _, rows, cols = q.shape
    y_rows = site.shape[2]
    out_spec = pl.BlockSpec((1, 2, rows, y_rows), lambda v: (v, 0, 0, 0))
    shape = (mpo_count, 2, rows, y_rows)
    return pl.pallas_call(
        second_kernel,
        grid=(mpo_count,),
        in_specs=[
            pl.BlockSpec((1, phys, 2, rows, cols), lambda v: (v, 0, 0, 0, 0)),
            pl.BlockSpec((phys, 2, y_rows, cols), lambda v: (0, 0, 0, 0)),
        ],
        out_specs=[out_spec, out_spec],
        out_shape=[jax.ShapeDtypeStruct(shape, F32), jax.ShapeDtypeStruct(shape, BF16)],
        compiler_params=params(1),
        cost_estimate=pl.CostEstimate(
            flops=8 * mpo_count * phys * rows * y_rows * cols,
            bytes_accessed=q.size * 2 + site.size * 2 + 12 * mpo_count * rows * y_rows,
            transcendentals=0,
        ),
        name="second_product",
    )(q, site)


def after(value, *earlier):
    return lax.optimization_barrier((value,) + earlier)[0]


def shift(value, axis, count):
    return lax.ppermute(value, axis, [(i, (i + 1) % count) for i in range(count)])


def swap(value):
    return lax.ppermute(value, "depth", [(0, 1), (1, 0)])


def on_device(environment, site_tensor, mpo):
    row_count, col_count = lax.axis_size("row"), lax.axis_size("col")
    row, col, depth = (lax.axis_index(axis) for axis in ("row", "col", "depth"))
    w_local, _, rows, half = environment.shape
    phys = site_tensor.shape[0]
    cols = half // 2
    pieces = col_count * 2
    bond = pieces * cols

    env_own = lax.dynamic_slice_in_dim(environment, depth * cols, cols, 3)
    env_sib = swap(lax.dynamic_slice_in_dim(environment, (1 - depth) * cols, cols, 3))
    mpo_mine = jnp.concatenate(
        [
            lax.dynamic_slice_in_dim(mpo, depth * w_local, w_local, 0),
            lax.dynamic_slice_in_dim(mpo, (1 - depth) * w_local, w_local, 0),
        ],
        axis=0,
    )
    planar = jnp.transpose(site_tensor.reshape(phys, rows, 2, 2, cols), (3, 0, 2, 1, 4))
    site_own = lax.dynamic_index_in_dim(planar, depth, 0, keepdims=False)

    by_col = [planar]
    travelling = site_own
    for _ in range(col_count - 1):
        travelling = shift(travelling, "col", col_count)
        sibling = swap(travelling)
        pair = jnp.stack([travelling, sibling])
        by_col.append(jnp.where(depth == 0, pair, pair[::-1]))
    site_pieces = jnp.concatenate(by_col, axis=0)

    def piece_at(index):
        there = lax.rem(col - index // 2 + col_count, col_count)
        return lax.dynamic_index_in_dim(site_pieces, there * 2 + index % 2, 0, keepdims=False)

    ring = row_count == pieces

    total = None
    if ring:
        own, sib = env_own, env_sib
        for step in range(row_count):
            block = lax.rem(row - step + row_count, row_count)
            total = first_product(piece_at(block), own, sib, total)
            if step < row_count - 1:
                own, sib = shift(own, "row", row_count), shift(sib, "row", row_count)
    else:
        own = lax.all_gather(env_own, "row", axis=2, tiled=True)
        sib = lax.all_gather(env_sib, "row", axis=2, tiled=True)
        for index in range(pieces):
            block = slice(index * cols, (index + 1) * cols)
            total = first_product(piece_at(index), own[:, :, block], sib[:, :, block], total)
    q = mix(mpo_mine, total)

    if not ring:
        site_all = lax.all_gather(site_own, "row", axis=2, tiled=True)
        parts = []
        for index in range(pieces):
            block = slice(index * cols, (index + 1) * cols)
            parts.append(second_product(q, site_all[:, :, block])[0])
        return lax.psum_scatter(
            jnp.concatenate(parts, axis=3), ("col", "depth"), scatter_dimension=3, tiled=True
        )

    axes = ("row", "col", "depth")
    place = lambda r, c, d: (r * col_count + c) * 2 + d
    chunks = 2
    y_rows = rows // chunks
    mine = col * 2 + depth
    outs = []
    for chunk in range(chunks):
        travelling = site_own[:, :, chunk * y_rows : (chunk + 1) * y_rows]
        travelling = after(travelling, own)
        out = None
        for step in range(row_count):
            target = [(r - step) % row_count for r in range(row_count)]
            wide, low = second_product(q, travelling)
            if step < row_count - 1:
                travelling = shift(travelling, "row", row_count)
            low = lax.ppermute(
                low,
                axes,
                [
                    (place(r, c, 1 - target[r] % 2), place(r, c, target[r] % 2))
                    for r in range(row_count)
                    for c in range(col_count)
                ],
            )
            wide = wide + low.astype(F32)
            low = wide.astype(BF16)
            for away in range(1, col_count):
                came = lax.ppermute(
                    low,
                    axes,
                    [
                        (
                            place(r, (target[r] // 2 + away) % col_count, target[r] % 2),
                            place(r, target[r] // 2, target[r] % 2),
                        )
                        for r in range(row_count)
                    ],
                )
                wide = wide + came.astype(F32)
            if out is None:
                out = wide
            else:
                out = jnp.where(mine == lax.rem(row - step + row_count, row_count), wide, out)
        outs.append(out)
    return jnp.concatenate(outs, axis=3)


def solution(mesh):
    placed = (
        P(("groups", "depth"), None, "row", "col"),
        P("groups", "row", None, "col"),
        P("groups", None, None, None),
    )
    return jax.shard_map(
        on_device,
        mesh=mesh,
        in_specs=placed,
        out_specs=P("groups", None, "row", ("col", "depth")),
        check_vma=False,
    )
```

```python
import jax
import jax.numpy as jnp
from jax import lax
from jax.experimental import pallas as pl
from jax.experimental.pallas import tpu as pltpu
from jax.sharding import PartitionSpec as P

F32 = jnp.float32
BF16 = jnp.bfloat16
VMEM_BYTES = 56 * 1024 * 1024


def params(steps):
    return pltpu.CompilerParams(
        dimension_semantics=("arbitrary",) * steps, vmem_limit_bytes=VMEM_BYTES
    )


def mul(left, right):
    return jnp.dot(left, right, preferred_element_type=F32)


def mul_t(left, right):
    return lax.dot_general(left, right, (((1,), (1,)), ((), ())), preferred_element_type=F32)


def first_kernel(place_ref, mpo_ref, site_ref, *refs):
    g_ref, q_ref = refs[-1], refs[-2]
    env_refs = refs[:-2]
    blocks = len(env_refs) // 2
    w_local = env_refs[0].shape[0]
    mpo_count, phys, _, rows, cols = q_ref.shape
    for which in range(2):
        for w in range(w_local):
            g_real, g_imag = None, None
            for block in range(blocks):
                piece = place_ref[block]
                depth = site_ref.shape[-1]
                real = site_ref[piece, :, 0].reshape(phys * rows, depth)
                imag = site_ref[piece, :, 1].reshape(phys * rows, depth)
                env_real = env_refs[block * 2 + which][w, 0]
                env_imag = env_refs[block * 2 + which][w, 1]
                more_real = mul(real, env_real) + mul(imag, env_imag)
                more_imag = mul(real, env_imag) + mul(imag, -env_real)
                g_real = more_real if g_real is None else g_real + more_real
                g_imag = more_imag if g_imag is None else g_imag + more_imag
            g_ref[which * w_local + w, 0] = g_real
            g_ref[which * w_local + w, 1] = g_imag
    for part in range(2):
        for v in range(mpo_count):
            for t in range(phys):
                total = None
                for w in range(2 * w_local):
                    for s in range(phys):
                        term = mpo_ref[w, v, s, t] * g_ref[w, part, s * rows : (s + 1) * rows]
                        total = term if total is None else total + term
                q_ref[v, t, part] = total.astype(BF16)


def first_product(place, mpo, site, envs, row_tile, col_tile):
    pieces, phys, _, rows, depth = site.shape
    w_local, _, _, cols = envs[0].shape
    mpo_count = mpo.shape[1]
    row_tile, col_tile = min(row_tile, rows), min(col_tile, cols)
    env_spec = pl.BlockSpec((w_local, 2, depth, col_tile), lambda i, j: (0, 0, 0, j))
    smem = pl.BlockSpec(memory_space=pltpu.SMEM)
    return pl.pallas_call(
        first_kernel,
        grid=(rows // row_tile, cols // col_tile),
        in_specs=[
            smem,
            smem,
            pl.BlockSpec((pieces, phys, 2, row_tile, depth), lambda i, j: (0, 0, 0, i, 0)),
        ]
        + [env_spec] * len(envs),
        out_specs=pl.BlockSpec(
            (mpo_count, phys, 2, row_tile, col_tile), lambda i, j: (0, 0, 0, i, j)
        ),
        out_shape=jax.ShapeDtypeStruct((mpo_count, phys, 2, rows, cols), BF16),
        scratch_shapes=[pltpu.VMEM((2 * w_local, 2, phys * row_tile, col_tile), F32)],
        compiler_params=params(2),
        cost_estimate=pl.CostEstimate(
            flops=8 * len(envs) * w_local * phys * rows * depth * cols,
            bytes_accessed=2 * (site.size + len(envs) * envs[0].size) + 4 * mpo_count * phys * rows * cols,
            transcendentals=0,
        ),
        name="first_product",
    )(place, mpo, site, *envs)


def second_kernel(flip_ref, q_one, q_two, site_even, site_odd, *outs):
    def work(site_keep, site_send):
        for q_ref, wide_ref, low_ref in ((q_one, outs[0], outs[2]), (q_two, outs[1], outs[3])):
            for site_ref, out_ref in ((site_keep, wide_ref), (site_send, low_ref)):
                out_real, out_imag = None, None
                for t in range(q_ref.shape[1]):
                    q_real, q_imag = q_ref[0, t, 0], q_ref[0, t, 1]
                    real, imag = site_ref[t, 0], site_ref[t, 1]
                    more_real = mul_t(q_real, real) + mul_t(-q_imag, imag)
                    more_imag = mul_t(q_real, imag) + mul_t(q_imag, real)
                    out_real = more_real if out_real is None else out_real + more_real
                    out_imag = more_imag if out_imag is None else out_imag + more_imag
                out_ref[0, 0] = out_real.astype(out_ref.dtype)
                out_ref[0, 1] = out_imag.astype(out_ref.dtype)

    @pl.when(flip_ref[0] == 0)
    def _():
        work(site_even, site_odd)

    @pl.when(flip_ref[0] != 0)
    def _():
        work(site_odd, site_even)


def second_product(flip, q_one, q_two, site_even, site_odd, row_tile):
    mpo_count, phys, _, rows, cols = q_one.shape
    y_rows = site_even.shape[2]
    row_tile = min(row_tile, rows)
    out_spec = pl.BlockSpec((1, 2, row_tile, y_rows), lambda v, i: (v, 0, i, 0))
    q_spec = pl.BlockSpec((1, phys, 2, row_tile, cols), lambda v, i: (v, 0, 0, i, 0))
    site_spec = pl.BlockSpec((phys, 2, y_rows, cols), lambda v, i: (0, 0, 0, 0))
    shape = (mpo_count, 2, rows, y_rows)
    return pl.pallas_call(
        second_kernel,
        grid=(mpo_count, rows // row_tile),
        in_specs=[pl.BlockSpec(memory_space=pltpu.SMEM), q_spec, q_spec, site_spec, site_spec],
        out_specs=[out_spec] * 4,
        out_shape=[jax.ShapeDtypeStruct(shape, kind) for kind in (F32, F32, BF16, BF16)],
        compiler_params=params(2),
        cost_estimate=pl.CostEstimate(
            flops=32 * mpo_count * phys * rows * y_rows * cols,
            bytes_accessed=q_one.size * 4 + site_even.size * 4 + 24 * mpo_count * rows * y_rows,
            transcendentals=0,
        ),
        name="second_product",
    )(flip, q_one, q_two, site_even, site_odd)


def after(value, *earlier):
    return lax.optimization_barrier((value,) + earlier)[0]


def swap(value):
    return lax.ppermute(value, "depth", [(0, 1), (1, 0)])


def by_depth(depth, mine, sibling):
    return jnp.where(depth == 0, jnp.stack([mine, sibling]), jnp.stack([sibling, mine]))


def split_inputs(environment, site_tensor, mpo):
    depth = lax.axis_index("depth")
    w_local, _, rows, half = environment.shape
    phys = site_tensor.shape[0]
    cols = half // 2
    env_own = lax.dynamic_slice_in_dim(environment, depth * cols, cols, 3)
    env_sib = swap(lax.dynamic_slice_in_dim(environment, (1 - depth) * cols, cols, 3))
    mpo_mine = jnp.concatenate(
        [
            lax.dynamic_slice_in_dim(mpo, depth * w_local, w_local, 0),
            lax.dynamic_slice_in_dim(mpo, (1 - depth) * w_local, w_local, 0),
        ],
        axis=0,
    )
    planar = jnp.transpose(site_tensor.reshape(phys, rows, 2, 2, cols), (3, 0, 2, 1, 4))
    return env_own, env_sib, mpo_mine, planar


def any_line(environment, site_tensor, mpo):
    col_count, depth = lax.axis_size("col"), lax.axis_index("depth")
    env_own, env_sib, mpo_mine, planar = split_inputs(environment, site_tensor, mpo)
    site_own = lax.dynamic_index_in_dim(planar, depth, 0, keepdims=False)
    cols = site_own.shape[3]
    pieces = col_count * 2
    gathered = lax.all_gather(site_own, "col", axis=0)
    site = jnp.moveaxis(by_depth(depth, gathered, swap(gathered)), 0, 1)
    site = site.reshape((pieces,) + site_own.shape)
    env_own = lax.all_gather(env_own, "row", axis=2, tiled=True)
    env_sib = lax.all_gather(env_sib, "row", axis=2, tiled=True)
    envs = []
    for index in range(pieces):
        block = slice(index * cols, (index + 1) * cols)
        envs += [env_own[:, :, block], env_sib[:, :, block]]
    q = first_product(jnp.arange(pieces, dtype=jnp.int32), mpo_mine, site, envs, 256, 256)
    site_all = lax.all_gather(site_own, "row", axis=2, tiled=True)
    total = None
    for t in range(q.shape[1]):
        q_real, q_imag = q[:, t, 0], q[:, t, 1]
        real, imag = site_all[t, 0], site_all[t, 1]
        one = lambda a, b: jnp.einsum("vxc,yc->vxy", a, b, preferred_element_type=F32)
        more = jnp.stack(
            [one(q_real, real) - one(q_imag, imag), one(q_real, imag) + one(q_imag, real)], axis=1
        )
        total = more if total is None else total + more
    return lax.psum_scatter(total, ("col", "depth"), scatter_dimension=3, tiled=True)


def four_rows(environment, site_tensor, mpo):
    row, col, depth = (lax.axis_index(axis) for axis in ("row", "col", "depth"))
    rows = site_tensor.shape[1]
    axes = ("row", "col", "depth")
    place = lambda r, c, d: (r * 2 + c) * 2 + d
    to_host = lambda value: lax.ppermute(value, "row", [(0, 1), (3, 2)])
    to_end = lambda value: lax.ppermute(value, "row", [(1, 0), (2, 3)])
    across = lambda value: lax.ppermute(value, "row", [(1, 2), (2, 1)])
    turn = lambda value: lax.ppermute(value, "col", [(0, 1), (1, 0)])

    def to_col(value, which_rows, far):
        pairs = []
        for r in which_rows:
            goal = r // 2 if not far else 1 - r // 2
            pairs += [(place(r, 1 - goal, d), place(r, goal, d)) for d in range(2)]
        return lax.ppermute(value, axes, pairs)

    env_own, env_sib, mpo_mine, planar = split_inputs(environment, site_tensor, mpo)
    end_own, end_sib = to_host(env_own), to_host(env_sib)
    over_own, over_sib = across(env_own), across(env_sib)
    over_end_own, over_end_sib = across(end_own), across(end_sib)

    planar = after(planar, env_sib)
    site_own = lax.dynamic_index_in_dim(planar, depth, 0, keepdims=False)
    other = turn(site_own)
    here = jnp.concatenate([planar, by_depth(depth, other, swap(other))], axis=0)

    chunks = 2
    y_rows = rows // chunks
    own_chunks = [site_own[:, :, m * y_rows : (m + 1) * y_rows] for m in range(chunks)]
    end_chunks, there = [], []
    gate = end_sib
    for m in range(chunks):
        chunk = to_host(after(own_chunks[m], gate))
        gate = chunk
        other = turn(chunk)
        there.append(
            jnp.concatenate(
                [by_depth(depth, chunk, swap(chunk)), by_depth(depth, other, swap(other))], axis=0
            )
        )
        end_chunks.append(chunk)
    end_site = jnp.concatenate(end_chunks, axis=2)
    there = jnp.concatenate(there, axis=3)

    base = row // 2
    blocks = [row, base * 4 + 1 - row, 3 - row, 3 - (base * 4 + 1 - row)]
    piece = jnp.stack([jnp.where(b // 2 == col, 0, 2) + b % 2 for b in blocks]).astype(jnp.int32)
    envs = [env_own, env_sib, end_own, end_sib, over_own, over_sib, over_end_own, over_end_sib]
    q_here = first_product(piece, mpo_mine, here, envs, 256, 256)
    q_there = first_product(piece, mpo_mine, there, envs, 256, 256)

    is_host = (row == 1) | (row == 2)

    def outputs(site_one, site_two, flip, far):
        keep_here, keep_there, send_here, send_there = second_product(
            flip.astype(jnp.int32).reshape(1), q_here, q_there, site_one, site_two, 256
        )
        low_there = (keep_there + swap(send_there).astype(F32)).astype(BF16)
        sum_here = keep_here + swap(send_here).astype(F32)
        came_here = to_col(sum_here.astype(BF16), (1, 2), far)
        came_there = to_end(low_there)
        turned = to_col(came_there, (0, 3), far)
        total = jnp.where(is_host, sum_here, 0.0)
        for more in (came_here, came_there, turned):
            total = total + more.astype(F32)
        return total

    near = outputs(site_own, end_site, depth != row % 2, False)
    far, gates = [], (over_end_sib, over_end_sib)
    for m in range(chunks):
        over_site = across(after(own_chunks[m], gates[0]))
        over_end_site = across(after(end_chunks[m], gates[1]))
        gates = (over_site, over_end_site)
        far.append(outputs(over_site, over_end_site, depth == row % 2, True))
    far = jnp.concatenate(far, axis=3)
    return jnp.where(col == row // 2, near, far)


def solution(mesh):
    placed = (
        P(("groups", "depth"), None, "row", "col"),
        P("groups", "row", None, "col"),
        P("groups", None, None, None),
    )
    line = mesh.shape["row"] == 4 and mesh.shape["col"] == 2 and mesh.shape["depth"] == 2
    return jax.shard_map(
        four_rows if line else any_line,
        mesh=mesh,
        in_specs=placed,
        out_specs=P("groups", None, "row", ("col", "depth")),
        check_vma=False,
    )
```

```python
import functools
import jax
import jax.numpy as jnp
from jax import lax
from jax.experimental import pallas as pl
from jax.experimental.pallas import tpu as pltpu
from jax.sharding import PartitionSpec as P

F32 = jnp.float32
BF16 = jnp.bfloat16
VMEM_BYTES = 56 * 1024 * 1024
LIGHT = pl.CostEstimate(flops=0, bytes_accessed=0, transcendentals=0)


def params(steps):
    return pltpu.CompilerParams(
        dimension_semantics=("arbitrary",) * steps, vmem_limit_bytes=VMEM_BYTES
    )


def mul(left, right):
    return jnp.dot(left, right, preferred_element_type=F32)


def mul_t(left, right):
    return lax.dot_general(left, right, (((1,), (1,)), ((), ())), preferred_element_type=F32)


def first_kernel(w_local, block_ref, mpo_ref, site_ref, *refs):
    q_ref, g_ref = refs[-2:]
    env_refs = refs[:-2]
    mpo_count, phys, _, rows, _ = q_ref.shape
    depth = site_ref.shape[-1]
    for which in range(2):
        for w in range(w_local):
            g_real, g_imag = None, None
            for block in range(len(env_refs) // 2):
                piece = block_ref[block]
                real = site_ref[piece, :, 0].reshape(phys * rows, depth)
                imag = site_ref[piece, :, 1].reshape(phys * rows, depth)
                env_real = env_refs[block * 2 + which][w, 0]
                env_imag = env_refs[block * 2 + which][w, 1]
                more_real = mul(real, env_real) + mul(imag, env_imag)
                more_imag = mul(real, env_imag) + mul(imag, -env_real)
                g_real = more_real if g_real is None else g_real + more_real
                g_imag = more_imag if g_imag is None else g_imag + more_imag
            g_ref[which * w_local + w, 0] = g_real
            g_ref[which * w_local + w, 1] = g_imag
    for part in range(2):
        for v in range(mpo_count):
            for t in range(phys):
                total = None
                for w in range(2 * w_local):
                    for s in range(phys):
                        term = mpo_ref[w, v, s, t] * g_ref[w, part, s * rows : (s + 1) * rows]
                        total = term if total is None else total + term
                q_ref[v, t, part] = total.astype(BF16)


def first_product(blocks, mpo, site, envs, col_tile):
    pieces, phys, _, rows, depth = site.shape
    w_local, _, _, cols = envs[0].shape
    mpo_count = mpo.shape[1]
    col_tile = min(col_tile, cols)
    smem = pl.BlockSpec(memory_space=pltpu.SMEM)
    return pl.pallas_call(
        functools.partial(first_kernel, w_local),
        grid=(cols // col_tile,),
        in_specs=[smem, smem, pl.BlockSpec((pieces, phys, 2, rows, depth), lambda j: (0, 0, 0, 0, 0))]
        + [pl.BlockSpec((w_local, 2, depth, col_tile), lambda j: (0, 0, 0, j))] * len(envs),
        out_specs=pl.BlockSpec((mpo_count, phys, 2, rows, col_tile), lambda j: (0, 0, 0, 0, j)),
        out_shape=jax.ShapeDtypeStruct((mpo_count, phys, 2, rows, cols), BF16),
        scratch_shapes=[pltpu.VMEM((2 * w_local, 2, phys * rows, col_tile), F32)],
        compiler_params=params(1),
        cost_estimate=LIGHT,
        name="first_product",
    )(blocks, mpo, site, *envs)


def second_kernel(tiles, sets, pick_ref, *refs):
    q_refs, out_ref = refs[: 2 * tiles], refs[-1]
    site_refs = refs[2 * tiles : -1]
    per_set = len(site_refs) // sets
    phys, _, rows, _ = q_refs[0].shape[1:]
    mine = pick_ref[0]

    def work(chosen):
        y_first = 0
        for site_ref in chosen:
            y_rows = site_ref.shape[3]
            for tile in range(tiles):
                out_real, out_imag = None, None
                for which in range(2):
                    quarter = mine if which == 0 else 1 - mine
                    q_ref = q_refs[tile * 2 + which]
                    for t in range(phys):
                        q_real, q_imag = q_ref[0, t, 0], q_ref[0, t, 1]
                        real, imag = site_ref[quarter, t, 0], site_ref[quarter, t, 1]
                        more_real = mul_t(q_real, real) + mul_t(-q_imag, imag)
                        more_imag = mul_t(q_real, imag) + mul_t(q_imag, real)
                        out_real = more_real if out_real is None else out_real + more_real
                        out_imag = more_imag if out_imag is None else out_imag + more_imag
                there = (slice(tile * rows, (tile + 1) * rows), slice(y_first, y_first + y_rows))
                out_ref[(0, 0) + there] = out_real.astype(BF16)
                out_ref[(0, 1) + there] = out_imag.astype(BF16)
            y_first += y_rows

    if sets == 1:
        work(site_refs)
    else:
        for number in range(sets):
            pl.when(pick_ref[1] == number)(
                functools.partial(work, site_refs[number * per_set : (number + 1) * per_set])
            )


def second_product(pick, q_tiles, site_sets):
    tiles, sets = len(q_tiles), len(site_sets)
    mpo_count, phys, _, rows, cols = q_tiles[0][0].shape
    sites = [block for chosen in site_sets for block in chosen]
    y_rows = sum(block.shape[3] for block in site_sets[0])
    site_specs = [
        pl.BlockSpec(
            (2,) + block.shape[1:],
            (lambda v, pick: (0, 0, 0, 0, 0)) if block.shape[0] == 2 else (lambda v, pick: (pick[2], 0, 0, 0, 0)),
        )
        for block in sites
    ]
    q_spec = pl.BlockSpec((1, phys, 2, rows, cols), lambda v, pick: (v, 0, 0, 0, 0))
    return pl.pallas_call(
        functools.partial(second_kernel, tiles, sets),
        grid_spec=pltpu.PrefetchScalarGridSpec(
            num_scalar_prefetch=1,
            grid=(mpo_count,),
            in_specs=[q_spec] * (2 * tiles) + site_specs,
            out_specs=pl.BlockSpec((1, 2, tiles * rows, y_rows), lambda v, pick: (v, 0, 0, 0)),
        ),
        out_shape=jax.ShapeDtypeStruct((mpo_count, 2, tiles * rows, y_rows), BF16),
        compiler_params=params(1),
        cost_estimate=LIGHT,
        name="second_product",
    )(pick, *[q for pair in q_tiles for q in pair], *sites)


def finish_kernel(kinds, pick_ref, *refs):
    out_ref = refs[-1]
    pairs = [(refs[2 * i], refs[2 * i + 1]) for i in range(len(refs) // 2)]
    for number, (whole, first, count) in enumerate(kinds):

        @pl.when(pick_ref[0] == number)
        def _(whole=whole, first=first, count=count):
            at = 0
            for one, two in pairs[first : first + count]:
                total = one[0, 0].astype(F32) + two[0, 0].astype(F32)
                if whole == "rows":
                    out_ref[0, 0, at : at + total.shape[0]] = total
                    at += total.shape[0]
                else:
                    out_ref[0, 0, :, at : at + total.shape[1]] = total
                    at += total.shape[1]


def finish(pick, cases):
    kinds, addends = [], []
    for whole, pairs in cases:
        kinds.append((whole, len(addends) // 2, len(pairs)))
        addends += [value for pair in pairs for value in pair]
    mpo_count = addends[0].shape[0]
    rows = sum(pair[0].shape[2] for pair in cases[0][1])
    cols = cases[0][1][0][0].shape[3]
    return pl.pallas_call(
        functools.partial(finish_kernel, kinds),
        grid=(mpo_count, 2),
        in_specs=[pl.BlockSpec(memory_space=pltpu.SMEM)]
        + [pl.BlockSpec((1, 1) + value.shape[2:], lambda v, p: (v, p, 0, 0)) for value in addends],
        out_specs=pl.BlockSpec((1, 1, rows, cols), lambda v, p: (v, p, 0, 0)),
        out_shape=jax.ShapeDtypeStruct((mpo_count, 2, rows, cols), F32),
        compiler_params=params(2),
        name="finish",
    )(pick, *addends)


def after(value, *earlier):
    return lax.optimization_barrier((value,) + earlier)[0]


def swap(value):
    return lax.ppermute(value, "depth", [(0, 1), (1, 0)])


def split_inputs(environment, mpo):
    depth = lax.axis_index("depth")
    w_local, half = environment.shape[0], environment.shape[3]
    cols = half // 2
    env_own = lax.dynamic_slice_in_dim(environment, depth * cols, cols, 3)
    env_sib = swap(lax.dynamic_slice_in_dim(environment, (1 - depth) * cols, cols, 3))
    mpo_mine = jnp.concatenate(
        [
            lax.dynamic_slice_in_dim(mpo, depth * w_local, w_local, 0),
            lax.dynamic_slice_in_dim(mpo, (1 - depth) * w_local, w_local, 0),
        ],
        axis=0,
    )
    return env_own, env_sib, mpo_mine


def one_product(left, right, dims):
    return jnp.einsum(dims, left, right, preferred_element_type=F32)


def any_line(environment, site_tensor, mpo):
    depth = lax.axis_index("depth")
    env_own, env_sib, mpo_mine = split_inputs(environment, mpo)
    env_own = lax.all_gather(env_own, "row", axis=2, tiled=True)
    env_sib = lax.all_gather(env_sib, "row", axis=2, tiled=True)
    env = jnp.concatenate([env_own, env_sib], axis=0)
    cols = env.shape[3]
    planar = jnp.transpose(site_tensor, (0, 2, 1, 3))
    site_own = lax.dynamic_slice_in_dim(planar, depth * cols, cols, 3)
    site = lax.all_gather(planar, "col", axis=3, tiled=True)
    first = functools.partial(one_product, dims="sxa,wac->wsxc")
    g = jnp.stack(
        [
            first(site[:, 0], env[:, 0]) + first(site[:, 1], env[:, 1]),
            first(site[:, 0], env[:, 1]) - first(site[:, 1], env[:, 0]),
        ],
        axis=2,
    )
    q = jnp.einsum("wvst,wspxc->vtpxc", mpo_mine, g, precision=lax.Precision.HIGHEST).astype(BF16)
    site = lax.all_gather(site_own, "row", axis=2, tiled=True)
    second = functools.partial(one_product, dims="vtxc,tyc->vxy")
    total = jnp.stack(
        [
            second(q[:, :, 0], site[:, 0]) - second(q[:, :, 1], site[:, 1]),
            second(q[:, :, 0], site[:, 1]) + second(q[:, :, 1], site[:, 0]),
        ],
        axis=1,
    )
    return lax.psum_scatter(total, ("col", "depth"), scatter_dimension=3, tiled=True)


def four_rows(environment, site_tensor, mpo):
    row, col, depth = (lax.axis_index(axis) for axis in ("row", "col", "depth"))
    rows = site_tensor.shape[1]
    cols = site_tensor.shape[3] // 2
    axes = ("row", "col", "depth")
    place = lambda r, c, d: (r * 2 + c) * 2 + d
    to_host = lambda value: lax.ppermute(value, "row", [(0, 1), (3, 2)])
    to_end = lambda value: lax.ppermute(value, "row", [(1, 0), (2, 3)])
    across = lambda value: lax.ppermute(value, "row", [(1, 2), (2, 1)])

    def to_col(value, which_rows, far):
        pairs = []
        for r in which_rows:
            goal = r // 2 if not far else 1 - r // 2
            pairs += [(place(r, 1 - goal, d), place(r, goal, d)) for d in range(2)]
        return lax.ppermute(value, axes, pairs)

    env_own, env_sib, mpo_mine = split_inputs(environment, mpo)
    over_own, end_own = across(env_own), to_host(env_own)
    over_sib, end_sib = across(env_sib), to_host(env_sib)
    over_end_own = across(after(end_own, over_own))
    over_end_sib = across(after(end_sib, over_sib))
    envs = [env_own, env_sib, end_own, end_sib, over_own, over_sib, over_end_own, over_end_sib]

    quarter = lax.dynamic_slice_in_dim(after(site_tensor, env_sib), depth * cols, cols, 3)
    quarter = jnp.transpose(quarter, (0, 2, 1, 3))
    tiles = 2
    tile_rows = rows // tiles
    gather = lambda value: lax.all_gather(value, ("col", "depth"), axis=0)
    own = [quarter[:, :, m * tile_rows : (m + 1) * tile_rows] for m in range(tiles)]
    here = [gather(after(own[0], over_own, end_own)), gather(after(own[1], over_sib, end_sib))]
    came = [to_host(after(own[0], end_sib))]
    came.append(to_host(after(own[1], came[0])))
    there = [gather(after(came[0], over_end_own, *here)), gather(after(came[1], over_end_sib))]

    side = row // 2
    end = side * 4 + 1 - row
    blocks = jnp.stack([row, end, 3 - row, 3 - end]).astype(jnp.int32)
    pick = jnp.stack([depth, jnp.where(depth == row % 2, 0, 1), col]).astype(jnp.int32)

    def over(part, earlier):
        m, first = part // 2, (part % 2) * (tile_rows // 2)
        chunk = slice(first, first + tile_rows // 2)
        chosen = [
            lax.dynamic_slice_in_dim(whole[m][:, :, :, chunk], col * 2, 2, 0) for whole in (here, there)
        ]
        return across(after(jnp.where(pick[1] == 0, *chosen), earlier))

    def first(site, *earlier):
        return first_product(after(blocks, *earlier), mpo_mine, site, envs, 256)

    def second(q_tiles, sites, *earlier):
        return second_product(after(pick, *earlier), q_tiles, sites)

    near = [here, there]
    over_0 = over(0, over_end_sib)
    q_there_0 = first(there[0])
    pair_there_0 = (q_there_0, swap(q_there_0))
    q_here_0 = first(here[0], q_there_0)
    pair_here_0 = (q_here_0, swap(q_here_0))
    near_there_0 = second([pair_there_0], near, q_here_0, over_0)
    came_there_0 = to_end(near_there_0)
    over_1 = over(1, over_0)
    q_there_1 = first(there[1], near_there_0)
    pair_there_1 = (q_there_1, swap(q_there_1))
    near_there_1 = second([pair_there_1], near, q_there_1, over_1)
    came_there_1 = to_end(near_there_1)
    over_2 = over(2, over_1)
    pairs_there = [pair_there_0, pair_there_1]
    far_there_0 = second(pairs_there, [[over_0, over_1]], near_there_1, came_there_0)
    came_far_0 = to_end(far_there_0)
    turned_there_0 = to_col(came_there_0, (0, 3), False)
    q_here_1 = first(here[1], far_there_0)
    pairs_here = [pair_here_0, (q_here_1, swap(q_here_1))]
    far_there_1 = second(pairs_there, [[over_2]], q_here_1)
    came_far_1 = to_end(far_there_1)
    over_3 = over(3, over_2)
    near_here = second(pairs_here, near, far_there_1, came_there_1, turned_there_0)
    turned_near_here = to_col(near_here, (1, 2), False)
    turned_there_1 = to_col(came_there_1, (0, 3), False)
    far_here_0 = second(pairs_here, [[over_0, over_1]], near_here, over_3)
    turned_far_here_0 = to_col(far_here_0, (1, 2), True)
    far_there_2 = second(pairs_there, [[over_3]], far_here_0)
    came_far_2 = to_end(far_there_2)
    far_here_1 = second(pairs_here, [[over_2, over_3]], far_there_2, came_far_0, turned_there_1)
    turned_far_here_1 = to_col(far_here_1, (1, 2), True)
    near_there = [(came_there_0, turned_there_0), (came_there_1, turned_there_1)]
    near_here = [(near_here, turned_near_here)]
    far_here = [(far_here_0, turned_far_here_0), (far_here_1, turned_far_here_1)]
    far_there = [(came, to_col(came, (0, 3), True)) for came in (came_far_0, came_far_1, came_far_2)]

    is_end = (row == 0) | (row == 3)
    case = jnp.where(is_end, 2, 0) + jnp.where(col == side, 0, 1)
    return finish(
        case.astype(jnp.int32).reshape(1),
        [("cols", near_here), ("cols", far_here), ("rows", near_there), ("cols", far_there)],
    )


def solution(mesh):
    placed = (
        P(("groups", "depth"), None, "row", "col"),
        P("groups", "row", None, "col"),
        P("groups", None, None, None),
    )
    line = mesh.shape["row"] == 4 and mesh.shape["col"] == 2 and mesh.shape["depth"] == 2
    return jax.shard_map(
        four_rows if line else any_line,
        mesh=mesh,
        in_specs=placed,
        out_specs=P("groups", None, "row", ("col", "depth")),
        check_vma=False,
    )
```

```python
import functools
import jax
import jax.numpy as jnp
from jax import lax
from jax.experimental import pallas as pl
from jax.experimental.pallas import tpu as pltpu
from jax.sharding import PartitionSpec as P

F32 = jnp.float32
BF16 = jnp.bfloat16
VMEM_BYTES = 56 * 1024 * 1024
LIGHT = pl.CostEstimate(flops=0, bytes_accessed=0, transcendentals=0)


def params(steps):
    return pltpu.CompilerParams(
        dimension_semantics=("arbitrary",) * steps, vmem_limit_bytes=VMEM_BYTES
    )


def mul(left, right):
    return jnp.dot(left, right, preferred_element_type=F32)


def mul_t(left, right):
    return lax.dot_general(left, right, (((1,), (1,)), ((), ())), preferred_element_type=F32)


def first_kernel(w_local, block_ref, mpo_ref, site_ref, *refs):
    q_ref, g_ref = refs[-2:]
    env_refs = refs[:-2]
    mpo_count, phys, _, rows, _ = q_ref.shape
    depth = env_refs[0].shape[2]
    per_col = site_ref.shape[-1] // depth
    for which in range(2):
        for w in range(w_local):
            g_real, g_imag = None, None
            for number in range(len(env_refs) // 2):
                block = block_ref[number]
                piece = pl.ds(pl.multiple_of((block % per_col) * depth, depth), depth)
                real = site_ref[block // per_col, :, 0, :, piece].reshape(phys * rows, depth)
                imag = site_ref[block // per_col, :, 1, :, piece].reshape(phys * rows, depth)
                env_real = env_refs[number * 2 + which][w, 0]
                env_imag = env_refs[number * 2 + which][w, 1]
                more_real = mul(real, env_real) + mul(imag, env_imag)
                more_imag = mul(real, env_imag) + mul(imag, -env_real)
                g_real = more_real if g_real is None else g_real + more_real
                g_imag = more_imag if g_imag is None else g_imag + more_imag
            g_ref[which * w_local + w, 0] = g_real
            g_ref[which * w_local + w, 1] = g_imag
    for part in range(2):
        for v in range(mpo_count):
            for t in range(phys):
                total = None
                for w in range(2 * w_local):
                    for s in range(phys):
                        term = mpo_ref[w, v, s, t] * g_ref[w, part, s * rows : (s + 1) * rows]
                        total = term if total is None else total + term
                q_ref[v, t, part] = total.astype(BF16)


def first_product(blocks, mpo, site, envs, row_tile, col_tile):
    col_count, phys, _, rows, wide = site.shape
    w_local, _, depth, cols = envs[0].shape
    mpo_count = mpo.shape[1]
    smem = pl.BlockSpec(memory_space=pltpu.SMEM)
    return pl.pallas_call(
        functools.partial(first_kernel, w_local),
        grid=(rows // row_tile, cols // col_tile),
        in_specs=[
            smem,
            smem,
            pl.BlockSpec((col_count, phys, 2, row_tile, wide), lambda i, j: (0, 0, 0, i, 0)),
        ]
        + [pl.BlockSpec((w_local, 2, depth, col_tile), lambda i, j: (0, 0, 0, j))] * len(envs),
        out_specs=pl.BlockSpec((mpo_count, phys, 2, row_tile, col_tile), lambda i, j: (0, 0, 0, i, j)),
        out_shape=jax.ShapeDtypeStruct((mpo_count, phys, 2, rows, cols), BF16),
        scratch_shapes=[pltpu.VMEM((2 * w_local, 2, phys * row_tile, col_tile), F32)],
        compiler_params=params(2),
        cost_estimate=LIGHT,
        name="first_product",
    )(blocks, mpo, site, *envs)


def second_kernel(pick_ref, q_ref, *refs):
    site_refs, out_ref = refs[:-1], refs[-1]
    join = lambda t, part: jnp.concatenate([site_ref[t, part] for site_ref in site_refs], axis=0)
    out_real, out_imag = None, None
    for t in range(q_ref.shape[1]):
        q_real, q_imag = q_ref[0, t, 0], q_ref[0, t, 1]
        real, imag = join(t, 0), join(t, 1)
        more_real = mul_t(q_real, real) + mul_t(-q_imag, imag)
        more_imag = mul_t(q_real, imag) + mul_t(q_imag, real)
        out_real = more_real if out_real is None else out_real + more_real
        out_imag = more_imag if out_imag is None else out_imag + more_imag
    out_ref[0, 0] = out_real.astype(BF16)
    out_ref[0, 1] = out_imag.astype(BF16)


def second_product(pick, q, sites, row_tile):
    mpo_count, phys, _, rows, cols = q.shape
    y_rows = sum(site.shape[2] for site in sites)
    return pl.pallas_call(
        second_kernel,
        grid=(mpo_count, rows // row_tile),
        in_specs=[
            pl.BlockSpec(memory_space=pltpu.SMEM),
            pl.BlockSpec((1, phys, 2, row_tile, cols), lambda v, i: (v, 0, 0, i, 0)),
        ]
        + [pl.BlockSpec(site.shape, lambda v, i: (0, 0, 0, 0)) for site in sites],
        out_specs=pl.BlockSpec((1, 2, row_tile, y_rows), lambda v, i: (v, 0, i, 0)),
        out_shape=jax.ShapeDtypeStruct((mpo_count, 2, rows, y_rows), BF16),
        compiler_params=params(2),
        cost_estimate=LIGHT,
        name="second_product",
    )(pick, q, *sites)


def finish_kernel(counts, pick_ref, *refs):
    out_ref = refs[-1]
    at = 0
    for step, sizes in enumerate(counts):
        parts = []
        for size in sizes:
            parts.append(refs[at : at + size])
            at += size

        @pl.when(pick_ref[0] == step)
        def _(parts=parts):
            half = sum(part[0].shape[3] for part in parts)
            for other, first in ((False, pick_ref[1]), (True, 1 - pick_ref[1])):
                for number, part in enumerate(parts):
                    width = part[0].shape[3]
                    total = sum(one[0, 0].astype(F32) for one in (part[2:] if other else part[:2]))
                    place = pl.ds(pl.multiple_of(first * half + number * width, width), width)
                    out_ref[0, 0, :, place] = total


def finish(pick, steps):
    parts = [value for step in steps for part in step for value in part]
    owners = [number for number, step in enumerate(steps) for part in step for _ in part]
    mpo_count, _, rows, _ = parts[0].shape
    cols = 2 * sum(part[0].shape[3] for part in steps[0])

    def spec(value, owner):
        def index(v, p, pick):
            mine = (pick[0] == owner).astype(jnp.int32)
            return (v * mine, p * mine, 0, 0)

        return pl.BlockSpec((1, 1) + value.shape[2:], index)

    return pl.pallas_call(
        functools.partial(finish_kernel, [[len(part) for part in step] for step in steps]),
        grid_spec=pltpu.PrefetchScalarGridSpec(
            num_scalar_prefetch=1,
            grid=(mpo_count, 2),
            in_specs=[spec(value, owner) for value, owner in zip(parts, owners)],
            out_specs=pl.BlockSpec((1, 1, rows, cols), lambda v, p, pick: (v, p, 0, 0)),
        ),
        out_shape=jax.ShapeDtypeStruct((mpo_count, 2, rows, cols), F32),
        compiler_params=params(2),
        name="finish",
    )(pick, *parts)


def after(value, *earlier):
    return lax.optimization_barrier((value,) + earlier)[0]


def swap(value):
    return lax.ppermute(value, "depth", [(0, 1), (1, 0)])


def split_inputs(environment, mpo):
    depth = lax.axis_index("depth")
    w_local, half = environment.shape[0], environment.shape[3]
    cols = half // 2
    env_own = lax.dynamic_slice_in_dim(environment, depth * cols, cols, 3)
    env_sib = swap(lax.dynamic_slice_in_dim(environment, (1 - depth) * cols, cols, 3))
    mpo_mine = jnp.concatenate(
        [
            lax.dynamic_slice_in_dim(mpo, depth * w_local, w_local, 0),
            lax.dynamic_slice_in_dim(mpo, (1 - depth) * w_local, w_local, 0),
        ],
        axis=0,
    )
    return env_own, env_sib, mpo_mine


def one_product(left, right, dims):
    return jnp.einsum(dims, left, right, preferred_element_type=F32)


def any_line(environment, site_tensor, mpo):
    depth = lax.axis_index("depth")
    env_own, env_sib, mpo_mine = split_inputs(environment, mpo)
    env_own = lax.all_gather(env_own, "row", axis=2, tiled=True)
    env_sib = lax.all_gather(env_sib, "row", axis=2, tiled=True)
    env = jnp.concatenate([env_own, env_sib], axis=0)
    cols = env.shape[3]
    planar = jnp.transpose(site_tensor, (0, 2, 1, 3))
    site_own = lax.dynamic_slice_in_dim(planar, depth * cols, cols, 3)
    site = lax.all_gather(planar, "col", axis=3, tiled=True)
    first = functools.partial(one_product, dims="sxa,wac->wsxc")
    g = jnp.stack(
        [
            first(site[:, 0], env[:, 0]) + first(site[:, 1], env[:, 1]),
            first(site[:, 0], env[:, 1]) - first(site[:, 1], env[:, 0]),
        ],
        axis=2,
    )
    q = jnp.einsum("wvst,wspxc->vtpxc", mpo_mine, g, precision=lax.Precision.HIGHEST).astype(BF16)
    site = lax.all_gather(site_own, "row", axis=2, tiled=True)
    second = functools.partial(one_product, dims="vtxc,tyc->vxy")
    total = jnp.stack(
        [
            second(q[:, :, 0], site[:, 0]) - second(q[:, :, 1], site[:, 1]),
            second(q[:, :, 0], site[:, 1]) + second(q[:, :, 1], site[:, 0]),
        ],
        axis=1,
    )
    return lax.psum_scatter(total, ("col", "depth"), scatter_dimension=3, tiled=True)


def ring(environment, site_tensor, mpo):
    row_count, col_count = lax.axis_size("row"), lax.axis_size("col")
    row, col, depth = (lax.axis_index(axis) for axis in ("row", "col", "depth"))
    axes = ("row", "col", "depth")
    place = lambda r, c, d: (r * col_count + c) * 2 + d
    shift = lambda value: lax.ppermute(
        value, "row", [(r, (r + 1) % row_count) for r in range(row_count)]
    )
    turn = lambda value: lax.ppermute(value, "col", [(0, 1), (1, 0)])
    in_order = lambda mine, sibling, axis: jnp.where(
        depth == 0,
        jnp.concatenate([mine, sibling], axis=axis),
        jnp.concatenate([sibling, mine], axis=axis),
    )

    env_own, env_sib, mpo_mine = split_inputs(environment, mpo)
    envs = [env_own, env_sib]
    for _ in range(row_count - 1):
        envs += [shift(envs[-2]), shift(envs[-1])]

    planar = jnp.transpose(after(site_tensor, envs[3]), (0, 2, 1, 3))
    rows = planar.shape[2]
    half = rows // 2
    mine = lax.dynamic_slice_in_dim(planar, depth * half, half, 2)
    other = turn(after(mine, envs[4]))
    other = in_order(other, swap(after(other, envs[5])), 2)
    site = jnp.where(col == 0, jnp.stack([planar, other]), jnp.stack([other, planar]))

    parts = [mine[:, :, : half // 2], mine[:, :, half // 2 :]]
    travelling = [[shift(after(part, env)) for part, env in zip(parts, envs[-2:])]]
    for _ in range(row_count - 2):
        travelling.append([shift(part) for part in travelling[-1]])

    blocks = jnp.stack([lax.rem(row - k + row_count, row_count) for k in range(row_count)])
    blocks = after(blocks.astype(jnp.int32), travelling[0][0])
    q = first_product(blocks, mpo_mine, site, envs, half, half)
    q = in_order(q, swap(after(q, travelling[0][1])), 4)

    pick = jnp.stack([lax.rem(row - col * 2 - depth + row_count, row_count), depth]).astype(jnp.int32)
    steps, gate = [], (q,)
    for step in range(row_count):
        goal = [((r - step) % row_count // 2, (r - step) % row_count % 2) for r in range(row_count)]

        def send(value, turned, crossed, cores=(0,)):
            pairs = []
            for r, (c, d) in enumerate(goal):
                for flip in cores:
                    e = d ^ flip
                    source = place(r, 1 - c if turned else c, 1 - e if crossed else e)
                    pairs.append((source, place(r, c, e)))
            return lax.ppermute(value, axes, pairs)

        if step < row_count - 1:
            low = second_product(after(pick, *gate), q, travelling[step - 1] if step else parts, half)
            turned = send(low, True, False, (0, 1))
            total = (low.astype(F32) + turned.astype(F32)).astype(BF16)
            steps.append([(low, turned, send(total, False, True))])
            gate = (low,) + ((travelling[1][0],) if step == 0 else ())
        else:
            done = []
            for number, site in enumerate(travelling[-1]):
                low = second_product(after(pick, *gate), q, [site], half)
                done.append(
                    (low, send(low, True, False), send(low, True, True), send(low, False, True))
                )
                gate = (low,) + steps[number][0][1:]
            steps.append(done)
        if step == row_count - 2:
            gate = gate + steps[0][0][1:2]
    return finish(pick, steps)


def solution(mesh):
    placed = (
        P(("groups", "depth"), None, "row", "col"),
        P("groups", "row", None, "col"),
        P("groups", None, None, None),
    )
    fits = mesh.shape["col"] == 2 and mesh.shape["row"] == 2 * mesh.shape["col"]
    return jax.shard_map(
        ring if fits else any_line,
        mesh=mesh,
        in_specs=placed,
        out_specs=P("groups", None, "row", ("col", "depth")),
        check_vma=False,
    )
```

```python
import functools
import jax
import jax.numpy as jnp
from jax import lax
from jax.experimental import pallas as pl
from jax.experimental.pallas import tpu as pltpu
from jax.sharding import PartitionSpec as P

F32 = jnp.float32
BF16 = jnp.bfloat16
VMEM_BYTES = 56 * 1024 * 1024
LIGHT = pl.CostEstimate(flops=0, bytes_accessed=0, transcendentals=0)


def params(steps):
    return pltpu.CompilerParams(
        dimension_semantics=("arbitrary",) * steps, vmem_limit_bytes=VMEM_BYTES
    )


def mul(left, right):
    return jnp.dot(left, right, preferred_element_type=F32)


def mul_t(left, right):
    return lax.dot_general(left, right, (((1,), (1,)), ((), ())), preferred_element_type=F32)


def first_kernel(w_local, block_ref, mpo_ref, site_ref, *refs):
    q_ref, g_ref = refs[-2:]
    env_refs = refs[:-2]
    mpo_count, phys, _, rows, _ = q_ref.shape
    depth = env_refs[0].shape[2]
    per_col = site_ref.shape[-1] // depth
    for which in range(2):
        for w in range(w_local):
            g_real, g_imag = None, None
            for number in range(len(env_refs) // 2):
                block = block_ref[number]
                piece = pl.ds(pl.multiple_of((block % per_col) * depth, depth), depth)
                real = site_ref[block // per_col, :, 0, :, piece].reshape(phys * rows, depth)
                imag = site_ref[block // per_col, :, 1, :, piece].reshape(phys * rows, depth)
                env_real = env_refs[number * 2 + which][w, 0]
                env_imag = env_refs[number * 2 + which][w, 1]
                more_real = mul(real, env_real) + mul(imag, env_imag)
                more_imag = mul(real, env_imag) + mul(imag, -env_real)
                g_real = more_real if g_real is None else g_real + more_real
                g_imag = more_imag if g_imag is None else g_imag + more_imag
            g_ref[which * w_local + w, 0] = g_real
            g_ref[which * w_local + w, 1] = g_imag
    for part in range(2):
        for v in range(mpo_count):
            for t in range(phys):
                total = None
                for w in range(2 * w_local):
                    for s in range(phys):
                        term = mpo_ref[w, v, s, t] * g_ref[w, part, s * rows : (s + 1) * rows]
                        total = term if total is None else total + term
                q_ref[v, t, part] = total.astype(BF16)


def first_product(blocks, mpo, site, envs, row_tile, col_tile):
    col_count, phys, _, rows, wide = site.shape
    w_local, _, depth, cols = envs[0].shape
    mpo_count = mpo.shape[1]
    smem = pl.BlockSpec(memory_space=pltpu.SMEM)
    return pl.pallas_call(
        functools.partial(first_kernel, w_local),
        grid=(rows // row_tile, cols // col_tile),
        in_specs=[
            smem,
            smem,
            pl.BlockSpec((col_count, phys, 2, row_tile, wide), lambda i, j: (0, 0, 0, i, 0)),
        ]
        + [pl.BlockSpec((w_local, 2, depth, col_tile), lambda i, j: (0, 0, 0, j))] * len(envs),
        out_specs=pl.BlockSpec((mpo_count, phys, 2, row_tile, col_tile), lambda i, j: (0, 0, 0, i, j)),
        out_shape=jax.ShapeDtypeStruct((mpo_count, phys, 2, rows, cols), BF16),
        scratch_shapes=[pltpu.VMEM((2 * w_local, 2, phys * row_tile, col_tile), F32)],
        compiler_params=params(2),
        cost_estimate=LIGHT,
        name="first_product",
    )(blocks, mpo, site, *envs)


def second_kernel(pick_ref, q_ref, *refs):
    site_refs, out_ref = refs[:-1], refs[-1]
    join = lambda t, part: jnp.concatenate([site_ref[t, part] for site_ref in site_refs], axis=0)
    out_real, out_imag = None, None
    for t in range(q_ref.shape[1]):
        q_real, q_imag = q_ref[0, t, 0], q_ref[0, t, 1]
        real, imag = join(t, 0), join(t, 1)
        more_real = mul_t(q_real, real) + mul_t(-q_imag, imag)
        more_imag = mul_t(q_real, imag) + mul_t(q_imag, real)
        out_real = more_real if out_real is None else out_real + more_real
        out_imag = more_imag if out_imag is None else out_imag + more_imag
    out_ref[0, 0] = out_real.astype(BF16)
    out_ref[0, 1] = out_imag.astype(BF16)


def second_product(pick, q, sites, row_tile):
    mpo_count, phys, _, rows, cols = q.shape
    y_rows = sum(site.shape[2] for site in sites)
    return pl.pallas_call(
        second_kernel,
        grid=(mpo_count, rows // row_tile),
        in_specs=[
            pl.BlockSpec(memory_space=pltpu.SMEM),
            pl.BlockSpec((1, phys, 2, row_tile, cols), lambda v, i: (v, 0, 0, i, 0)),
        ]
        + [pl.BlockSpec(site.shape, lambda v, i: (0, 0, 0, 0)) for site in sites],
        out_specs=pl.BlockSpec((1, 2, row_tile, y_rows), lambda v, i: (v, 0, i, 0)),
        out_shape=jax.ShapeDtypeStruct((mpo_count, 2, rows, y_rows), BF16),
        compiler_params=params(2),
        cost_estimate=LIGHT,
        name="second_product",
    )(pick, q, *sites)


def finish_kernel(counts, pick_ref, *refs):
    out_ref = refs[-1]
    at = 0
    for step, sizes in enumerate(counts):
        parts = []
        for size in sizes:
            parts.append(refs[at : at + size])
            at += size

        @pl.when(pick_ref[0] == step)
        def _(parts=parts):
            half = sum(part[0].shape[3] for part in parts)
            for other, first in ((False, pick_ref[1]), (True, 1 - pick_ref[1])):
                for number, part in enumerate(parts):
                    width = part[0].shape[3]
                    total = sum(one[0, 0].astype(F32) for one in (part[2:] if other else part[:2]))
                    place = pl.ds(pl.multiple_of(first * half + number * width, width), width)
                    out_ref[0, 0, :, place] = total


def finish(pick, steps):
    parts = [value for step in steps for part in step for value in part]
    owners = [number for number, step in enumerate(steps) for part in step for _ in part]
    mpo_count, _, rows, _ = parts[0].shape
    cols = 2 * sum(part[0].shape[3] for part in steps[0])

    def spec(value, owner):
        def index(v, p, pick):
            mine = (pick[0] == owner).astype(jnp.int32)
            return (v * mine, p * mine, 0, 0)

        return pl.BlockSpec((1, 1) + value.shape[2:], index)

    return pl.pallas_call(
        functools.partial(finish_kernel, [[len(part) for part in step] for step in steps]),
        grid_spec=pltpu.PrefetchScalarGridSpec(
            num_scalar_prefetch=1,
            grid=(mpo_count, 2),
            in_specs=[spec(value, owner) for value, owner in zip(parts, owners)],
            out_specs=pl.BlockSpec((1, 1, rows, cols), lambda v, p, pick: (v, p, 0, 0)),
        ),
        out_shape=jax.ShapeDtypeStruct((mpo_count, 2, rows, cols), F32),
        compiler_params=params(2),
        name="finish",
    )(pick, *parts)


def after(value, *earlier):
    return lax.optimization_barrier((value,) + earlier)[0]


def swap(value):
    return lax.ppermute(value, "depth", [(0, 1), (1, 0)])


def split_inputs(environment, mpo):
    depth = lax.axis_index("depth")
    w_local, half = environment.shape[0], environment.shape[3]
    cols = half // 2
    env_own = lax.dynamic_slice_in_dim(environment, depth * cols, cols, 3)
    env_sib = swap(lax.dynamic_slice_in_dim(environment, (1 - depth) * cols, cols, 3))
    mpo_mine = jnp.concatenate(
        [
            lax.dynamic_slice_in_dim(mpo, depth * w_local, w_local, 0),
            lax.dynamic_slice_in_dim(mpo, (1 - depth) * w_local, w_local, 0),
        ],
        axis=0,
    )
    return env_own, env_sib, mpo_mine


def one_product(left, right, dims):
    return jnp.einsum(dims, left, right, preferred_element_type=F32)


def any_line(environment, site_tensor, mpo):
    depth = lax.axis_index("depth")
    env_own, env_sib, mpo_mine = split_inputs(environment, mpo)
    env_own = lax.all_gather(env_own, "row", axis=2, tiled=True)
    env_sib = lax.all_gather(env_sib, "row", axis=2, tiled=True)
    env = jnp.concatenate([env_own, env_sib], axis=0)
    cols = env.shape[3]
    planar = jnp.transpose(site_tensor, (0, 2, 1, 3))
    site_own = lax.dynamic_slice_in_dim(planar, depth * cols, cols, 3)
    site = lax.all_gather(planar, "col", axis=3, tiled=True)
    first = functools.partial(one_product, dims="sxa,wac->wsxc")
    g = jnp.stack(
        [
            first(site[:, 0], env[:, 0]) + first(site[:, 1], env[:, 1]),
            first(site[:, 0], env[:, 1]) - first(site[:, 1], env[:, 0]),
        ],
        axis=2,
    )
    q = jnp.einsum("wvst,wspxc->vtpxc", mpo_mine, g, precision=lax.Precision.HIGHEST).astype(BF16)
    site = lax.all_gather(site_own, "row", axis=2, tiled=True)
    second = functools.partial(one_product, dims="vtxc,tyc->vxy")
    total = jnp.stack(
        [
            second(q[:, :, 0], site[:, 0]) - second(q[:, :, 1], site[:, 1]),
            second(q[:, :, 0], site[:, 1]) + second(q[:, :, 1], site[:, 0]),
        ],
        axis=1,
    )
    return lax.psum_scatter(total, ("col", "depth"), scatter_dimension=3, tiled=True)


def ring(environment, site_tensor, mpo):
    row_count, col_count = lax.axis_size("row"), lax.axis_size("col")
    row, col, depth = (lax.axis_index(axis) for axis in ("row", "col", "depth"))
    axes = ("row", "col", "depth")
    place = lambda r, c, d: (r * col_count + c) * 2 + d
    shift = lambda value: lax.ppermute(
        value, "row", [(r, (r + 1) % row_count) for r in range(row_count)]
    )
    turn = lambda value: lax.ppermute(value, "col", [(0, 1), (1, 0)])
    in_order = lambda mine, sibling, axis: jnp.where(
        depth == 0,
        jnp.concatenate([mine, sibling], axis=axis),
        jnp.concatenate([sibling, mine], axis=axis),
    )

    env_own, env_sib, mpo_mine = split_inputs(environment, mpo)
    envs = [env_own, env_sib]
    for _ in range(row_count - 1):
        envs += [shift(envs[-2]), shift(envs[-1])]

    planar = jnp.transpose(after(site_tensor, envs[3]), (0, 2, 1, 3))
    rows = planar.shape[2]
    half = rows // 2
    mine = lax.dynamic_slice_in_dim(planar, depth * half, half, 2)
    other = turn(after(mine, envs[4]))
    other = in_order(other, swap(after(other, envs[5])), 2)
    site = jnp.where(col == 0, jnp.stack([planar, other]), jnp.stack([other, planar]))

    parts = [mine[:, :, : half // 2], mine[:, :, half // 2 :]]
    travelling = [[shift(after(part, env, site)) for part, env in zip(parts, envs[-2:])]]
    for _ in range(row_count - 2):
        travelling.append([shift(part) for part in travelling[-1]])

    blocks = jnp.stack([lax.rem(row - k + row_count, row_count) for k in range(row_count)])
    blocks = after(blocks.astype(jnp.int32), *travelling[0])
    q = first_product(blocks, mpo_mine, site, envs, half, half)
    q = in_order(q, swap(after(q, travelling[1][0])), 4)

    pick = jnp.stack([lax.rem(row - col * 2 - depth + row_count, row_count), depth]).astype(jnp.int32)
    steps, gate = [], (q,)
    for step in range(row_count):
        goal = [((r - step) % row_count // 2, (r - step) % row_count % 2) for r in range(row_count)]

        def send(value, turned, crossed, cores=(0,)):
            pairs = []
            for r, (c, d) in enumerate(goal):
                for flip in cores:
                    e = d ^ flip
                    source = place(r, 1 - c if turned else c, 1 - e if crossed else e)
                    pairs.append((source, place(r, c, e)))
            return lax.ppermute(value, axes, pairs)

        if step < row_count - 1:
            low = second_product(after(pick, *gate), q, travelling[step - 1] if step else parts, half)
            turned = send(low, True, False, (0, 1))
            total = (low.astype(F32) + turned.astype(F32)).astype(BF16)
            steps.append([(low, turned, send(total, False, True))])
            gate = (low,) + ((travelling[1][0],) if step == 0 else ())
        else:
            done = []
            for number, site in enumerate(travelling[-1]):
                low = second_product(after(pick, *gate), q, [site], half)
                done.append(
                    (low, send(low, True, False), send(low, True, True), send(low, False, True))
                )
                gate = (low,) + steps[number][0][1:]
            steps.append(done)
        if step == row_count - 2:
            gate = gate + steps[0][0][1:2]
    return finish(pick, steps)


def solution(mesh):
    placed = (
        P(("groups", "depth"), None, "row", "col"),
        P("groups", "row", None, "col"),
        P("groups", None, None, None),
    )
    fits = mesh.shape["col"] == 2 and mesh.shape["row"] == 2 * mesh.shape["col"]
    return jax.shard_map(
        ring if fits else any_line,
        mesh=mesh,
        in_specs=placed,
        out_specs=P("groups", None, "row", ("col", "depth")),
        check_vma=False,
    )
```

```python
import functools
import jax
import jax.numpy as jnp
from jax import lax
from jax.experimental import pallas as pl
from jax.experimental.pallas import tpu as pltpu
from jax.sharding import PartitionSpec as P

F32 = jnp.float32
BF16 = jnp.bfloat16
VMEM_BYTES = 56 * 1024 * 1024
LIGHT = pl.CostEstimate(flops=0, bytes_accessed=0, transcendentals=0)


def params(steps):
    return pltpu.CompilerParams(
        dimension_semantics=("arbitrary",) * steps, vmem_limit_bytes=VMEM_BYTES
    )


def mul(left, right):
    return jnp.dot(left, right, preferred_element_type=F32)


def mul_t(left, right):
    return lax.dot_general(left, right, (((1,), (1,)), ((), ())), preferred_element_type=F32)


def first_kernel(w_local, block_ref, mpo_ref, site_ref, *refs):
    q_ref, g_ref = refs[-2:]
    env_refs = refs[:-2]
    mpo_count, phys, _, rows, _ = q_ref.shape
    depth = env_refs[0].shape[2]
    per_col = site_ref.shape[-1] // depth
    for which in range(2):
        for w in range(w_local):
            g_real, g_imag = None, None
            for number in range(len(env_refs) // 2):
                block = block_ref[number]
                piece = pl.ds(pl.multiple_of((block % per_col) * depth, depth), depth)
                real = site_ref[block // per_col, :, 0, :, piece].reshape(phys * rows, depth)
                imag = site_ref[block // per_col, :, 1, :, piece].reshape(phys * rows, depth)
                env_real = env_refs[number * 2 + which][w, 0]
                env_imag = env_refs[number * 2 + which][w, 1]
                more_real = mul(real, env_real) + mul(imag, env_imag)
                more_imag = mul(real, env_imag) + mul(imag, -env_real)
                g_real = more_real if g_real is None else g_real + more_real
                g_imag = more_imag if g_imag is None else g_imag + more_imag
            g_ref[which * w_local + w, 0] = g_real
            g_ref[which * w_local + w, 1] = g_imag
    for part in range(2):
        for v in range(mpo_count):
            for t in range(phys):
                total = None
                for w in range(2 * w_local):
                    for s in range(phys):
                        term = mpo_ref[w, v, s, t] * g_ref[w, part, s * rows : (s + 1) * rows]
                        total = term if total is None else total + term
                q_ref[v, t, part] = total.astype(BF16)


def first_product(blocks, mpo, site, envs, row_tile, col_tile):
    col_count, phys, _, rows, wide = site.shape
    w_local, _, depth, cols = envs[0].shape
    mpo_count = mpo.shape[1]
    smem = pl.BlockSpec(memory_space=pltpu.SMEM)
    return pl.pallas_call(
        functools.partial(first_kernel, w_local),
        grid=(rows // row_tile, cols // col_tile),
        in_specs=[
            smem,
            smem,
            pl.BlockSpec((col_count, phys, 2, row_tile, wide), lambda i, j: (0, 0, 0, i, 0)),
        ]
        + [pl.BlockSpec((w_local, 2, depth, col_tile), lambda i, j: (0, 0, 0, j))] * len(envs),
        out_specs=pl.BlockSpec((mpo_count, phys, 2, row_tile, col_tile), lambda i, j: (0, 0, 0, i, j)),
        out_shape=jax.ShapeDtypeStruct((mpo_count, phys, 2, rows, cols), BF16),
        scratch_shapes=[pltpu.VMEM((2 * w_local, 2, phys * row_tile, col_tile), F32)],
        compiler_params=params(2),
        cost_estimate=LIGHT,
        name="first_product",
    )(blocks, mpo, site, *envs)


def second_kernel(pick_ref, q_ref, *refs):
    site_refs, out_ref = refs[:-1], refs[-1]
    join = lambda t, part: jnp.concatenate([site_ref[t, part] for site_ref in site_refs], axis=0)
    out_real, out_imag = None, None
    for t in range(q_ref.shape[1]):
        q_real, q_imag = q_ref[0, t, 0], q_ref[0, t, 1]
        real, imag = join(t, 0), join(t, 1)
        more_real = mul_t(q_real, real) + mul_t(-q_imag, imag)
        more_imag = mul_t(q_real, imag) + mul_t(q_imag, real)
        out_real = more_real if out_real is None else out_real + more_real
        out_imag = more_imag if out_imag is None else out_imag + more_imag
    out_ref[0, 0] = out_real.astype(BF16)
    out_ref[0, 1] = out_imag.astype(BF16)


def second_product(pick, q, sites, row_tile):
    mpo_count, phys, _, rows, cols = q.shape
    y_rows = sum(site.shape[2] for site in sites)
    return pl.pallas_call(
        second_kernel,
        grid=(mpo_count, rows // row_tile),
        in_specs=[
            pl.BlockSpec(memory_space=pltpu.SMEM),
            pl.BlockSpec((1, phys, 2, row_tile, cols), lambda v, i: (v, 0, 0, i, 0)),
        ]
        + [pl.BlockSpec(site.shape, lambda v, i: (0, 0, 0, 0)) for site in sites],
        out_specs=pl.BlockSpec((1, 2, row_tile, y_rows), lambda v, i: (v, 0, i, 0)),
        out_shape=jax.ShapeDtypeStruct((mpo_count, 2, rows, y_rows), BF16),
        compiler_params=params(2),
        cost_estimate=LIGHT,
        name="second_product",
    )(pick, q, *sites)


def finish_kernel(counts, pick_ref, *refs):
    out_ref = refs[-1]
    at = 0
    for step, sizes in enumerate(counts):
        parts = []
        for size in sizes:
            parts.append(refs[at : at + size])
            at += size

        @pl.when(pick_ref[0] == step)
        def _(parts=parts):
            half = sum(part[0].shape[3] for part in parts)
            for other, first in ((False, pick_ref[1]), (True, 1 - pick_ref[1])):
                for number, part in enumerate(parts):
                    width = part[0].shape[3]
                    total = sum(one[0, 0].astype(F32) for one in (part[2:] if other else part[:2]))
                    place = pl.ds(pl.multiple_of(first * half + number * width, width), width)
                    out_ref[0, 0, :, place] = total


def finish(pick, steps):
    parts = [value for step in steps for part in step for value in part]
    owners = [number for number, step in enumerate(steps) for part in step for _ in part]
    mpo_count, _, rows, _ = parts[0].shape
    cols = 2 * sum(part[0].shape[3] for part in steps[0])

    def spec(value, owner):
        def index(v, p, pick):
            mine = (pick[0] == owner).astype(jnp.int32)
            return (v * mine, p * mine, 0, 0)

        return pl.BlockSpec((1, 1) + value.shape[2:], index)

    return pl.pallas_call(
        functools.partial(finish_kernel, [[len(part) for part in step] for step in steps]),
        grid_spec=pltpu.PrefetchScalarGridSpec(
            num_scalar_prefetch=1,
            grid=(mpo_count, 2),
            in_specs=[spec(value, owner) for value, owner in zip(parts, owners)],
            out_specs=pl.BlockSpec((1, 1, rows, cols), lambda v, p, pick: (v, p, 0, 0)),
        ),
        out_shape=jax.ShapeDtypeStruct((mpo_count, 2, rows, cols), F32),
        compiler_params=params(2),
        name="finish",
    )(pick, *parts)


def after(value, *earlier):
    return lax.optimization_barrier((value,) + earlier)[0]


def swap(value):
    return lax.ppermute(value, "depth", [(0, 1), (1, 0)])


def split_inputs(environment, mpo):
    depth = lax.axis_index("depth")
    w_local, half = environment.shape[0], environment.shape[3]
    cols = half // 2
    env_own = lax.dynamic_slice_in_dim(environment, depth * cols, cols, 3)
    env_sib = swap(lax.dynamic_slice_in_dim(environment, (1 - depth) * cols, cols, 3))
    mpo_mine = jnp.concatenate(
        [
            lax.dynamic_slice_in_dim(mpo, depth * w_local, w_local, 0),
            lax.dynamic_slice_in_dim(mpo, (1 - depth) * w_local, w_local, 0),
        ],
        axis=0,
    )
    return env_own, env_sib, mpo_mine


def one_product(left, right, dims):
    return jnp.einsum(dims, left, right, preferred_element_type=F32)


def any_line(environment, site_tensor, mpo):
    depth = lax.axis_index("depth")
    env_own, env_sib, mpo_mine = split_inputs(environment, mpo)
    env_own = lax.all_gather(env_own, "row", axis=2, tiled=True)
    env_sib = lax.all_gather(env_sib, "row", axis=2, tiled=True)
    env = jnp.concatenate([env_own, env_sib], axis=0)
    cols = env.shape[3]
    planar = jnp.transpose(site_tensor, (0, 2, 1, 3))
    site_own = lax.dynamic_slice_in_dim(planar, depth * cols, cols, 3)
    site = lax.all_gather(planar, "col", axis=3, tiled=True)
    first = functools.partial(one_product, dims="sxa,wac->wsxc")
    g = jnp.stack(
        [
            first(site[:, 0], env[:, 0]) + first(site[:, 1], env[:, 1]),
            first(site[:, 0], env[:, 1]) - first(site[:, 1], env[:, 0]),
        ],
        axis=2,
    )
    q = jnp.einsum("wvst,wspxc->vtpxc", mpo_mine, g, precision=lax.Precision.HIGHEST).astype(BF16)
    site = lax.all_gather(site_own, "row", axis=2, tiled=True)
    second = functools.partial(one_product, dims="vtxc,tyc->vxy")
    total = jnp.stack(
        [
            second(q[:, :, 0], site[:, 0]) - second(q[:, :, 1], site[:, 1]),
            second(q[:, :, 0], site[:, 1]) + second(q[:, :, 1], site[:, 0]),
        ],
        axis=1,
    )
    return lax.psum_scatter(total, ("col", "depth"), scatter_dimension=3, tiled=True)


def ring(environment, site_tensor, mpo):
    row_count, col_count = lax.axis_size("row"), lax.axis_size("col")
    row, col, depth = (lax.axis_index(axis) for axis in ("row", "col", "depth"))
    axes = ("row", "col", "depth")
    place = lambda r, c, d: (r * col_count + c) * 2 + d
    shift = lambda value: lax.ppermute(
        value, "row", [(r, (r + 1) % row_count) for r in range(row_count)]
    )
    turn = lambda value: lax.ppermute(value, "col", [(0, 1), (1, 0)])
    in_order = lambda mine, sibling, axis: jnp.where(
        depth == 0,
        jnp.concatenate([mine, sibling], axis=axis),
        jnp.concatenate([sibling, mine], axis=axis),
    )

    env_own, env_sib, mpo_mine = split_inputs(environment, mpo)
    envs = [env_own, env_sib]
    for _ in range(row_count - 1):
        envs += [shift(envs[-2]), shift(envs[-1])]

    planar = jnp.transpose(after(site_tensor, env_sib), (0, 2, 1, 3))
    rows = planar.shape[2]
    half = rows // 2
    mine = lax.dynamic_slice_in_dim(planar, depth * half, half, 2)
    other = turn(mine)
    other = in_order(other, swap(after(other, envs[4], envs[5])), 2)
    site = jnp.where(col == 0, jnp.stack([planar, other]), jnp.stack([other, planar]))

    parts = [mine[:, :, : half // 2], mine[:, :, half // 2 :]]
    travelling = [[shift(after(part, env, site)) for part, env in zip(parts, envs[-2:])]]
    for _ in range(row_count - 2):
        travelling.append([shift(part) for part in travelling[-1]])

    blocks = jnp.stack([lax.rem(row - k + row_count, row_count) for k in range(row_count)])
    blocks = after(blocks.astype(jnp.int32), *travelling[0])
    q = first_product(blocks, mpo_mine, site, envs, half, half)
    q = in_order(q, swap(after(q, travelling[1][0])), 4)

    pick = jnp.stack([lax.rem(row - col * 2 - depth + row_count, row_count), depth]).astype(jnp.int32)
    steps, gate = [], (q,)
    for step in range(row_count):
        goal = [((r - step) % row_count // 2, (r - step) % row_count % 2) for r in range(row_count)]

        def send(value, turned, crossed, cores=(0,)):
            pairs = []
            for r, (c, d) in enumerate(goal):
                for flip in cores:
                    e = d ^ flip
                    source = place(r, 1 - c if turned else c, 1 - e if crossed else e)
                    pairs.append((source, place(r, c, e)))
            return lax.ppermute(value, axes, pairs)

        if step < row_count - 1:
            low = second_product(after(pick, *gate), q, travelling[step - 1] if step else parts, half)
            turned = send(low, True, False, (0, 1))
            total = (low.astype(F32) + turned.astype(F32)).astype(BF16)
            steps.append([(low, turned, send(total, False, True))])
            gate = (low,) + ((travelling[1][0],) if step == 0 else ())
        else:
            done = []
            for number, site in enumerate(travelling[-1]):
                low = second_product(after(pick, *gate), q, [site], half)
                done.append(
                    (low, send(low, True, False), send(low, True, True), send(low, False, True))
                )
                gate = (low,) + steps[number][0][1:]
            steps.append(done)
        if step == row_count - 2:
            gate = gate + steps[0][0][1:2]
    return finish(pick, steps)


def solution(mesh):
    placed = (
        P(("groups", "depth"), None, "row", "col"),
        P("groups", "row", None, "col"),
        P("groups", None, None, None),
    )
    fits = mesh.shape["col"] == 2 and mesh.shape["row"] == 2 * mesh.shape["col"]
    return jax.shard_map(
        ring if fits else any_line,
        mesh=mesh,
        in_specs=placed,
        out_specs=P("groups", None, "row", ("col", "depth")),
        check_vma=False,
    )
```

```python
import functools
import jax
import jax.numpy as jnp
from jax import lax
from jax.experimental import pallas as pl
from jax.experimental.pallas import tpu as pltpu
from jax.sharding import PartitionSpec as P

F32 = jnp.float32
BF16 = jnp.bfloat16
VMEM_BYTES = 56 * 1024 * 1024
LIGHT = pl.CostEstimate(flops=0, bytes_accessed=0, transcendentals=0)


def params(steps):
    return pltpu.CompilerParams(
        dimension_semantics=("arbitrary",) * steps, vmem_limit_bytes=VMEM_BYTES
    )


def mul(left, right):
    return jnp.dot(left, right, preferred_element_type=F32)


def mul_t(left, right):
    return lax.dot_general(left, right, (((1,), (1,)), ((), ())), preferred_element_type=F32)


def first_kernel(w_local, block_ref, mpo_ref, site_ref, *refs):
    q_ref, g_ref = refs[-2:]
    env_refs = refs[:-2]
    mpo_count, phys, _, rows, _ = q_ref.shape
    depth = env_refs[0].shape[2]
    per_col = site_ref.shape[-1] // depth
    for which in range(2):
        for w in range(w_local):
            with_real, with_imag = None, None
            for number in range(len(env_refs) // 2):
                block = block_ref[number]
                piece = pl.ds(pl.multiple_of((block % per_col) * depth, depth), depth)
                left = site_ref[block // per_col, :, :, :, piece].reshape(phys * 2 * rows, depth)
                env_ref = env_refs[number * 2 + which]
                more_real, more_imag = mul(left, env_ref[w, 0]), mul(left, env_ref[w, 1])
                with_real = more_real if with_real is None else with_real + more_real
                with_imag = more_imag if with_imag is None else with_imag + more_imag
            for s in range(phys):
                real, imag = (slice((2 * s + part) * rows, (2 * s + part + 1) * rows) for part in range(2))
                there = slice(s * rows, (s + 1) * rows)
                g_ref[which * w_local + w, 0, there] = with_real[real] + with_imag[imag]
                g_ref[which * w_local + w, 1, there] = with_imag[real] - with_real[imag]
    for part in range(2):
        for v in range(mpo_count):
            for t in range(phys):
                total = None
                for w in range(2 * w_local):
                    for s in range(phys):
                        term = mpo_ref[w, v, s, t] * g_ref[w, part, s * rows : (s + 1) * rows]
                        total = term if total is None else total + term
                q_ref[v, t, part] = total.astype(BF16)


def first_product(blocks, mpo, site, envs, row_tile, col_tile):
    col_count, phys, _, rows, wide = site.shape
    w_local, _, depth, cols = envs[0].shape
    mpo_count = mpo.shape[1]
    smem = pl.BlockSpec(memory_space=pltpu.SMEM)
    return pl.pallas_call(
        functools.partial(first_kernel, w_local),
        grid=(rows // row_tile, cols // col_tile),
        in_specs=[
            smem,
            smem,
            pl.BlockSpec((col_count, phys, 2, row_tile, wide), lambda i, j: (0, 0, 0, i, 0)),
        ]
        + [pl.BlockSpec((w_local, 2, depth, col_tile), lambda i, j: (0, 0, 0, j))] * len(envs),
        out_specs=pl.BlockSpec((mpo_count, phys, 2, row_tile, col_tile), lambda i, j: (0, 0, 0, i, j)),
        out_shape=jax.ShapeDtypeStruct((mpo_count, phys, 2, rows, cols), BF16),
        scratch_shapes=[pltpu.VMEM((2 * w_local, 2, phys * row_tile, col_tile), F32)],
        compiler_params=params(2),
        cost_estimate=LIGHT,
        name="first_product",
    )(blocks, mpo, site, *envs)


def second_kernel(pick_ref, own_ref, sib_ref, *refs):
    site_refs, out_ref = refs[:-1], refs[-1]
    phys, _, rows, cols = own_ref.shape[1:]
    with_real, with_imag = None, None
    for q_ref, quarter in ((own_ref, pick_ref[0]), (sib_ref, 1 - pick_ref[0])):
        piece = pl.ds(pl.multiple_of(quarter * cols, cols), cols)
        join = lambda t, part: jnp.concatenate([site_ref[t, part, :, piece] for site_ref in site_refs], axis=0)
        for t in range(phys):
            left = q_ref[0, t].reshape(2 * rows, cols)
            more_real, more_imag = mul_t(left, join(t, 0)), mul_t(left, join(t, 1))
            with_real = more_real if with_real is None else with_real + more_real
            with_imag = more_imag if with_imag is None else with_imag + more_imag
    out_ref[0, 0] = (with_real[:rows] - with_imag[rows:]).astype(BF16)
    out_ref[0, 1] = (with_imag[:rows] + with_real[rows:]).astype(BF16)


def second_product(pick, own, sib, sites):
    mpo_count, phys, _, rows, cols = own.shape
    y_rows = sum(site.shape[2] for site in sites)
    q_spec = pl.BlockSpec((1, phys, 2, rows, cols), lambda v: (v, 0, 0, 0, 0))
    return pl.pallas_call(
        second_kernel,
        grid=(mpo_count,),
        in_specs=[pl.BlockSpec(memory_space=pltpu.SMEM), q_spec, q_spec]
        + [pl.BlockSpec(site.shape, lambda v: (0, 0, 0, 0)) for site in sites],
        out_specs=pl.BlockSpec((1, 2, rows, y_rows), lambda v: (v, 0, 0, 0)),
        out_shape=jax.ShapeDtypeStruct((mpo_count, 2, rows, y_rows), BF16),
        compiler_params=params(1),
        cost_estimate=LIGHT,
        name="second_product",
    )(pick, own, sib, *sites)


def finish_kernel(pick_ref, base_ref, *refs):
    out_ref = refs[-1]
    parts = [refs[at : at + 4] for at in range(0, len(refs) - 1, 4)]

    @pl.when(pick_ref[0] == 0)
    def _():
        out_ref[0, 0] = base_ref[0, 0].astype(F32)

    @pl.when(pick_ref[0] != 0)
    def _():
        half = sum(part[0].shape[3] for part in parts)
        for side, first in ((0, pick_ref[1]), (1, 1 - pick_ref[1])):
            for number, part in enumerate(parts):
                one, two = part[2 * side : 2 * side + 2]
                width = one.shape[3]
                place = pl.ds(pl.multiple_of(first * half + number * width, width), width)
                out_ref[0, 0, :, place] = one[0, 0].astype(F32) + two[0, 0].astype(F32)


def finish(pick, base, parts):
    addends = [value for part in parts for value in part]
    mpo_count, _, rows, cols = base.shape

    def spec(value, used):
        def index(v, p, pick):
            mine = (pick[0] == used).astype(jnp.int32)
            return (v * mine, p * mine, 0, 0)

        return pl.BlockSpec((1, 1) + value.shape[2:], index)

    return pl.pallas_call(
        finish_kernel,
        grid_spec=pltpu.PrefetchScalarGridSpec(
            num_scalar_prefetch=1,
            grid=(mpo_count, 2),
            in_specs=[spec(base, 0)] + [spec(value, 1) for value in addends],
            out_specs=pl.BlockSpec((1, 1, rows, cols), lambda v, p, pick: (v, p, 0, 0)),
        ),
        out_shape=jax.ShapeDtypeStruct((mpo_count, 2, rows, cols), F32),
        compiler_params=params(2),
        cost_estimate=LIGHT,
        name="finish",
    )(pick, base, *addends)


def after(value, *earlier):
    return lax.optimization_barrier((value,) + earlier)[0]


def swap(value):
    return lax.ppermute(value, "depth", [(0, 1), (1, 0)])


def split_inputs(environment, mpo):
    depth = lax.axis_index("depth")
    w_local, half = environment.shape[0], environment.shape[3]
    cols = half // 2
    env_own = lax.dynamic_slice_in_dim(environment, depth * cols, cols, 3)
    env_sib = swap(lax.dynamic_slice_in_dim(environment, (1 - depth) * cols, cols, 3))
    mpo_mine = jnp.concatenate(
        [
            lax.dynamic_slice_in_dim(mpo, depth * w_local, w_local, 0),
            lax.dynamic_slice_in_dim(mpo, (1 - depth) * w_local, w_local, 0),
        ],
        axis=0,
    )
    return env_own, env_sib, mpo_mine


def one_product(left, right, dims):
    return jnp.einsum(dims, left, right, preferred_element_type=F32)


def any_line(environment, site_tensor, mpo):
    depth = lax.axis_index("depth")
    env_own, env_sib, mpo_mine = split_inputs(environment, mpo)
    env_own = lax.all_gather(env_own, "row", axis=2, tiled=True)
    env_sib = lax.all_gather(env_sib, "row", axis=2, tiled=True)
    env = jnp.concatenate([env_own, env_sib], axis=0)
    cols = env.shape[3]
    planar = jnp.transpose(site_tensor, (0, 2, 1, 3))
    site_own = lax.dynamic_slice_in_dim(planar, depth * cols, cols, 3)
    site = lax.all_gather(planar, "col", axis=3, tiled=True)
    first = functools.partial(one_product, dims="sxa,wac->wsxc")
    g = jnp.stack(
        [
            first(site[:, 0], env[:, 0]) + first(site[:, 1], env[:, 1]),
            first(site[:, 0], env[:, 1]) - first(site[:, 1], env[:, 0]),
        ],
        axis=2,
    )
    q = jnp.einsum("wvst,wspxc->vtpxc", mpo_mine, g, precision=lax.Precision.HIGHEST).astype(BF16)
    site = lax.all_gather(site_own, "row", axis=2, tiled=True)
    second = functools.partial(one_product, dims="vtxc,tyc->vxy")
    total = jnp.stack(
        [
            second(q[:, :, 0], site[:, 0]) - second(q[:, :, 1], site[:, 1]),
            second(q[:, :, 0], site[:, 1]) + second(q[:, :, 1], site[:, 0]),
        ],
        axis=1,
    )
    return lax.psum_scatter(total, ("col", "depth"), scatter_dimension=3, tiled=True)


def ring(environment, site_tensor, mpo):
    row_count, col_count = lax.axis_size("row"), lax.axis_size("col")
    row, col, depth = (lax.axis_index(axis) for axis in ("row", "col", "depth"))
    axes = ("row", "col", "depth")
    place = lambda r, c, d: (r * col_count + c) * 2 + d
    shift = lambda value: lax.ppermute(
        value, "row", [(r, (r + 1) % row_count) for r in range(row_count)]
    )
    turn = lambda value: lax.ppermute(value, "col", [(0, 1), (1, 0)])
    in_order = lambda mine, sibling, axis: jnp.where(
        depth == 0,
        jnp.concatenate([mine, sibling], axis=axis),
        jnp.concatenate([sibling, mine], axis=axis),
    )

    env_own, env_sib, mpo_mine = split_inputs(environment, mpo)
    envs = [env_own, env_sib]
    for _ in range(row_count - 1):
        envs += [shift(envs[-2]), shift(envs[-1])]

    planar = jnp.transpose(after(site_tensor, env_sib), (0, 2, 1, 3))
    rows = planar.shape[2]
    half = rows // 2
    mine = lax.dynamic_slice_in_dim(planar, depth * half, half, 2)
    other = turn(mine)
    other = in_order(other, swap(after(other, envs[4], envs[5])), 2)
    site = jnp.where(col == 0, jnp.stack([planar, other]), jnp.stack([other, planar]))

    parts = [mine[:, :, : half // 2], mine[:, :, half // 2 :]]
    travelling = [[shift(after(part, env, site)) for part, env in zip(parts, envs[-2:])]]
    for _ in range(row_count - 2):
        travelling.append([shift(part) for part in travelling[-1]])

    blocks = jnp.stack([lax.rem(row - k + row_count, row_count) for k in range(row_count)])
    blocks = after(blocks.astype(jnp.int32), *travelling[0])
    q = first_product(blocks, mpo_mine, site, envs, half, half)
    q_sib = swap(after(q, travelling[1][0]))

    goals = [
        [((r - step) % row_count // 2, (r - step) % row_count % 2) for r in range(row_count)]
        for step in range(row_count)
    ]
    pick = depth.astype(jnp.int32).reshape(1)

    def second(sites, *earlier):
        return second_product(after(pick, *earlier), q, q_sib, sites)

    def turn_to_goal(value, goal):
        return lax.ppermute(
            value,
            axes,
            [(place(r, 1 - c, d), place(r, c, d)) for r, (c, _) in enumerate(goal) for d in range(2)],
        )

    def send(value, goal, turned, crossed):
        return lax.ppermute(
            value,
            axes,
            [
                (place(r, 1 - c if turned else c, 1 - d if crossed else d), place(r, c, d))
                for r, (c, d) in enumerate(goal)
            ],
        )

    step_of = lambda d: lax.rem(row - col * 2 - d + row_count, row_count)
    lows = [second(parts)]
    turned = [turn_to_goal(lows[0], goals[0])]
    lows.append(second(travelling[0], lows[0], travelling[1][1]))
    turned.append(turn_to_goal(lows[1], goals[1]))
    lows.append(second(travelling[1], lows[1], turned[0]))
    turned.append(turn_to_goal(lows[2], goals[2]))
    totals = [(low.astype(F32) + came.astype(F32)).astype(BF16) for low, came in zip(lows, turned)]

    def total_at(step):
        return jnp.where(step == 0, totals[0], jnp.where(step == 1, totals[1], totals[2]))

    def last_part(number, *earlier):
        low = second([travelling[2][number]], *earlier)
        ways = ((True, False), (True, True), (False, True))
        return [low] + [send(low, goals[3], *way) for way in ways]

    last = [last_part(0, lows[2])]
    mine, siblings = total_at(step_of(depth)), total_at(step_of(1 - depth))
    last.append(last_part(1, *last[0], mine, siblings))
    base = in_order(mine, swap(after(siblings, last[1][0])), 3)
    came_last = (step_of(depth) == row_count - 1).astype(jnp.int32)
    return finish(jnp.stack([came_last, depth.astype(jnp.int32)]), base, last)


def solution(mesh):
    placed = (
        P(("groups", "depth"), None, "row", "col"),
        P("groups", "row", None, "col"),
        P("groups", None, None, None),
    )
    fits = mesh.shape["col"] == 2 and mesh.shape["row"] == 2 * mesh.shape["col"]
    return jax.shard_map(
        ring if fits else any_line,
        mesh=mesh,
        in_specs=placed,
        out_specs=P("groups", None, "row", ("col", "depth")),
        check_vma=False,
    )
```

```python
import functools
import jax
import jax.numpy as jnp
from jax import lax
from jax.experimental import pallas as pl
from jax.experimental.pallas import tpu as pltpu
from jax.sharding import PartitionSpec as P

F32 = jnp.float32
BF16 = jnp.bfloat16
VMEM_BYTES = 56 * 1024 * 1024
LIGHT = pl.CostEstimate(flops=0, bytes_accessed=0, transcendentals=0)


def params(steps):
    return pltpu.CompilerParams(
        dimension_semantics=("arbitrary",) * steps, vmem_limit_bytes=VMEM_BYTES
    )


def mul(left, right):
    return jnp.dot(left, right, preferred_element_type=F32)


def mul_t(left, right):
    return lax.dot_general(left, right, (((1,), (1,)), ((), ())), preferred_element_type=F32)


def first_kernel(w_local, block_ref, mpo_ref, site_ref, *refs):
    q_ref, g_ref = refs[-2:]
    env_refs = refs[:-2]
    mpo_count, phys, _, rows, _ = q_ref.shape
    depth = env_refs[0].shape[2]
    per_col = site_ref.shape[-1] // depth
    for which in range(2):
        for w in range(w_local):
            with_real, with_imag = None, None
            for number in range(len(env_refs) // 2):
                block = block_ref[number]
                piece = pl.ds(pl.multiple_of((block % per_col) * depth, depth), depth)
                left = site_ref[block // per_col, :, :, :, piece].reshape(phys * 2 * rows, depth)
                env_ref = env_refs[number * 2 + which]
                more_real, more_imag = mul(left, env_ref[w, 0]), mul(left, env_ref[w, 1])
                with_real = more_real if with_real is None else with_real + more_real
                with_imag = more_imag if with_imag is None else with_imag + more_imag
            for s in range(phys):
                real, imag = (slice((2 * s + part) * rows, (2 * s + part + 1) * rows) for part in range(2))
                there = slice(s * rows, (s + 1) * rows)
                g_ref[which * w_local + w, 0, there] = with_real[real] + with_imag[imag]
                g_ref[which * w_local + w, 1, there] = with_imag[real] - with_real[imag]
    for part in range(2):
        for v in range(mpo_count):
            for t in range(phys):
                total = None
                for w in range(2 * w_local):
                    for s in range(phys):
                        term = mpo_ref[w, v, s, t] * g_ref[w, part, s * rows : (s + 1) * rows]
                        total = term if total is None else total + term
                q_ref[v, t, part] = total.astype(BF16)


def first_product(blocks, mpo, site, envs, row_tile, col_tile):
    col_count, phys, _, rows, wide = site.shape
    w_local, _, depth, cols = envs[0].shape
    mpo_count = mpo.shape[1]
    smem = pl.BlockSpec(memory_space=pltpu.SMEM)
    return pl.pallas_call(
        functools.partial(first_kernel, w_local),
        grid=(rows // row_tile, cols // col_tile),
        in_specs=[
            smem,
            smem,
            pl.BlockSpec((col_count, phys, 2, row_tile, wide), lambda i, j: (0, 0, 0, i, 0)),
        ]
        + [pl.BlockSpec((w_local, 2, depth, col_tile), lambda i, j: (0, 0, 0, j))] * len(envs),
        out_specs=pl.BlockSpec((mpo_count, phys, 2, row_tile, col_tile), lambda i, j: (0, 0, 0, i, j)),
        out_shape=jax.ShapeDtypeStruct((mpo_count, phys, 2, rows, cols), BF16),
        scratch_shapes=[pltpu.VMEM((2 * w_local, 2, phys * row_tile, col_tile), F32)],
        compiler_params=params(2),
        cost_estimate=LIGHT,
        name="first_product",
    )(blocks, mpo, site, *envs)


def second_kernel(pick_ref, own_ref, sib_ref, *refs):
    site_refs, out_ref = refs[:-1], refs[-1]
    phys, _, rows, cols = own_ref.shape[1:]
    with_real, with_imag = None, None
    for q_ref, quarter in ((own_ref, pick_ref[0]), (sib_ref, 1 - pick_ref[0])):
        piece = pl.ds(pl.multiple_of(quarter * cols, cols), cols)
        join = lambda t, part: jnp.concatenate([site_ref[t, part, :, piece] for site_ref in site_refs], axis=0)
        for t in range(phys):
            left = q_ref[0, t].reshape(2 * rows, cols)
            more_real, more_imag = mul_t(left, join(t, 0)), mul_t(left, join(t, 1))
            with_real = more_real if with_real is None else with_real + more_real
            with_imag = more_imag if with_imag is None else with_imag + more_imag
    out_ref[0, 0] = (with_real[:rows] - with_imag[rows:]).astype(BF16)
    out_ref[0, 1] = (with_imag[:rows] + with_real[rows:]).astype(BF16)


def second_product(pick, own, sib, sites):
    mpo_count, phys, _, rows, cols = own.shape
    y_rows = sum(site.shape[2] for site in sites)
    q_spec = pl.BlockSpec((1, phys, 2, rows, cols), lambda v: (v, 0, 0, 0, 0))
    return pl.pallas_call(
        second_kernel,
        grid=(mpo_count,),
        in_specs=[pl.BlockSpec(memory_space=pltpu.SMEM), q_spec, q_spec]
        + [pl.BlockSpec(site.shape, lambda v: (0, 0, 0, 0)) for site in sites],
        out_specs=pl.BlockSpec((1, 2, rows, y_rows), lambda v: (v, 0, 0, 0)),
        out_shape=jax.ShapeDtypeStruct((mpo_count, 2, rows, y_rows), BF16),
        compiler_params=params(1),
        cost_estimate=LIGHT,
        name="second_product",
    )(pick, own, sib, *sites)


def finish_kernel(pick_ref, mine_ref, siblings_ref, *refs):
    out_ref = refs[-1]
    parts = [refs[at : at + 4] for at in range(0, len(refs) - 1, 4)]
    half = mine_ref.shape[3]
    halves = [pl.multiple_of(core * half, half) for core in (pick_ref[1], 1 - pick_ref[1])]

    @pl.when(pick_ref[0] == 0)
    def _():
        for ref, first in zip((mine_ref, siblings_ref), halves):
            out_ref[0, 0, :, pl.ds(first, half)] = ref[0, 0].astype(F32)

    @pl.when(pick_ref[0] != 0)
    def _():
        for side, first in enumerate(halves):
            for number, part in enumerate(parts):
                one, two = part[2 * side : 2 * side + 2]
                width = one.shape[3]
                place = pl.ds(pl.multiple_of(first + number * width, width), width)
                out_ref[0, 0, :, place] = one[0, 0].astype(F32) + two[0, 0].astype(F32)


def finish(pick, mine, siblings, parts):
    addends = [value for part in parts for value in part]
    mpo_count, _, rows, half = mine.shape

    def spec(value, used):
        def index(v, p, pick):
            wanted = (pick[0] == used).astype(jnp.int32)
            return (v * wanted, p * wanted, 0, 0)

        return pl.BlockSpec((1, 1) + value.shape[2:], index)

    return pl.pallas_call(
        finish_kernel,
        grid_spec=pltpu.PrefetchScalarGridSpec(
            num_scalar_prefetch=1,
            grid=(mpo_count, 2),
            in_specs=[spec(mine, 0), spec(siblings, 0)] + [spec(value, 1) for value in addends],
            out_specs=pl.BlockSpec((1, 1, rows, 2 * half), lambda v, p, pick: (v, p, 0, 0)),
        ),
        out_shape=jax.ShapeDtypeStruct((mpo_count, 2, rows, 2 * half), F32),
        compiler_params=params(2),
        cost_estimate=LIGHT,
        name="finish",
    )(pick, mine, siblings, *addends)


def after(value, *earlier):
    return lax.optimization_barrier((value,) + earlier)[0]


def swap(value):
    return lax.ppermute(value, "depth", [(0, 1), (1, 0)])


def split_inputs(environment, mpo):
    depth = lax.axis_index("depth")
    w_local, half = environment.shape[0], environment.shape[3]
    cols = half // 2
    env_own = lax.dynamic_slice_in_dim(environment, depth * cols, cols, 3)
    env_sib = swap(lax.dynamic_slice_in_dim(environment, (1 - depth) * cols, cols, 3))
    mpo_mine = jnp.concatenate(
        [
            lax.dynamic_slice_in_dim(mpo, depth * w_local, w_local, 0),
            lax.dynamic_slice_in_dim(mpo, (1 - depth) * w_local, w_local, 0),
        ],
        axis=0,
    )
    return env_own, env_sib, mpo_mine


def one_product(left, right, dims):
    return jnp.einsum(dims, left, right, preferred_element_type=F32)


def any_line(environment, site_tensor, mpo):
    depth = lax.axis_index("depth")
    env_own, env_sib, mpo_mine = split_inputs(environment, mpo)
    env_own = lax.all_gather(env_own, "row", axis=2, tiled=True)
    env_sib = lax.all_gather(env_sib, "row", axis=2, tiled=True)
    env = jnp.concatenate([env_own, env_sib], axis=0)
    cols = env.shape[3]
    planar = jnp.transpose(site_tensor, (0, 2, 1, 3))
    site_own = lax.dynamic_slice_in_dim(planar, depth * cols, cols, 3)
    site = lax.all_gather(planar, "col", axis=3, tiled=True)
    first = functools.partial(one_product, dims="sxa,wac->wsxc")
    g = jnp.stack(
        [
            first(site[:, 0], env[:, 0]) + first(site[:, 1], env[:, 1]),
            first(site[:, 0], env[:, 1]) - first(site[:, 1], env[:, 0]),
        ],
        axis=2,
    )
    q = jnp.einsum("wvst,wspxc->vtpxc", mpo_mine, g, precision=lax.Precision.HIGHEST).astype(BF16)
    site = lax.all_gather(site_own, "row", axis=2, tiled=True)
    second = functools.partial(one_product, dims="vtxc,tyc->vxy")
    total = jnp.stack(
        [
            second(q[:, :, 0], site[:, 0]) - second(q[:, :, 1], site[:, 1]),
            second(q[:, :, 0], site[:, 1]) + second(q[:, :, 1], site[:, 0]),
        ],
        axis=1,
    )
    return lax.psum_scatter(total, ("col", "depth"), scatter_dimension=3, tiled=True)


def ring(environment, site_tensor, mpo):
    row_count, col_count = lax.axis_size("row"), lax.axis_size("col")
    row, col, depth = (lax.axis_index(axis) for axis in ("row", "col", "depth"))
    axes = ("row", "col", "depth")
    place = lambda r, c, d: (r * col_count + c) * 2 + d
    shift = lambda value: lax.ppermute(
        value, "row", [(r, (r + 1) % row_count) for r in range(row_count)]
    )
    turn = lambda value: lax.ppermute(value, "col", [(0, 1), (1, 0)])
    in_order = lambda mine, sibling, axis: jnp.where(
        depth == 0,
        jnp.concatenate([mine, sibling], axis=axis),
        jnp.concatenate([sibling, mine], axis=axis),
    )

    env_own, env_sib, mpo_mine = split_inputs(environment, mpo)
    envs = [env_own, env_sib]
    for _ in range(row_count - 1):
        envs += [shift(envs[-2]), shift(envs[-1])]

    planar = jnp.transpose(after(site_tensor, env_sib), (0, 2, 1, 3))
    rows = planar.shape[2]
    half = rows // 2
    mine = lax.dynamic_slice_in_dim(planar, depth * half, half, 2)
    other = turn(mine)
    other = in_order(other, swap(after(other, envs[4], envs[5])), 2)
    site = jnp.where(col == 0, jnp.stack([planar, other]), jnp.stack([other, planar]))

    parts = [mine[:, :, : half // 2], mine[:, :, half // 2 :]]
    travelling = [[shift(after(part, env, site)) for part, env in zip(parts, envs[-2:])]]
    for _ in range(row_count - 2):
        travelling.append([shift(part) for part in travelling[-1]])

    blocks = jnp.stack([lax.rem(row - k + row_count, row_count) for k in range(row_count)])
    blocks = after(blocks.astype(jnp.int32), travelling[0][0])
    q = first_product(blocks, mpo_mine, site, envs, half, half)
    q_sib = swap(after(q, travelling[0][1]))

    goals = [
        [((r - step) % row_count // 2, (r - step) % row_count % 2) for r in range(row_count)]
        for step in range(row_count)
    ]
    pick = depth.astype(jnp.int32).reshape(1)

    def second(sites, *earlier):
        return second_product(after(pick, *earlier), q, q_sib, sites)

    def turn_to_goal(value, goal):
        return lax.ppermute(
            value,
            axes,
            [(place(r, 1 - c, d), place(r, c, d)) for r, (c, _) in enumerate(goal) for d in range(2)],
        )

    def send(value, goal, turned, crossed):
        return lax.ppermute(
            value,
            axes,
            [
                (place(r, 1 - c if turned else c, 1 - d if crossed else d), place(r, c, d))
                for r, (c, d) in enumerate(goal)
            ],
        )

    step_of = lambda d: lax.rem(row - col * 2 - d + row_count, row_count)
    lows = [second(parts)]
    turned = [turn_to_goal(lows[0], goals[0])]
    lows.append(second(travelling[0], lows[0], travelling[1][0]))
    turned.append(turn_to_goal(lows[1], goals[1]))
    lows.append(second(travelling[1], lows[1], turned[0]))
    turned.append(turn_to_goal(lows[2], goals[2]))
    totals = [low.astype(F32) + came.astype(F32) for low, came in zip(lows, turned)]

    def total_at(step):
        return jnp.where(step == 0, totals[0], jnp.where(step == 1, totals[1], totals[2]))

    def last_part(number, *earlier):
        low = second([travelling[2][number]], *earlier)
        ways = ((True, False), (True, True), (False, True))
        return [low] + [send(low, goals[3], *way) for way in ways]

    last = [last_part(0, lows[2])]
    mine, siblings = total_at(step_of(depth)), total_at(step_of(1 - depth)).astype(BF16)
    last.append(last_part(1, *last[0], mine, siblings))
    siblings = swap(siblings)
    came_last = (step_of(depth) == row_count - 1).astype(jnp.int32)
    return finish(jnp.stack([came_last, depth.astype(jnp.int32)]), mine, siblings, last)


def solution(mesh):
    placed = (
        P(("groups", "depth"), None, "row", "col"),
        P("groups", "row", None, "col"),
        P("groups", None, None, None),
    )
    fits = mesh.shape["col"] == 2 and mesh.shape["row"] == 2 * mesh.shape["col"]
    return jax.shard_map(
        ring if fits else any_line,
        mesh=mesh,
        in_specs=placed,
        out_specs=P("groups", None, "row", ("col", "depth")),
        check_vma=False,
    )
```

```python
import functools
import jax
import jax.numpy as jnp
from jax import lax
from jax.experimental import pallas as pl
from jax.experimental.pallas import tpu as pltpu
from jax.sharding import PartitionSpec as P

F32 = jnp.float32
BF16 = jnp.bfloat16
VMEM_BYTES = 56 * 1024 * 1024
LIGHT = pl.CostEstimate(flops=0, bytes_accessed=0, transcendentals=0)


def params(steps):
    return pltpu.CompilerParams(
        dimension_semantics=("arbitrary",) * steps, vmem_limit_bytes=VMEM_BYTES
    )


def mul(left, right):
    return jnp.dot(left, right, preferred_element_type=F32)


def mul_t(left, right):
    return lax.dot_general(left, right, (((1,), (1,)), ((), ())), preferred_element_type=F32)


def first_kernel(block_ref, mpo_ref, site_ref, *refs):
    q_ref, g_ref = refs[-2:]
    env_refs = refs[:-2]
    mpo_count, phys, _, rows, _ = q_ref.shape
    depth = env_refs[0].shape[2]
    per_col = site_ref.shape[-1] // depth
    w_local = mpo_count // 2
    for w in range(mpo_count):
        with_real, with_imag = None, None
        for number in range(len(env_refs) // 2):
            env_ref = env_refs[number * 2 + w // w_local]
            block = block_ref[number]
            piece = pl.ds(pl.multiple_of((block % per_col) * depth, depth), depth)
            left = site_ref[block // per_col, :, :, :, piece].reshape(phys * 2 * rows, depth)
            more_real, more_imag = mul(left, env_ref[w % w_local, 0]), mul(left, env_ref[w % w_local, 1])
            with_real = more_real if with_real is None else with_real + more_real
            with_imag = more_imag if with_imag is None else with_imag + more_imag
        for s in range(phys):
            real, imag = (slice((2 * s + part) * rows, (2 * s + part + 1) * rows) for part in range(2))
            there = slice(s * rows, (s + 1) * rows)
            g_ref[w, 0, there] = with_real[real] + with_imag[imag]
            g_ref[w, 1, there] = with_imag[real] - with_real[imag]
    for part in range(2):
        for v in range(mpo_count):
            for t in range(phys):
                total = None
                for w in range(mpo_count):
                    for s in range(phys):
                        term = mpo_ref[w, v, s, t] * g_ref[w, part, s * rows : (s + 1) * rows]
                        total = term if total is None else total + term
                q_ref[v, t, part] = total.astype(BF16)


def first_product(blocks, mpo, site, envs, row_tile, col_tile):
    col_count, phys, _, rows, wide = site.shape
    w_local, _, depth, cols = envs[0].shape
    mpo_count = mpo.shape[1]
    smem = pl.BlockSpec(memory_space=pltpu.SMEM)
    return pl.pallas_call(
        first_kernel,
        grid=(rows // row_tile, cols // col_tile),
        in_specs=[
            smem,
            smem,
            pl.BlockSpec((col_count, phys, 2, row_tile, wide), lambda i, j: (0, 0, 0, i, 0)),
        ]
        + [pl.BlockSpec((w_local, 2, depth, col_tile), lambda i, j: (0, 0, 0, j))] * len(envs),
        out_specs=pl.BlockSpec((mpo_count, phys, 2, row_tile, col_tile), lambda i, j: (0, 0, 0, i, j)),
        out_shape=jax.ShapeDtypeStruct((mpo_count, phys, 2, rows, cols), BF16),
        scratch_shapes=[pltpu.VMEM((mpo_count, 2, phys * row_tile, col_tile), F32)],
        compiler_params=params(2),
        cost_estimate=LIGHT,
        name="first_product",
    )(blocks, mpo, site, *envs)


def second_kernel(pick_ref, own_ref, sib_ref, *refs):
    site_refs, out_ref = refs[:-1], refs[-1]
    phys, _, rows, cols = own_ref.shape[1:]
    total = None
    for q_ref, quarter in ((own_ref, pick_ref[0]), (sib_ref, 1 - pick_ref[0])):
        piece = pl.ds(pl.multiple_of(quarter * cols, cols), cols)
        for t in range(phys):
            right = [site_ref[t, part, :, piece] for part in range(2) for site_ref in site_refs]
            more = mul_t(q_ref[0, t].reshape(2 * rows, cols), jnp.concatenate(right, axis=0))
            total = more if total is None else total + more
    width = total.shape[1] // 2
    out_ref[0, 0] = (total[:rows, :width] - total[rows:, width:]).astype(BF16)
    out_ref[0, 1] = (total[:rows, width:] + total[rows:, :width]).astype(BF16)


def second_product(pick, own, sib, sites):
    mpo_count, phys, _, rows, cols = own.shape
    y_rows = sum(site.shape[2] for site in sites)
    q_spec = pl.BlockSpec((1, phys, 2, rows, cols), lambda v: (v, 0, 0, 0, 0))
    return pl.pallas_call(
        second_kernel,
        grid=(mpo_count,),
        in_specs=[pl.BlockSpec(memory_space=pltpu.SMEM), q_spec, q_spec]
        + [pl.BlockSpec(site.shape, lambda v: (0, 0, 0, 0)) for site in sites],
        out_specs=pl.BlockSpec((1, 2, rows, y_rows), lambda v: (v, 0, 0, 0)),
        out_shape=jax.ShapeDtypeStruct((mpo_count, 2, rows, y_rows), BF16),
        compiler_params=params(1),
        cost_estimate=LIGHT,
        name="second_product",
    )(pick, own, sib, *sites)


def finish_kernel(pick_ref, mine_ref, siblings_ref, out_ref):
    half = mine_ref.shape[3]
    for ref, core in ((mine_ref, pick_ref[0]), (siblings_ref, 1 - pick_ref[0])):
        out_ref[0, 0, :, pl.ds(pl.multiple_of(core * half, half), half)] = ref[0, 0].astype(F32)


def finish(pick, mine, siblings):
    mpo_count, _, rows, half = mine.shape
    half_spec = pl.BlockSpec((1, 1, rows, half), lambda v, p: (v, p, 0, 0))
    return pl.pallas_call(
        finish_kernel,
        grid=(mpo_count, 2),
        in_specs=[pl.BlockSpec(memory_space=pltpu.SMEM), half_spec, half_spec],
        out_specs=pl.BlockSpec((1, 1, rows, 2 * half), lambda v, p: (v, p, 0, 0)),
        out_shape=jax.ShapeDtypeStruct((mpo_count, 2, rows, 2 * half), F32),
        compiler_params=params(2),
        cost_estimate=LIGHT,
        name="finish",
    )(pick, mine, siblings)


def after(value, *earlier):
    return lax.optimization_barrier((value,) + earlier)[0]


def swap(value):
    return lax.ppermute(value, "depth", [(0, 1), (1, 0)])


def split_inputs(environment, mpo):
    depth = lax.axis_index("depth")
    w_local, half = environment.shape[0], environment.shape[3]
    cols = half // 2
    env_own = lax.dynamic_slice_in_dim(environment, depth * cols, cols, 3)
    env_sib = swap(lax.dynamic_slice_in_dim(environment, (1 - depth) * cols, cols, 3))
    mpo_mine = jnp.concatenate(
        [
            lax.dynamic_slice_in_dim(mpo, depth * w_local, w_local, 0),
            lax.dynamic_slice_in_dim(mpo, (1 - depth) * w_local, w_local, 0),
        ],
        axis=0,
    )
    return env_own, env_sib, mpo_mine


def one_product(left, right, dims):
    return jnp.einsum(dims, left, right, preferred_element_type=F32)


def any_line(environment, site_tensor, mpo):
    depth = lax.axis_index("depth")
    env_own, env_sib, mpo_mine = split_inputs(environment, mpo)
    env_own = lax.all_gather(env_own, "row", axis=2, tiled=True)
    env_sib = lax.all_gather(env_sib, "row", axis=2, tiled=True)
    env = jnp.concatenate([env_own, env_sib], axis=0)
    cols = env.shape[3]
    planar = jnp.transpose(site_tensor, (0, 2, 1, 3))
    site_own = lax.dynamic_slice_in_dim(planar, depth * cols, cols, 3)
    site = lax.all_gather(planar, "col", axis=3, tiled=True)
    first = functools.partial(one_product, dims="sxa,wac->wsxc")
    g = jnp.stack(
        [
            first(site[:, 0], env[:, 0]) + first(site[:, 1], env[:, 1]),
            first(site[:, 0], env[:, 1]) - first(site[:, 1], env[:, 0]),
        ],
        axis=2,
    )
    q = jnp.einsum("wvst,wspxc->vtpxc", mpo_mine, g, precision=lax.Precision.HIGHEST).astype(BF16)
    site = lax.all_gather(site_own, "row", axis=2, tiled=True)
    second = functools.partial(one_product, dims="vtxc,tyc->vxy")
    total = jnp.stack(
        [
            second(q[:, :, 0], site[:, 0]) - second(q[:, :, 1], site[:, 1]),
            second(q[:, :, 0], site[:, 1]) + second(q[:, :, 1], site[:, 0]),
        ],
        axis=1,
    )
    return lax.psum_scatter(total, ("col", "depth"), scatter_dimension=3, tiled=True)


def four_rows(environment, site_tensor, mpo):
    row, col, depth = (lax.axis_index(axis) for axis in ("row", "col", "depth"))
    axes = ("row", "col", "depth")
    place = lambda r, c, d: (r * 2 + c) * 2 + d
    both = lambda value: lax.ppermute(value, "row", [(0, 1), (1, 0), (2, 3), (3, 2)])
    to_host = lambda value: lax.ppermute(value, "row", [(0, 1), (3, 2)])
    to_end = lambda value: lax.ppermute(value, "row", [(1, 0), (2, 3)])
    across = lambda value: lax.ppermute(value, "row", [(1, 2), (2, 1)])
    turn = lambda value: lax.ppermute(value, "col", [(0, 1), (1, 0)])

    def to_col(value, which_rows, far):
        pairs = []
        for r in which_rows:
            goal = 1 - r // 2 if far else r // 2
            pairs += [(place(r, 1 - goal, d), place(r, goal, d)) for d in range(2)]
        return lax.ppermute(value, axes, pairs)

    in_order = lambda mine, sibling, axis: jnp.where(
        depth == 0,
        jnp.concatenate([mine, sibling], axis=axis),
        jnp.concatenate([sibling, mine], axis=axis),
    )
    is_host = (row == 1) | (row == 2)
    hosts_or = lambda at_host, at_end: jnp.where(is_host, at_host, at_end)

    env_own, env_sib, mpo_mine = split_inputs(environment, mpo)
    env = [env_own, env_sib]
    planar = jnp.transpose(after(site_tensor, env_sib), (0, 2, 1, 3))
    rows = planar.shape[2]
    half = rows // 2
    mine = lax.dynamic_slice_in_dim(planar, depth * half, half, 2)

    def rows_of(own, turned, own_swapped, turned_swapped):
        near = in_order(own, own_swapped, 2)
        other = in_order(turned, turned_swapped, 2)
        return jnp.where(col == 0, jnp.stack([near, other]), jnp.stack([other, near]))

    parts = [mine[:, :, : half // 2], mine[:, :, half // 2 :]]
    side_env, over_env = [both(one) for one in env], [across(one) for one in env]
    turned = turn(mine)
    swapped = [swap(after(value, *side_env)) for value in (mine, turned)]
    far_env, over_side_env, side_parts, there_parts, turned_parts = [], [], [], [], []
    gates = (*side_env, *over_env)
    for m in range(2):
        far_env.append(to_end(after(over_env[m], *gates)))
        over_side_env.append(across(after(side_env[m], *gates)))
        side_parts.append(to_host(after(parts[m], *gates)))
        there_parts.append(hosts_or(side_parts[m], parts[m]))
        gates = (far_env[m], over_side_env[m], side_parts[m], *swapped)
    site_here = rows_of(mine, turned, *swapped)
    turned_parts = [turn(part) for part in there_parts]
    gates = (*gates, turned_parts[0])
    over_site = across(after(mine, *gates))
    over_side_env_both = jnp.concatenate(over_side_env, axis=0)
    far_side_env = to_end(after(over_side_env_both, *gates))
    gates = (over_site, far_side_env)
    over_side_parts, host_parts = [], []
    for m in range(2):
        over_side_parts.append(across(after(side_parts[m], *gates)))
        host_parts.append(to_end(after(parts[m], *gates)))
        gates = (over_side_parts[m], host_parts[m])

    side = row ^ 1
    at_host = jnp.stack([row, side, 3 - row, 3 - side]).astype(jnp.int32)
    at_end = jnp.stack([row, side, 3 - side, 3 - row]).astype(jnp.int32)
    pick = depth.astype(jnp.int32).reshape(1)

    def first(blocks, site, envs, *earlier):
        q = first_product(blocks, mpo_mine, site, envs, half, half)
        return q, swap(after(q, *earlier))

    def second(q, sites, *earlier):
        return second_product(after(pick, *earlier), q[0], q[1], sites)

    q_here = first(at_host, site_here, env + side_env + over_env + over_side_env)
    there, turned = (
        jnp.concatenate([after(part, q_here[0]) for part in pair], axis=2)
        for pair in (there_parts, turned_parts)
    )
    site_there = rows_of(there, turned, swap(there), swap(turned))
    last_env = hosts_or(over_side_env_both, far_side_env)
    w_local = environment.shape[0]
    q_there = first(
        hosts_or(at_host, at_end),
        site_there,
        env
        + side_env
        + [hosts_or(*pair) for pair in zip(over_env, far_env)]
        + [last_env[:w_local], last_env[w_local:]],
        over_side_parts[0],
        host_parts[0],
    )
    here_over = second(q_here, [over_site], q_there[0])
    here_own = second(q_here, [mine], here_over)
    there_own = second(q_there, [hosts_or(over_site, after(mine, q_there[0]))], here_own)
    there_side = second(
        q_there, [hosts_or(*part) for part in zip(over_side_parts, host_parts)], there_own
    )
    came_here_over = to_col(here_over, (1, 2), True)
    far_there_own = to_end(there_own)
    near_own = hosts_or(here_own, there_own)
    came_near_own = to_col(near_own, range(4), False)
    far_there_side = to_end(there_side)
    here_side = second(q_here, side_parts, there_side, came_here_over)
    near_side = hosts_or(here_side, there_side)
    came_near_side = to_col(near_side, range(4), False)
    came_far_own = to_col(far_there_own, (0, 3), True)
    here_over_side = second(q_here, over_side_parts, here_side, far_there_own, came_near_own)
    came_here_over_side = to_col(here_over_side, (1, 2), True)
    came_far_side = to_col(after(far_there_side, came_far_own), (0, 3), True)

    is_near = col == row // 2
    wide = lambda value: value.astype(F32)
    one = jnp.where(
        is_near,
        wide(near_own) + wide(came_near_own),
        hosts_or(wide(here_over) + wide(came_here_over), wide(far_there_own) + wide(came_far_own)),
    )
    two = jnp.where(
        is_near,
        wide(near_side) + wide(came_near_side),
        hosts_or(wide(here_over_side) + wide(came_here_over_side), wide(far_there_side)),
    )
    one, two = lax.optimization_barrier((one, two))
    two = two + wide(came_far_side)
    one_is_mine = (depth == row % 2) ^ (is_host & ~is_near)
    kept = jnp.where(one_is_mine, one, two)
    given = jnp.where(one_is_mine, two, one).astype(BF16)
    return finish(pick, kept, swap(given))


def solution(mesh):
    placed = (
        P(("groups", "depth"), None, "row", "col"),
        P("groups", "row", None, "col"),
        P("groups", None, None, None),
    )
    fits = mesh.shape["col"] == 2 and mesh.shape["row"] == 4
    return jax.shard_map(
        four_rows if fits else any_line,
        mesh=mesh,
        in_specs=placed,
        out_specs=P("groups", None, "row", ("col", "depth")),
        check_vma=False,
    )
```

```python
import functools
import jax
import jax.numpy as jnp
from jax import lax
from jax.experimental import pallas as pl
from jax.experimental.pallas import tpu as pltpu
from jax.sharding import PartitionSpec as P

F32 = jnp.float32
BF16 = jnp.bfloat16
VMEM_BYTES = 56 * 1024 * 1024
LIGHT = pl.CostEstimate(flops=0, bytes_accessed=0, transcendentals=0)


def params(steps):
    return pltpu.CompilerParams(
        dimension_semantics=("arbitrary",) * steps, vmem_limit_bytes=VMEM_BYTES
    )


def mul(left, right):
    return jnp.dot(left, right, preferred_element_type=F32)


def mul_t(left, right):
    return lax.dot_general(left, right, (((1,), (1,)), ((), ())), preferred_element_type=F32)


def first_kernel(sources, pick_ref, mpo_ref, *refs):
    q_ref, site_ref, env_ref, g_ref, site_sems, env_sems = refs[-6:]
    site_refs, env_refs = refs[:4], refs[4:-6]
    mpo_count, phys, _, rows, cols = q_ref.shape
    w_local, _, depth, _ = env_ref.shape[1:]
    per_col = site_ref.shape[-1] // depth
    tile, col_tile = pl.program_id(0), pl.program_id(1)

    def site_copy(which, other):
        there = 1 - pick_ref[1] if other else pick_ref[1]
        return pltpu.make_async_copy(
            site_refs[other * 2 + which], site_ref.at[which, there], site_sems.at[which, other]
        )

    def env_copy(number, at_end):
        source, first = sources[number][1 if at_end and len(sources[number]) > 1 else 0]
        return pltpu.make_async_copy(
            env_refs[source].at[pl.ds(first, w_local)], env_ref.at[number], env_sems.at[number]
        )

    def start_envs(at_end):
        for number in range(len(sources)):
            env_copy(number, at_end).start()

    @pl.when((tile == 0) & (col_tile == 0))
    def _():
        for other in range(2):
            site_copy(0, other).start()
        pl.when(pick_ref[2] == 0)(functools.partial(start_envs, False))
        pl.when(pick_ref[2] != 0)(functools.partial(start_envs, True))
        for other in range(2):
            site_copy(1, other).start()
        for other in range(2):
            site_copy(0, other).wait()
        for number in range(len(sources)):
            env_copy(number, False).wait()

    @pl.when((tile == 1) & (col_tile == 0))
    def _():
        for other in range(2):
            site_copy(1, other).wait()

    columns = pl.ds(pl.multiple_of(col_tile * cols, cols), cols)
    for w in range(mpo_count):
        with_real, with_imag = None, None
        for number in range(len(sources) // 2):
            block = pick_ref[3 + number]
            piece = pl.ds(pl.multiple_of((block % per_col) * depth, depth), depth)
            left = site_ref[tile, block // per_col, :, :, :, piece].reshape(phys * 2 * rows, depth)
            env = number * 2 + w // w_local
            more_real = mul(left, env_ref[env, w % w_local, 0, :, columns])
            more_imag = mul(left, env_ref[env, w % w_local, 1, :, columns])
            with_real = more_real if with_real is None else with_real + more_real
            with_imag = more_imag if with_imag is None else with_imag + more_imag
        for s in range(phys):
            real, imag = (slice((2 * s + part) * rows, (2 * s + part + 1) * rows) for part in range(2))
            there = slice(s * rows, (s + 1) * rows)
            g_ref[w, 0, there] = with_real[real] + with_imag[imag]
            g_ref[w, 1, there] = with_imag[real] - with_real[imag]
    for part in range(2):
        for v in range(mpo_count):
            for t in range(phys):
                total = None
                for w in range(mpo_count):
                    for s in range(phys):
                        term = mpo_ref[w, v, s, t] * g_ref[w, part, s * rows : (s + 1) * rows]
                        total = term if total is None else total + term
                q_ref[v, t, part] = total.astype(BF16)


def first_product(pick, mpo, site, envs, col_tile):
    phys, _, half, wide = site[0].shape
    arrays, sources = [], []
    for choices in envs:
        sources.append([])
        for array, start in choices:
            known = [number for number, one in enumerate(arrays) if one is array]
            if not known:
                arrays.append(array)
            sources[-1].append((known[0] if known else len(arrays) - 1, start))
    _, _, depth, cols = arrays[0].shape
    mpo_count = mpo.shape[1]
    w_local = mpo_count // 2
    anywhere = pl.BlockSpec(memory_space=pl.ANY)
    return pl.pallas_call(
        functools.partial(first_kernel, sources),
        grid_spec=pltpu.PrefetchScalarGridSpec(
            num_scalar_prefetch=1,
            grid=(2, cols // col_tile),
            in_specs=[pl.BlockSpec(memory_space=pltpu.SMEM)] + [anywhere] * (4 + len(arrays)),
            out_specs=pl.BlockSpec(
                (mpo_count, phys, 2, half, col_tile),
                lambda i, j, pick: (0, 0, 0, jnp.where(i == 0, pick[0], 1 - pick[0]), j),
            ),
            scratch_shapes=[
                pltpu.VMEM((2, 2, phys, 2, half, wide), BF16),
                pltpu.VMEM((len(sources), w_local, 2, depth, cols), BF16),
                pltpu.VMEM((mpo_count, 2, phys * half, col_tile), F32),
                pltpu.SemaphoreType.DMA((2, 2)),
                pltpu.SemaphoreType.DMA((len(sources),)),
            ],
        ),
        out_shape=jax.ShapeDtypeStruct((mpo_count, phys, 2, 2 * half, cols), BF16),
        compiler_params=params(2),
        cost_estimate=LIGHT,
        name="first_product",
    )(pick, mpo, *site, *arrays)


def second_kernel(groups, pick_ref, own_ref, sib_ref, *refs):
    count = len(groups)
    sems, scratch = refs[-1], refs[-1 - count : -1]
    out_refs = refs[-1 - 2 * count : -1 - count]
    site_refs = refs[: -1 - 2 * count]
    phys, _, rows, cols = own_ref.shape[1:]

    def copies(at_end):
        sem = 0
        for group, (parts, y_rows) in enumerate(groups):
            first = 0
            for choices, extent in parts:
                source = site_refs[choices[-1] if at_end else choices[0]]
                for part in range(2):
                    there = scratch[group].at[:, pl.ds(part * y_rows + first, extent)]
                    yield pltpu.make_async_copy(source.at[:, part], there, sems.at[sem])
                    sem += 1
                first += extent

    def start(at_end):
        for copy in copies(at_end):
            copy.start()

    @pl.when(pl.program_id(0) == 0)
    def _():
        pl.when(pick_ref[2] == 0)(functools.partial(start, False))
        pl.when(pick_ref[2] != 0)(functools.partial(start, True))
        for copy in copies(False):
            copy.wait()

    for (_, width), site_ref, out_ref in zip(groups, scratch, out_refs):
        total = None
        for q_ref, quarter in ((own_ref, pick_ref[0]), (sib_ref, 1 - pick_ref[0])):
            piece = pl.ds(pl.multiple_of(quarter * cols, cols), cols)
            for t in range(phys):
                more = mul_t(q_ref[0, t].reshape(2 * rows, cols), site_ref[t, :, piece])
                total = more if total is None else total + more
        out_ref[0, 0] = (total[:rows, :width] - total[rows:, width:]).astype(BF16)
        out_ref[0, 1] = (total[:rows, width:] + total[rows:, :width]).astype(BF16)


def second_product(pick, own, sib, site_groups):
    mpo_count, phys, _, rows, cols = own.shape
    arrays, groups = [], []
    for group in site_groups:
        parts = []
        for choices in group:
            choices = choices if isinstance(choices, tuple) else (choices,)
            parts.append((list(range(len(arrays), len(arrays) + len(choices))), choices[0].shape[2]))
            arrays += choices
        groups.append((parts, sum(extent for _, extent in parts)))
    wide = arrays[0].shape[3]
    q_spec = pl.BlockSpec((1, phys, 2, rows, cols), lambda v, pick: (v, 0, 0, 0, 0))
    widths = [width for _, width in groups]
    return pl.pallas_call(
        functools.partial(second_kernel, groups),
        grid_spec=pltpu.PrefetchScalarGridSpec(
            num_scalar_prefetch=1,
            grid=(mpo_count,),
            in_specs=[q_spec, q_spec] + [pl.BlockSpec(memory_space=pl.ANY)] * len(arrays),
            out_specs=[pl.BlockSpec((1, 2, rows, width), lambda v, pick: (v, 0, 0, 0)) for width in widths],
            scratch_shapes=[pltpu.VMEM((phys, 2 * width, wide), BF16) for width in widths]
            + [pltpu.SemaphoreType.DMA((2 * sum(len(parts) for parts, _ in groups),))],
        ),
        out_shape=[jax.ShapeDtypeStruct((mpo_count, 2, rows, width), BF16) for width in widths],
        compiler_params=params(1),
        cost_estimate=LIGHT,
        name="second_product",
    )(pick, own, sib, *arrays)


def finish_kernel(pick_ref, mine_ref, siblings_ref, out_ref):
    half = mine_ref.shape[3]
    for ref, core in ((mine_ref, pick_ref[0]), (siblings_ref, 1 - pick_ref[0])):
        out_ref[0, 0, :, pl.ds(pl.multiple_of(core * half, half), half)] = ref[0, 0].astype(F32)


def finish(pick, mine, siblings):
    mpo_count, _, rows, half = mine.shape
    half_spec = pl.BlockSpec((1, 1, rows, half), lambda v, p: (v, p, 0, 0))
    return pl.pallas_call(
        finish_kernel,
        grid=(mpo_count, 2),
        in_specs=[pl.BlockSpec(memory_space=pltpu.SMEM), half_spec, half_spec],
        out_specs=pl.BlockSpec((1, 1, rows, 2 * half), lambda v, p: (v, p, 0, 0)),
        out_shape=jax.ShapeDtypeStruct((mpo_count, 2, rows, 2 * half), F32),
        compiler_params=params(2),
        cost_estimate=LIGHT,
        name="finish",
    )(pick, mine, siblings)


def after(value, *earlier):
    return lax.optimization_barrier((value,) + earlier)[0]


def swap(value):
    return lax.ppermute(value, "depth", [(0, 1), (1, 0)])


def split_inputs(environment, mpo):
    depth = lax.axis_index("depth")
    w_local, half = environment.shape[0], environment.shape[3]
    cols = half // 2
    env_own = lax.dynamic_slice_in_dim(environment, depth * cols, cols, 3)
    env_sib = swap(lax.dynamic_slice_in_dim(environment, (1 - depth) * cols, cols, 3))
    mpo_mine = jnp.concatenate(
        [
            lax.dynamic_slice_in_dim(mpo, depth * w_local, w_local, 0),
            lax.dynamic_slice_in_dim(mpo, (1 - depth) * w_local, w_local, 0),
        ],
        axis=0,
    )
    return env_own, env_sib, mpo_mine


def one_product(left, right, dims):
    return jnp.einsum(dims, left, right, preferred_element_type=F32)


def any_line(environment, site_tensor, mpo):
    depth = lax.axis_index("depth")
    env_own, env_sib, mpo_mine = split_inputs(environment, mpo)
    env_own = lax.all_gather(env_own, "row", axis=2, tiled=True)
    env_sib = lax.all_gather(env_sib, "row", axis=2, tiled=True)
    env = jnp.concatenate([env_own, env_sib], axis=0)
    cols = env.shape[3]
    planar = jnp.transpose(site_tensor, (0, 2, 1, 3))
    site_own = lax.dynamic_slice_in_dim(planar, depth * cols, cols, 3)
    site = lax.all_gather(planar, "col", axis=3, tiled=True)
    first = functools.partial(one_product, dims="sxa,wac->wsxc")
    g = jnp.stack(
        [
            first(site[:, 0], env[:, 0]) + first(site[:, 1], env[:, 1]),
            first(site[:, 0], env[:, 1]) - first(site[:, 1], env[:, 0]),
        ],
        axis=2,
    )
    q = jnp.einsum("wvst,wspxc->vtpxc", mpo_mine, g, precision=lax.Precision.HIGHEST).astype(BF16)
    site = lax.all_gather(site_own, "row", axis=2, tiled=True)
    second = functools.partial(one_product, dims="vtxc,tyc->vxy")
    total = jnp.stack(
        [
            second(q[:, :, 0], site[:, 0]) - second(q[:, :, 1], site[:, 1]),
            second(q[:, :, 0], site[:, 1]) + second(q[:, :, 1], site[:, 0]),
        ],
        axis=1,
    )
    return lax.psum_scatter(total, ("col", "depth"), scatter_dimension=3, tiled=True)


def four_rows(environment, site_tensor, mpo):
    row, col, depth = (lax.axis_index(axis) for axis in ("row", "col", "depth"))
    axes = ("row", "col", "depth")
    place = lambda r, c, d: (r * 2 + c) * 2 + d
    both = lambda value: lax.ppermute(value, "row", [(0, 1), (1, 0), (2, 3), (3, 2)])
    to_host = lambda value: lax.ppermute(value, "row", [(0, 1), (3, 2)])
    to_end = lambda value: lax.ppermute(value, "row", [(1, 0), (2, 3)])
    across = lambda value: lax.ppermute(value, "row", [(1, 2), (2, 1)])
    turn = lambda value: lax.ppermute(value, "col", [(0, 1), (1, 0)])

    def to_col(value, which_rows, far):
        pairs = []
        for r in which_rows:
            goal = 1 - r // 2 if far else r // 2
            pairs += [(place(r, 1 - goal, d), place(r, goal, d)) for d in range(2)]
        return lax.ppermute(value, axes, pairs)

    is_host = (row == 1) | (row == 2)
    hosts_or = lambda at_host, at_end: jnp.where(is_host, at_host, at_end)

    env_own, env_sib, mpo_mine = split_inputs(environment, mpo)
    w_local = environment.shape[0]
    env = [env_own, env_sib]
    side_env, over_env = [both(env_own)], [across(env_own)]
    second_part = after(env_sib, side_env[0], over_env[0])
    side_env.append(both(second_part))
    over_env.append(across(second_part))

    planar = jnp.transpose(after(site_tensor, env_sib), (0, 2, 1, 3))
    half = planar.shape[2] // 2
    mine = lax.dynamic_slice_in_dim(planar, depth * half, half, 2)
    parts = [mine[:, :, : half // 2], mine[:, :, half // 2 :]]
    turned = turn(mine)
    site_here = [mine, swap(after(mine, *side_env)), turned, swap(after(turned, *side_env))]
    far_env, over_side_env, side_parts = [], [], []
    gates = (*side_env, *over_env)
    for m in range(2):
        far_env.append(to_end(after(over_env[m], *gates)))
        over_side_env.append(across(after(side_env[m], *gates)))
        side_parts.append(to_host(after(parts[m], *gates)))
        gates = (far_env[m], over_side_env[m], side_parts[m], *site_here[1::2])
    there_parts = [hosts_or(side_parts[0], parts[0])]
    turned_parts = [turn(there_parts[0])]
    there_parts.append(hosts_or(side_parts[1], after(parts[1], turned_parts[0])))
    turned_parts.append(turn(there_parts[1]))
    gates = (*gates, turned_parts[0])
    over_site = across(after(mine, *gates))
    far_side_env = to_end(after(jnp.concatenate(over_side_env, axis=0), *gates))
    gates = (over_site, far_side_env)
    over_side_parts, host_parts = [], []
    for m in range(2):
        over_side_parts.append(across(after(side_parts[m], *gates)))
        host_parts.append(to_end(after(parts[m], *gates)))
        gates = (over_side_parts[m], host_parts[m])

    side = row ^ 1
    at_host, at_end = (row, side, 3 - row, 3 - side), (row, side, 3 - side, 3 - row)
    pick_here = jnp.stack([depth, col, 0 * row, *at_host]).astype(jnp.int32)
    pick_there = jnp.stack(
        [depth, col, hosts_or(0, 1), *[hosts_or(*pair) for pair in zip(at_host, at_end)]]
    ).astype(jnp.int32)
    pick = pick_there[:3]

    def second(q, site_groups, *earlier):
        outs = second_product(after(pick, *earlier), q[0], q[1], site_groups)
        return outs if len(outs) > 1 else outs[0]

    whole = lambda arrays: [[(one, 0)] for one in arrays]
    q_here = first_product(
        pick_here, mpo_mine, site_here, whole(env + side_env + over_env + over_side_env), half
    )
    there, turned = (
        jnp.concatenate([after(part, q_here) for part in pair], axis=2)
        for pair in (there_parts, turned_parts)
    )
    q_there = first_product(
        pick_there,
        mpo_mine,
        [there, swap(there), turned, swap(turned)],
        whole(env + side_env)
        + [[(at_host, 0), (at_end, 0)] for at_host, at_end in zip(over_env, far_env)]
        + [[(over_side_env[m], 0), (far_side_env, m * w_local)] for m in range(2)],
        half,
    )
    q_here = (q_here, swap(q_here))
    q_there = (q_there, swap(after(q_there, over_side_parts[0], host_parts[0])))
    here_over, here_own = second(q_here, [[over_site], [mine]], q_there[0])
    there_own = second(q_there, [[(over_site, mine)]], here_own)
    there_side = second(q_there, [list(zip(over_side_parts, host_parts))], there_own)
    came_here_over = to_col(here_over, (1, 2), True)
    far_there_own = to_end(there_own)
    near_own = hosts_or(here_own, there_own)
    came_near_own = to_col(near_own, range(4), False)
    far_there_side = to_end(there_side)
    here_side, here_over_side = second(
        q_here, [side_parts, over_side_parts], there_side, came_here_over, far_there_own, came_near_own
    )
    near_side = hosts_or(here_side, there_side)
    came_near_side = to_col(near_side, range(4), False)
    came_far_own = to_col(far_there_own, (0, 3), True)
    came_here_over_side = to_col(here_over_side, (1, 2), True)
    came_far_side = to_col(after(far_there_side, came_far_own), (0, 3), True)

    is_near = col == row // 2
    wide = lambda value: value.astype(F32)
    one = jnp.where(
        is_near,
        wide(near_own) + wide(came_near_own),
        hosts_or(wide(here_over) + wide(came_here_over), wide(far_there_own) + wide(came_far_own)),
    )
    two = jnp.where(
        is_near,
        wide(near_side) + wide(came_near_side),
        hosts_or(wide(here_over_side) + wide(came_here_over_side), wide(far_there_side)),
    )
    one, two = lax.optimization_barrier((one, two))
    two = two + wide(came_far_side)
    one_is_mine = (depth == row % 2) ^ (is_host & ~is_near)
    kept = jnp.where(one_is_mine, one, two)
    given = jnp.where(one_is_mine, two, one).astype(BF16)
    return finish(pick, kept, swap(given))


def solution(mesh):
    placed = (
        P(("groups", "depth"), None, "row", "col"),
        P("groups", "row", None, "col"),
        P("groups", None, None, None),
    )
    fits = mesh.shape["col"] == 2 and mesh.shape["row"] == 4
    return jax.shard_map(
        four_rows if fits else any_line,
        mesh=mesh,
        in_specs=placed,
        out_specs=P("groups", None, "row", ("col", "depth")),
        check_vma=False,
    )
```

```python
import functools
import jax
import jax.numpy as jnp
from jax import lax
from jax.experimental import pallas as pl
from jax.experimental.pallas import tpu as pltpu
from jax.sharding import PartitionSpec as P

F32 = jnp.float32
BF16 = jnp.bfloat16
VMEM_BYTES = 56 * 1024 * 1024
LIGHT = pl.CostEstimate(flops=0, bytes_accessed=0, transcendentals=0)


def params(steps):
    return pltpu.CompilerParams(
        dimension_semantics=("arbitrary",) * steps, vmem_limit_bytes=VMEM_BYTES
    )


def mul(left, right):
    return jnp.dot(left, right, preferred_element_type=F32)


def mul_t(left, right):
    return lax.dot_general(left, right, (((1,), (1,)), ((), ())), preferred_element_type=F32)


def first_kernel(site_sources, sources, pick_ref, mpo_ref, *refs):
    q_ref, site_ref, env_ref, g_ref, site_sems, env_sems = refs[-6:]
    source_refs = refs[:-6]
    mpo_count, phys, _, rows, cols = q_ref.shape
    w_local, _, depth, _ = env_ref.shape[1:]
    per_col = site_ref.shape[-1] // depth
    tile, col_tile = pl.program_id(0), pl.program_id(1)

    def start_site(which, at_end):
        for col in range(site_ref.shape[1]):
            first = 0
            for source in site_sources[-1 if at_end else 0]:
                extent = source_refs[source].shape[3]
                pltpu.make_async_copy(
                    source_refs[source].at[col * 2 + which],
                    site_ref.at[which, col, :, :, pl.ds(first, extent)],
                    site_sems.at[which, col],
                ).start()
                first += extent

    def wait_site(which):
        for col in range(site_ref.shape[1]):
            there = site_ref.at[which, col]
            pltpu.make_async_copy(there, there, site_sems.at[which, col]).wait()

    def env_copy(number, at_end):
        source, first = sources[number][-1 if at_end else 0]
        return pltpu.make_async_copy(
            source_refs[source].at[pl.ds(first, w_local)], env_ref.at[number], env_sems.at[number]
        )

    def start(at_end):
        start_site(0, at_end)
        for number in range(len(sources)):
            env_copy(number, at_end).start()
        start_site(1, at_end)

    @pl.when((tile == 0) & (col_tile == 0))
    def _():
        pl.when(pick_ref[1] == 0)(functools.partial(start, False))
        pl.when(pick_ref[1] != 0)(functools.partial(start, True))
        wait_site(0)
        for number in range(len(sources)):
            env_copy(number, False).wait()

    @pl.when((tile == 1) & (col_tile == 0))
    def _():
        wait_site(1)

    columns = pl.ds(pl.multiple_of(col_tile * cols, cols), cols)
    for w in range(mpo_count):
        with_real, with_imag = None, None
        for number in range(len(sources) // 2):
            block = pick_ref[2 + number]
            piece = pl.ds(pl.multiple_of((block % per_col) * depth, depth), depth)
            left = site_ref[tile, block // per_col, :, :, :, piece].reshape(phys * 2 * rows, depth)
            env = number * 2 + w // w_local
            more_real = mul(left, env_ref[env, w % w_local, 0, :, columns])
            more_imag = mul(left, env_ref[env, w % w_local, 1, :, columns])
            with_real = more_real if with_real is None else with_real + more_real
            with_imag = more_imag if with_imag is None else with_imag + more_imag
        for s in range(phys):
            real, imag = (slice((2 * s + part) * rows, (2 * s + part + 1) * rows) for part in range(2))
            there = slice(s * rows, (s + 1) * rows)
            g_ref[w, 0, there] = with_real[real] + with_imag[imag]
            g_ref[w, 1, there] = with_imag[real] - with_real[imag]
    for part in range(2):
        for v in range(mpo_count):
            for t in range(phys):
                total = None
                for w in range(mpo_count):
                    for s in range(phys):
                        term = mpo_ref[w, v, s, t] * g_ref[w, part, s * rows : (s + 1) * rows]
                        total = term if total is None else total + term
                q_ref[v, t, part] = total.astype(BF16)


def first_product(pick, mpo, sites, envs, col_tile):
    arrays = []

    def number_of(array):
        for number, one in enumerate(arrays):
            if one is array:
                return number
        arrays.append(array)
        return len(arrays) - 1

    site_sources = [[number_of(one) for one in choice] for choice in sites]
    sources = [[(number_of(one), start) for one, start in choices] for choices in envs]
    pieces, phys, _, _, wide = sites[0][0].shape
    half = sum(one.shape[3] for one in sites[0])
    _, _, depth, cols = envs[0][0][0].shape
    mpo_count = mpo.shape[1]
    w_local = mpo_count // 2
    return pl.pallas_call(
        functools.partial(first_kernel, site_sources, sources),
        grid_spec=pltpu.PrefetchScalarGridSpec(
            num_scalar_prefetch=1,
            grid=(2, cols // col_tile),
            in_specs=[pl.BlockSpec(memory_space=pltpu.SMEM)]
            + [pl.BlockSpec(memory_space=pl.ANY)] * len(arrays),
            out_specs=pl.BlockSpec(
                (mpo_count, phys, 2, half, col_tile), lambda i, j, pick: (0, 0, 0, i, j)
            ),
            scratch_shapes=[
                pltpu.VMEM((2, pieces // 2, phys, 2, half, wide), BF16),
                pltpu.VMEM((len(sources), w_local, 2, depth, cols), BF16),
                pltpu.VMEM((mpo_count, 2, phys * half, col_tile), F32),
                pltpu.SemaphoreType.DMA((2, pieces // 2)),
                pltpu.SemaphoreType.DMA((len(sources),)),
            ],
        ),
        out_shape=jax.ShapeDtypeStruct((mpo_count, phys, 2, 2 * half, cols), BF16),
        compiler_params=params(2),
        cost_estimate=LIGHT,
        name="first_product",
    )(pick, mpo, *arrays)


def second_kernel(groups, pick_ref, own_ref, sib_ref, *refs):
    count = len(groups)
    sems, scratch = refs[-1], refs[-1 - count : -1]
    out_refs = refs[-1 - 2 * count : -1 - count]
    site_refs = refs[: -1 - 2 * count]
    phys, _, rows, cols = own_ref.shape[1:]

    def copies(at_end):
        sem = 0
        for group, (parts, y_rows) in enumerate(groups):
            first = 0
            for choices, extent in parts:
                source = site_refs[choices[-1] if at_end else choices[0]]
                for part in range(2):
                    there = scratch[group].at[:, pl.ds(part * y_rows + first, extent)]
                    yield pltpu.make_async_copy(source.at[:, part], there, sems.at[sem])
                    sem += 1
                first += extent

    def start(at_end):
        for copy in copies(at_end):
            copy.start()

    @pl.when(pl.program_id(0) == 0)
    def _():
        pl.when(pick_ref[1] == 0)(functools.partial(start, False))
        pl.when(pick_ref[1] != 0)(functools.partial(start, True))
        for copy in copies(False):
            copy.wait()

    for (_, width), site_ref, out_ref in zip(groups, scratch, out_refs):
        total = None
        for q_ref, quarter in ((own_ref, pick_ref[0]), (sib_ref, 1 - pick_ref[0])):
            piece = pl.ds(pl.multiple_of(quarter * cols, cols), cols)
            for t in range(phys):
                more = mul_t(q_ref[0, t].reshape(2 * rows, cols), site_ref[t, :, piece])
                total = more if total is None else total + more
        out_ref[0, 0] = (total[:rows, :width] - total[rows:, width:]).astype(BF16)
        out_ref[0, 1] = (total[:rows, width:] + total[rows:, :width]).astype(BF16)


def second_product(pick, own, sib, site_groups):
    mpo_count, phys, _, rows, cols = own.shape
    arrays, groups = [], []
    for group in site_groups:
        parts = []
        for choices in group:
            choices = choices if isinstance(choices, tuple) else (choices,)
            parts.append((list(range(len(arrays), len(arrays) + len(choices))), choices[0].shape[2]))
            arrays += choices
        groups.append((parts, sum(extent for _, extent in parts)))
    wide = arrays[0].shape[3]
    q_spec = pl.BlockSpec((1, phys, 2, rows, cols), lambda v, pick: (v, 0, 0, 0, 0))
    widths = [width for _, width in groups]
    return pl.pallas_call(
        functools.partial(second_kernel, groups),
        grid_spec=pltpu.PrefetchScalarGridSpec(
            num_scalar_prefetch=1,
            grid=(mpo_count,),
            in_specs=[q_spec, q_spec] + [pl.BlockSpec(memory_space=pl.ANY)] * len(arrays),
            out_specs=[pl.BlockSpec((1, 2, rows, width), lambda v, pick: (v, 0, 0, 0)) for width in widths],
            scratch_shapes=[pltpu.VMEM((phys, 2 * width, wide), BF16) for width in widths]
            + [pltpu.SemaphoreType.DMA((2 * sum(len(parts) for parts, _ in groups),))],
        ),
        out_shape=[jax.ShapeDtypeStruct((mpo_count, 2, rows, width), BF16) for width in widths],
        compiler_params=params(1),
        cost_estimate=LIGHT,
        name="second_product",
    )(pick, own, sib, *arrays)


def finish_kernel(pick_ref, mine_ref, siblings_ref, out_ref):
    half = mine_ref.shape[3]
    for ref, core in ((mine_ref, pick_ref[0]), (siblings_ref, 1 - pick_ref[0])):
        out_ref[0, 0, :, pl.ds(pl.multiple_of(core * half, half), half)] = ref[0, 0].astype(F32)


def finish(pick, mine, siblings):
    mpo_count, _, rows, half = mine.shape
    half_spec = pl.BlockSpec((1, 1, rows, half), lambda v, p: (v, p, 0, 0))
    return pl.pallas_call(
        finish_kernel,
        grid=(mpo_count, 2),
        in_specs=[pl.BlockSpec(memory_space=pltpu.SMEM), half_spec, half_spec],
        out_specs=pl.BlockSpec((1, 1, rows, 2 * half), lambda v, p: (v, p, 0, 0)),
        out_shape=jax.ShapeDtypeStruct((mpo_count, 2, rows, 2 * half), F32),
        compiler_params=params(2),
        cost_estimate=LIGHT,
        name="finish",
    )(pick, mine, siblings)


def after(value, *earlier):
    return lax.optimization_barrier((value,) + earlier)[0]


def swap(value):
    return lax.ppermute(value, "depth", [(0, 1), (1, 0)])


def split_inputs(environment, mpo):
    depth = lax.axis_index("depth")
    w_local, half = environment.shape[0], environment.shape[3]
    cols = half // 2
    env_own = lax.dynamic_slice_in_dim(environment, depth * cols, cols, 3)
    env_sib = swap(lax.dynamic_slice_in_dim(environment, (1 - depth) * cols, cols, 3))
    mpo_mine = jnp.concatenate(
        [
            lax.dynamic_slice_in_dim(mpo, depth * w_local, w_local, 0),
            lax.dynamic_slice_in_dim(mpo, (1 - depth) * w_local, w_local, 0),
        ],
        axis=0,
    )
    return env_own, env_sib, mpo_mine


def one_product(left, right, dims):
    return jnp.einsum(dims, left, right, preferred_element_type=F32)


def any_line(environment, site_tensor, mpo):
    depth = lax.axis_index("depth")
    env_own, env_sib, mpo_mine = split_inputs(environment, mpo)
    env_own = lax.all_gather(env_own, "row", axis=2, tiled=True)
    env_sib = lax.all_gather(env_sib, "row", axis=2, tiled=True)
    env = jnp.concatenate([env_own, env_sib], axis=0)
    cols = env.shape[3]
    planar = jnp.transpose(site_tensor, (0, 2, 1, 3))
    site_own = lax.dynamic_slice_in_dim(planar, depth * cols, cols, 3)
    site = lax.all_gather(planar, "col", axis=3, tiled=True)
    first = functools.partial(one_product, dims="sxa,wac->wsxc")
    g = jnp.stack(
        [
            first(site[:, 0], env[:, 0]) + first(site[:, 1], env[:, 1]),
            first(site[:, 0], env[:, 1]) - first(site[:, 1], env[:, 0]),
        ],
        axis=2,
    )
    q = jnp.einsum("wvst,wspxc->vtpxc", mpo_mine, g, precision=lax.Precision.HIGHEST).astype(BF16)
    site = lax.all_gather(site_own, "row", axis=2, tiled=True)
    second = functools.partial(one_product, dims="vtxc,tyc->vxy")
    total = jnp.stack(
        [
            second(q[:, :, 0], site[:, 0]) - second(q[:, :, 1], site[:, 1]),
            second(q[:, :, 0], site[:, 1]) + second(q[:, :, 1], site[:, 0]),
        ],
        axis=1,
    )
    return lax.psum_scatter(total, ("col", "depth"), scatter_dimension=3, tiled=True)


def four_rows(environment, site_tensor, mpo):
    row, col, depth = (lax.axis_index(axis) for axis in ("row", "col", "depth"))
    axes = ("row", "col", "depth")
    place = lambda r, c, d: (r * 2 + c) * 2 + d
    both = lambda value: lax.ppermute(value, "row", [(0, 1), (1, 0), (2, 3), (3, 2)])
    to_host = lambda value: lax.ppermute(value, "row", [(0, 1), (3, 2)])
    to_end = lambda value: lax.ppermute(value, "row", [(1, 0), (2, 3)])
    across = lambda value: lax.ppermute(value, "row", [(1, 2), (2, 1)])
    turn = lambda value: lax.ppermute(value, "col", [(0, 1), (1, 0)])

    def to_col(value, which_rows, far):
        pairs = []
        for r in which_rows:
            goal = 1 - r // 2 if far else r // 2
            pairs += [(place(r, 1 - goal, d), place(r, goal, d)) for d in range(2)]
        return lax.ppermute(value, axes, pairs)

    is_host = (row == 1) | (row == 2)
    hosts_or = lambda at_host, at_end: jnp.where(is_host, at_host, at_end)

    env_own, env_sib, mpo_mine = split_inputs(environment, mpo)
    w_local = environment.shape[0]
    env = [env_own, env_sib]
    planar = jnp.transpose(after(site_tensor, env_sib), (0, 2, 1, 3))
    half = planar.shape[2] // 2
    mine = lax.dynamic_slice_in_dim(planar, depth * half, half, 2)
    parts = [mine[:, :, : half // 2], mine[:, :, half // 2 :]]
    gather = lambda value: lax.all_gather(value, ("col", "depth"), axis=0)
    site_here = gather(mine)

    side_env, over_env = [both(one) for one in env], [across(one) for one in env]
    far_env, over_side_env, side_parts = [], [], []
    for m in range(2):
        far_env.append(to_end(after(over_env[m], side_env[m])))
        over_side_env.append(across(after(side_env[m], over_env[m])))
        gates = (side_env[1], over_env[1]) if m == 0 else (side_parts[0], far_env[0], over_side_env[0])
        side_parts.append(to_host(after(parts[m], *gates)))
    over_site = [across(after(parts[m], over_side_env[m])) for m in range(2)]
    far_side_env = [to_end(after(over_side_env[m], far_env[m])) for m in range(2)]
    site_there = [gather(after(side_parts[m], far_env[m], over_side_env[m])) for m in range(2)]

    side = row ^ 1
    at_host, at_end = (row, side, 3 - row, 3 - side), (row, side, 3 - side, 3 - row)
    pick_here = jnp.stack([depth, 0 * row, *at_host]).astype(jnp.int32)
    pick_there = jnp.stack(
        [depth, hosts_or(0, 1), *[hosts_or(*pair) for pair in zip(at_host, at_end)]]
    ).astype(jnp.int32)
    pick = pick_there[:2]

    def second(q, site_groups, *earlier):
        outs = second_product(after(pick, *earlier), q[0], q[1], site_groups)
        return outs if len(outs) > 1 else outs[0]

    q_here = first_product(
        pick_here,
        mpo_mine,
        [[site_here]],
        [[(one, 0)] for one in env + side_env + over_env + over_side_env],
        half,
    )
    over_side_parts, host_parts = [], []
    gates = (*over_site, *far_side_env, q_here)
    for m in range(2):
        over_side_parts.append(across(after(side_parts[m], *gates)))
        host_parts.append(to_end(after(parts[m], *gates)))
        gates = (over_side_parts[0], host_parts[0])
    q_there = first_product(
        after(pick_there, q_here),
        mpo_mine,
        [site_there, [site_here]],
        [[(one, 0)] for one in env + side_env]
        + [[(at_host, 0), (at_end, 0)] for at_host, at_end in zip(over_env + over_side_env, far_env + far_side_env)],
        half,
    )
    q_here = (q_here, swap(q_here))
    q_there = (q_there, swap(after(q_there, over_side_parts[0], host_parts[0])))
    there_own = second(q_there, [list(zip(over_site, parts))])
    here_over, here_own = second(q_here, [over_site, parts], there_own)
    there_side = second(q_there, [list(zip(over_side_parts, host_parts))], here_own)
    far_there_own = to_end(there_own)
    came_here_over = to_col(here_over, (1, 2), True)
    near_own = hosts_or(here_own, there_own)
    came_near_own = to_col(near_own, range(4), False)
    far_there_side = to_end(there_side)
    here_side, here_over_side = second(
        q_here, [side_parts, over_side_parts], there_side, came_here_over, far_there_own, came_near_own
    )
    near_side = hosts_or(here_side, there_side)
    came_far_own = to_col(far_there_own, (0, 3), True)
    came_near_side = to_col(after(near_side, came_far_own), range(4), False)
    came_here_over_side = to_col(here_over_side, (1, 2), True)
    came_far_side = to_col(after(far_there_side, came_far_own), (0, 3), True)

    is_near = col == row // 2
    wide = lambda value: value.astype(F32)
    one = jnp.where(
        is_near,
        wide(near_own) + wide(came_near_own),
        hosts_or(wide(here_over) + wide(came_here_over), wide(far_there_own) + wide(came_far_own)),
    )
    two = jnp.where(
        is_near,
        wide(near_side) + wide(came_near_side),
        hosts_or(wide(here_over_side) + wide(came_here_over_side), wide(far_there_side)),
    )
    one, two = lax.optimization_barrier((one, two))
    two = two + wide(came_far_side)
    one_is_mine = (depth == row % 2) ^ (is_host & ~is_near)
    kept = jnp.where(one_is_mine, one, two)
    given = jnp.where(one_is_mine, two, one).astype(BF16)
    return finish(pick, kept, swap(given))


def solution(mesh):
    placed = (
        P(("groups", "depth"), None, "row", "col"),
        P("groups", "row", None, "col"),
        P("groups", None, None, None),
    )
    fits = mesh.shape["col"] == 2 and mesh.shape["row"] == 4
    return jax.shard_map(
        four_rows if fits else any_line,
        mesh=mesh,
        in_specs=placed,
        out_specs=P("groups", None, "row", ("col", "depth")),
        check_vma=False,
    )
```

```python
import functools
import jax
import jax.numpy as jnp
from jax import lax
from jax.experimental import pallas as pl
from jax.experimental.pallas import tpu as pltpu
from jax.sharding import PartitionSpec as P

F32 = jnp.float32
BF16 = jnp.bfloat16
VMEM_BYTES = 56 * 1024 * 1024
LIGHT = pl.CostEstimate(flops=0, bytes_accessed=0, transcendentals=0)


def params(steps):
    return pltpu.CompilerParams(
        dimension_semantics=("arbitrary",) * steps, vmem_limit_bytes=VMEM_BYTES
    )


def mul(left, right):
    return jnp.dot(left, right, preferred_element_type=F32)


def mul_t(left, right):
    return lax.dot_general(left, right, (((1,), (1,)), ((), ())), preferred_element_type=F32)


def first_kernel(w_local, block_ref, mpo_ref, site_ref, *refs):
    q_ref, g_ref = refs[-2:]
    env_refs = refs[:-2]
    mpo_count, phys, _, rows, _ = q_ref.shape
    depth = env_refs[0].shape[2]
    per_col = site_ref.shape[-1] // depth
    for which in range(2):
        for w in range(w_local):
            with_real, with_imag = None, None
            for number in range(len(env_refs) // 2):
                block = block_ref[number]
                piece = pl.ds(pl.multiple_of((block % per_col) * depth, depth), depth)
                left = site_ref[block // per_col, :, :, :, piece].reshape(phys * 2 * rows, depth)
                env_ref = env_refs[number * 2 + which]
                more_real, more_imag = mul(left, env_ref[w, 0]), mul(left, env_ref[w, 1])
                with_real = more_real if with_real is None else with_real + more_real
                with_imag = more_imag if with_imag is None else with_imag + more_imag
            for s in range(phys):
                real, imag = (slice((2 * s + part) * rows, (2 * s + part + 1) * rows) for part in range(2))
                there = slice(s * rows, (s + 1) * rows)
                g_ref[which * w_local + w, 0, there] = with_real[real] + with_imag[imag]
                g_ref[which * w_local + w, 1, there] = with_imag[real] - with_real[imag]
    for part in range(2):
        for v in range(mpo_count):
            for t in range(phys):
                total = None
                for w in range(2 * w_local):
                    for s in range(phys):
                        term = mpo_ref[w, v, s, t] * g_ref[w, part, s * rows : (s + 1) * rows]
                        total = term if total is None else total + term
                q_ref[v, t, part] = total.astype(BF16)


def first_product(blocks, mpo, site, envs, row_tile, col_tile):
    col_count, phys, _, rows, wide = site.shape
    w_local, _, depth, cols = envs[0].shape
    mpo_count = mpo.shape[1]
    smem = pl.BlockSpec(memory_space=pltpu.SMEM)
    return pl.pallas_call(
        functools.partial(first_kernel, w_local),
        grid=(rows // row_tile, cols // col_tile),
        in_specs=[
            smem,
            smem,
            pl.BlockSpec((col_count, phys, 2, row_tile, wide), lambda i, j: (0, 0, 0, i, 0)),
        ]
        + [pl.BlockSpec((w_local, 2, depth, col_tile), lambda i, j: (0, 0, 0, j))] * len(envs),
        out_specs=pl.BlockSpec((mpo_count, phys, 2, row_tile, col_tile), lambda i, j: (0, 0, 0, i, j)),
        out_shape=jax.ShapeDtypeStruct((mpo_count, phys, 2, rows, cols), BF16),
        scratch_shapes=[pltpu.VMEM((2 * w_local, 2, phys * row_tile, col_tile), F32)],
        compiler_params=params(2),
        cost_estimate=LIGHT,
        name="first_product",
    )(blocks, mpo, site, *envs)


def second_kernel(pick_ref, own_ref, sib_ref, *refs):
    site_refs, out_ref = refs[:-1], refs[-1]
    phys, _, rows, cols = own_ref.shape[1:]
    total = None
    for q_ref, quarter in ((own_ref, pick_ref[0]), (sib_ref, 1 - pick_ref[0])):
        piece = pl.ds(pl.multiple_of(quarter * cols, cols), cols)
        for t in range(phys):
            right = [site_ref[t, part, :, piece] for part in range(2) for site_ref in site_refs]
            more = mul_t(q_ref[0, t].reshape(2 * rows, cols), jnp.concatenate(right, axis=0))
            total = more if total is None else total + more
    width = total.shape[1] // 2
    out_ref[0, 0] = (total[:rows, :width] - total[rows:, width:]).astype(BF16)
    out_ref[0, 1] = (total[:rows, width:] + total[rows:, :width]).astype(BF16)


def second_product(pick, own, sib, sites):
    mpo_count, phys, _, rows, cols = own.shape
    y_rows = sum(site.shape[2] for site in sites)
    q_spec = pl.BlockSpec((1, phys, 2, rows, cols), lambda v: (v, 0, 0, 0, 0))
    return pl.pallas_call(
        second_kernel,
        grid=(mpo_count,),
        in_specs=[pl.BlockSpec(memory_space=pltpu.SMEM), q_spec, q_spec]
        + [pl.BlockSpec(site.shape, lambda v: (0, 0, 0, 0)) for site in sites],
        out_specs=pl.BlockSpec((1, 2, rows, y_rows), lambda v: (v, 0, 0, 0)),
        out_shape=jax.ShapeDtypeStruct((mpo_count, 2, rows, y_rows), BF16),
        compiler_params=params(1),
        cost_estimate=LIGHT,
        name="second_product",
    )(pick, own, sib, *sites)


def finish_kernel(pick_ref, mine_ref, siblings_ref, *refs):
    out_ref = refs[-1]
    parts = [refs[at : at + 4] for at in range(0, len(refs) - 1, 4)]
    half = mine_ref.shape[3]
    halves = [pl.multiple_of(core * half, half) for core in (pick_ref[1], 1 - pick_ref[1])]

    @pl.when(pick_ref[0] == 0)
    def _():
        for ref, first in zip((mine_ref, siblings_ref), halves):
            out_ref[0, 0, :, pl.ds(first, half)] = ref[0, 0].astype(F32)

    @pl.when(pick_ref[0] != 0)
    def _():
        for side, first in enumerate(halves):
            for number, part in enumerate(parts):
                one, two = part[2 * side : 2 * side + 2]
                width = one.shape[3]
                place = pl.ds(pl.multiple_of(first + number * width, width), width)
                out_ref[0, 0, :, place] = one[0, 0].astype(F32) + two[0, 0].astype(F32)


def finish(pick, mine, siblings, parts):
    addends = [value for part in parts for value in part]
    mpo_count, _, rows, half = mine.shape

    def spec(value, used):
        def index(v, p, pick):
            wanted = (pick[0] == used).astype(jnp.int32)
            return (v * wanted, p * wanted, 0, 0)

        return pl.BlockSpec((1, 1) + value.shape[2:], index)

    return pl.pallas_call(
        finish_kernel,
        grid_spec=pltpu.PrefetchScalarGridSpec(
            num_scalar_prefetch=1,
            grid=(mpo_count, 2),
            in_specs=[spec(mine, 0), spec(siblings, 0)] + [spec(value, 1) for value in addends],
            out_specs=pl.BlockSpec((1, 1, rows, 2 * half), lambda v, p, pick: (v, p, 0, 0)),
        ),
        out_shape=jax.ShapeDtypeStruct((mpo_count, 2, rows, 2 * half), F32),
        compiler_params=params(2),
        cost_estimate=LIGHT,
        name="finish",
    )(pick, mine, siblings, *addends)


def after(value, *earlier):
    return lax.optimization_barrier((value,) + earlier)[0]


def swap(value):
    return lax.ppermute(value, "depth", [(0, 1), (1, 0)])


def split_inputs(environment, mpo):
    depth = lax.axis_index("depth")
    w_local, half = environment.shape[0], environment.shape[3]
    cols = half // 2
    env_own = lax.dynamic_slice_in_dim(environment, depth * cols, cols, 3)
    env_sib = swap(lax.dynamic_slice_in_dim(environment, (1 - depth) * cols, cols, 3))
    mpo_mine = jnp.concatenate(
        [
            lax.dynamic_slice_in_dim(mpo, depth * w_local, w_local, 0),
            lax.dynamic_slice_in_dim(mpo, (1 - depth) * w_local, w_local, 0),
        ],
        axis=0,
    )
    return env_own, env_sib, mpo_mine


def one_product(left, right, dims):
    return jnp.einsum(dims, left, right, preferred_element_type=F32)


def any_line(environment, site_tensor, mpo):
    depth = lax.axis_index("depth")
    env_own, env_sib, mpo_mine = split_inputs(environment, mpo)
    env_own = lax.all_gather(env_own, "row", axis=2, tiled=True)
    env_sib = lax.all_gather(env_sib, "row", axis=2, tiled=True)
    env = jnp.concatenate([env_own, env_sib], axis=0)
    cols = env.shape[3]
    planar = jnp.transpose(site_tensor, (0, 2, 1, 3))
    site_own = lax.dynamic_slice_in_dim(planar, depth * cols, cols, 3)
    site = lax.all_gather(planar, "col", axis=3, tiled=True)
    first = functools.partial(one_product, dims="sxa,wac->wsxc")
    g = jnp.stack(
        [
            first(site[:, 0], env[:, 0]) + first(site[:, 1], env[:, 1]),
            first(site[:, 0], env[:, 1]) - first(site[:, 1], env[:, 0]),
        ],
        axis=2,
    )
    q = jnp.einsum("wvst,wspxc->vtpxc", mpo_mine, g, precision=lax.Precision.HIGHEST).astype(BF16)
    site = lax.all_gather(site_own, "row", axis=2, tiled=True)
    second = functools.partial(one_product, dims="vtxc,tyc->vxy")
    total = jnp.stack(
        [
            second(q[:, :, 0], site[:, 0]) - second(q[:, :, 1], site[:, 1]),
            second(q[:, :, 0], site[:, 1]) + second(q[:, :, 1], site[:, 0]),
        ],
        axis=1,
    )
    return lax.psum_scatter(total, ("col", "depth"), scatter_dimension=3, tiled=True)


def ring(environment, site_tensor, mpo):
    row_count, col_count = lax.axis_size("row"), lax.axis_size("col")
    row, col, depth = (lax.axis_index(axis) for axis in ("row", "col", "depth"))
    axes = ("row", "col", "depth")
    place = lambda r, c, d: (r * col_count + c) * 2 + d
    shift = lambda value: lax.ppermute(
        value, "row", [(r, (r + 1) % row_count) for r in range(row_count)]
    )
    turn = lambda value: lax.ppermute(value, "col", [(0, 1), (1, 0)])
    in_order = lambda mine, sibling, axis: jnp.where(
        depth == 0,
        jnp.concatenate([mine, sibling], axis=axis),
        jnp.concatenate([sibling, mine], axis=axis),
    )

    env_own, env_sib, mpo_mine = split_inputs(environment, mpo)
    envs = [env_own, env_sib]
    for _ in range(row_count - 1):
        envs += [shift(envs[-2]), shift(envs[-1])]

    planar = jnp.transpose(after(site_tensor, env_sib), (0, 2, 1, 3))
    rows = planar.shape[2]
    half = rows // 2
    mine = lax.dynamic_slice_in_dim(planar, depth * half, half, 2)
    other = turn(mine)
    other = in_order(other, swap(after(other, envs[4])), 2)
    site = jnp.where(col == 0, jnp.stack([planar, other]), jnp.stack([other, planar]))

    parts = [mine[:, :, : half // 2], mine[:, :, half // 2 :]]
    travelling = [[shift(after(part, env, site)) for part, env in zip(parts, envs[-2:])]]
    for _ in range(row_count - 2):
        travelling.append([shift(part) for part in travelling[-1]])

    blocks = jnp.stack([lax.rem(row - k + row_count, row_count) for k in range(row_count)])
    blocks = blocks.astype(jnp.int32)
    q = first_product(blocks, mpo_mine, site, envs, half, half)
    q_sib = swap(after(q, *travelling[0]))

    goals = [
        [((r - step) % row_count // 2, (r - step) % row_count % 2) for r in range(row_count)]
        for step in range(row_count)
    ]
    pick = depth.astype(jnp.int32).reshape(1)

    def second(sites, *earlier):
        return second_product(after(pick, *earlier), q, q_sib, sites)

    def turn_to_goal(value, goal):
        return lax.ppermute(
            value,
            axes,
            [(place(r, 1 - c, d), place(r, c, d)) for r, (c, _) in enumerate(goal) for d in range(2)],
        )

    def send(value, goal, turned, crossed):
        return lax.ppermute(
            value,
            axes,
            [
                (place(r, 1 - c if turned else c, 1 - d if crossed else d), place(r, c, d))
                for r, (c, d) in enumerate(goal)
            ],
        )

    step_of = lambda d: lax.rem(row - col * 2 - d + row_count, row_count)
    lows = [second(parts)]
    turned = [turn_to_goal(lows[0], goals[0])]
    lows.append(second(travelling[0], lows[0], travelling[1][0]))
    turned.append(turn_to_goal(lows[1], goals[1]))
    lows.append(second(travelling[1], lows[1], turned[0]))
    turned.append(turn_to_goal(lows[2], goals[2]))
    totals = [low.astype(F32) + came.astype(F32) for low, came in zip(lows, turned)]

    def total_at(step):
        return jnp.where(step == 0, totals[0], jnp.where(step == 1, totals[1], totals[2]))

    def last_part(number, *earlier):
        low = second([travelling[2][number]], *earlier)
        ways = ((True, False), (True, True), (False, True))
        return [low] + [send(low, goals[3], *way) for way in ways]

    last = [last_part(0, lows[2])]
    mine, siblings = total_at(step_of(depth)), total_at(step_of(1 - depth)).astype(BF16)
    last.append(last_part(1, *last[0], mine, siblings))
    siblings = swap(siblings)
    came_last = (step_of(depth) == row_count - 1).astype(jnp.int32)
    return finish(jnp.stack([came_last, depth.astype(jnp.int32)]), mine, siblings, last)


def solution(mesh):
    placed = (
        P(("groups", "depth"), None, "row", "col"),
        P("groups", "row", None, "col"),
        P("groups", None, None, None),
    )
    fits = mesh.shape["col"] == 2 and mesh.shape["row"] == 2 * mesh.shape["col"]
    return jax.shard_map(
        ring if fits else any_line,
        mesh=mesh,
        in_specs=placed,
        out_specs=P("groups", None, "row", ("col", "depth")),
        check_vma=False,
    )
```

```python
import functools
import jax
import jax.numpy as jnp
from jax import lax
from jax.experimental import pallas as pl
from jax.experimental.pallas import tpu as pltpu
from jax.sharding import PartitionSpec as P

F32 = jnp.float32
BF16 = jnp.bfloat16
VMEM_BYTES = 64 * 1024 * 1024
LIGHT = pl.CostEstimate(flops=0, bytes_accessed=0, transcendentals=0)


def params(steps):
    return pltpu.CompilerParams(
        dimension_semantics=("arbitrary",) * steps, vmem_limit_bytes=VMEM_BYTES
    )


def mul(left, right):
    return jnp.dot(left, right, preferred_element_type=F32)


def mul_t(left, right):
    return lax.dot_general(left, right, (((1,), (1,)), ((), ())), preferred_element_type=F32)


def first_kernel(w_local, block_ref, mpo_ref, site_ref, *refs):
    q_ref, g_ref = refs[-2:]
    env_refs = refs[:-2]
    mpo_count, phys, _, rows, _ = q_ref.shape
    depth = env_refs[0].shape[2]
    per_col = site_ref.shape[-1] // depth
    for which in range(2):
        for w in range(w_local):
            with_real, with_imag = None, None
            for number in range(len(env_refs) // 2):
                block = block_ref[number]
                piece = pl.ds(pl.multiple_of((block % per_col) * depth, depth), depth)
                left = site_ref[block // per_col, :, :, :, piece].reshape(phys * 2 * rows, depth)
                env_ref = env_refs[number * 2 + which]
                more_real, more_imag = mul(left, env_ref[w, 0]), mul(left, env_ref[w, 1])
                with_real = more_real if with_real is None else with_real + more_real
                with_imag = more_imag if with_imag is None else with_imag + more_imag
            for s in range(phys):
                real, imag = (slice((2 * s + part) * rows, (2 * s + part + 1) * rows) for part in range(2))
                there = slice(s * rows, (s + 1) * rows)
                g_ref[which * w_local + w, 0, there] = with_real[real] + with_imag[imag]
                g_ref[which * w_local + w, 1, there] = with_imag[real] - with_real[imag]
    for part in range(2):
        for v in range(mpo_count):
            for t in range(phys):
                total = None
                for w in range(2 * w_local):
                    for s in range(phys):
                        term = mpo_ref[w, v, s, t] * g_ref[w, part, s * rows : (s + 1) * rows]
                        total = term if total is None else total + term
                q_ref[v, t, part] = total.astype(BF16)


def first_product(blocks, mpo, site, envs, row_tile, col_tile):
    col_count, phys, _, rows, wide = site.shape
    w_local, _, depth, cols = envs[0].shape
    mpo_count = mpo.shape[1]
    smem = pl.BlockSpec(memory_space=pltpu.SMEM)
    return pl.pallas_call(
        functools.partial(first_kernel, w_local),
        grid=(rows // row_tile, cols // col_tile),
        in_specs=[
            smem,
            smem,
            pl.BlockSpec((col_count, phys, 2, row_tile, wide), lambda i, j: (0, 0, 0, i, 0)),
        ]
        + [pl.BlockSpec((w_local, 2, depth, col_tile), lambda i, j: (0, 0, 0, j))] * len(envs),
        out_specs=pl.BlockSpec((mpo_count, phys, 2, row_tile, col_tile), lambda i, j: (0, 0, 0, i, j)),
        out_shape=jax.ShapeDtypeStruct((mpo_count, phys, 2, rows, cols), BF16),
        scratch_shapes=[pltpu.VMEM((2 * w_local, 2, phys * row_tile, col_tile), F32)],
        compiler_params=params(2),
        cost_estimate=LIGHT,
        name="first_product",
    )(blocks, mpo, site, *envs)


def second_kernel(pick_ref, own_ref, sib_ref, *refs):
    site_refs, out_ref = refs[:-1], refs[-1]
    phys, _, rows, cols = own_ref.shape[1:]
    total = None
    for q_ref, quarter in ((own_ref, pick_ref[0]), (sib_ref, 1 - pick_ref[0])):
        piece = pl.ds(pl.multiple_of(quarter * cols, cols), cols)
        for t in range(phys):
            right = [site_ref[t, part, :, piece] for part in range(2) for site_ref in site_refs]
            more = mul_t(q_ref[0, t].reshape(2 * rows, cols), jnp.concatenate(right, axis=0))
            total = more if total is None else total + more
    width = total.shape[1] // 2
    out_ref[0, 0] = (total[:rows, :width] - total[rows:, width:]).astype(BF16)
    out_ref[0, 1] = (total[:rows, width:] + total[rows:, :width]).astype(BF16)


def second_product(pick, own, sib, sites):
    mpo_count, phys, _, rows, cols = own.shape
    y_rows = sum(site.shape[2] for site in sites)
    q_spec = pl.BlockSpec((1, phys, 2, rows, cols), lambda v: (v, 0, 0, 0, 0))
    return pl.pallas_call(
        second_kernel,
        grid=(mpo_count,),
        in_specs=[pl.BlockSpec(memory_space=pltpu.SMEM), q_spec, q_spec]
        + [pl.BlockSpec(site.shape, lambda v: (0, 0, 0, 0)) for site in sites],
        out_specs=pl.BlockSpec((1, 2, rows, y_rows), lambda v: (v, 0, 0, 0)),
        out_shape=jax.ShapeDtypeStruct((mpo_count, 2, rows, y_rows), BF16),
        compiler_params=params(1),
        cost_estimate=LIGHT,
        name="second_product",
    )(pick, own, sib, *sites)


def finish_kernel(pick_ref, mine_ref, siblings_ref, *refs):
    out_ref = refs[-1]
    half = mine_ref.shape[3]
    halves = [pl.multiple_of(core * half, half) for core in (pick_ref[1], 1 - pick_ref[1])]

    @pl.when(pick_ref[0] == 0)
    def _():
        for ref, first in zip((mine_ref, siblings_ref), halves):
            out_ref[0, 0, :, pl.ds(first, half)] = ref[0, 0].astype(F32)

    @pl.when(pick_ref[0] != 0)
    def _():
        for side, first in enumerate(halves):
            one, two = refs[2 * side : 2 * side + 2]
            place = pl.ds(first, one.shape[3])
            out_ref[0, 0, :, place] = one[0, 0].astype(F32) + two[0, 0].astype(F32)


def finish(pick, mine, siblings, part):
    mpo_count, _, rows, half = mine.shape

    def spec(value, used):
        def index(v, p, pick):
            wanted = (pick[0] == used).astype(jnp.int32)
            return (v * wanted, p * wanted, 0, 0)

        return pl.BlockSpec((1, 1) + value.shape[2:], index)

    return pl.pallas_call(
        finish_kernel,
        grid_spec=pltpu.PrefetchScalarGridSpec(
            num_scalar_prefetch=1,
            grid=(mpo_count, 2),
            in_specs=[spec(mine, 0), spec(siblings, 0)] + [spec(value, 1) for value in part],
            out_specs=pl.BlockSpec((1, 1, rows, 2 * half), lambda v, p, pick: (v, p, 0, 0)),
        ),
        out_shape=jax.ShapeDtypeStruct((mpo_count, 2, rows, 2 * half), F32),
        compiler_params=params(2),
        cost_estimate=LIGHT,
        name="finish",
    )(pick, mine, siblings, *part)


def finish_last_kernel(pick_ref, *refs):
    part, (_, out_ref, sum_ref, sems) = refs[:4], refs[4:]
    mpo_count, _, _, width = part[0].shape
    half = out_ref.shape[3] // 2

    @pl.when(pick_ref[0] != 0)
    def _():
        copies = []
        for v in range(mpo_count):
            for p in range(2):
                for side, core in enumerate((pick_ref[1], 1 - pick_ref[1])):
                    one, two = part[2 * side : 2 * side + 2]
                    sum_ref[side, v, p] = one[v, p].astype(F32) + two[v, p].astype(F32)
                    place = pl.ds(pl.multiple_of(core * half + half - width, width), width)
                    copies.append(
                        pltpu.make_async_copy(
                            sum_ref.at[side, v, p], out_ref.at[v, p, :, place], sems.at[side, v, p]
                        )
                    )
                    copies[-1].start()
        for copy in copies:
            copy.wait()


def finish_last(pick, out, part):
    mpo_count, _, rows, width = part[0].shape
    anywhere = pl.BlockSpec(memory_space=pl.ANY)
    return pl.pallas_call(
        finish_last_kernel,
        in_specs=[pl.BlockSpec(memory_space=pltpu.SMEM)]
        + [pl.BlockSpec(memory_space=pltpu.VMEM)] * 4
        + [anywhere],
        out_specs=anywhere,
        out_shape=jax.ShapeDtypeStruct(out.shape, F32),
        input_output_aliases={5: 0},
        scratch_shapes=[
            pltpu.VMEM((2, mpo_count, 2, rows, width), F32),
            pltpu.SemaphoreType.DMA((2, mpo_count, 2)),
        ],
        compiler_params=pltpu.CompilerParams(vmem_limit_bytes=VMEM_BYTES),
        cost_estimate=LIGHT,
        name="finish_last",
    )(pick, *part, out)


def after(value, *earlier):
    return lax.optimization_barrier((value,) + earlier)[0]


def swap(value):
    return lax.ppermute(value, "depth", [(0, 1), (1, 0)])


def split_inputs(environment, mpo):
    depth = lax.axis_index("depth")
    w_local, half = environment.shape[0], environment.shape[3]
    cols = half // 2
    env_own = lax.dynamic_slice_in_dim(environment, depth * cols, cols, 3)
    env_sib = swap(lax.dynamic_slice_in_dim(environment, (1 - depth) * cols, cols, 3))
    mpo_mine = jnp.concatenate(
        [
            lax.dynamic_slice_in_dim(mpo, depth * w_local, w_local, 0),
            lax.dynamic_slice_in_dim(mpo, (1 - depth) * w_local, w_local, 0),
        ],
        axis=0,
    )
    return env_own, env_sib, mpo_mine


def one_product(left, right, dims):
    return jnp.einsum(dims, left, right, preferred_element_type=F32)


def any_line(environment, site_tensor, mpo):
    depth = lax.axis_index("depth")
    env_own, env_sib, mpo_mine = split_inputs(environment, mpo)
    env_own = lax.all_gather(env_own, "row", axis=2, tiled=True)
    env_sib = lax.all_gather(env_sib, "row", axis=2, tiled=True)
    env = jnp.concatenate([env_own, env_sib], axis=0)
    cols = env.shape[3]
    planar = jnp.transpose(site_tensor, (0, 2, 1, 3))
    site_own = lax.dynamic_slice_in_dim(planar, depth * cols, cols, 3)
    site = lax.all_gather(planar, "col", axis=3, tiled=True)
    first = functools.partial(one_product, dims="sxa,wac->wsxc")
    g = jnp.stack(
        [
            first(site[:, 0], env[:, 0]) + first(site[:, 1], env[:, 1]),
            first(site[:, 0], env[:, 1]) - first(site[:, 1], env[:, 0]),
        ],
        axis=2,
    )
    q = jnp.einsum("wvst,wspxc->vtpxc", mpo_mine, g, precision=lax.Precision.HIGHEST).astype(BF16)
    site = lax.all_gather(site_own, "row", axis=2, tiled=True)
    second = functools.partial(one_product, dims="vtxc,tyc->vxy")
    total = jnp.stack(
        [
            second(q[:, :, 0], site[:, 0]) - second(q[:, :, 1], site[:, 1]),
            second(q[:, :, 0], site[:, 1]) + second(q[:, :, 1], site[:, 0]),
        ],
        axis=1,
    )
    return lax.psum_scatter(total, ("col", "depth"), scatter_dimension=3, tiled=True)


def ring(environment, site_tensor, mpo):
    row_count, col_count = lax.axis_size("row"), lax.axis_size("col")
    row, col, depth = (lax.axis_index(axis) for axis in ("row", "col", "depth"))
    axes = ("row", "col", "depth")
    place = lambda r, c, d: (r * col_count + c) * 2 + d
    shift = lambda value: lax.ppermute(
        value, "row", [(r, (r + 1) % row_count) for r in range(row_count)]
    )
    turn = lambda value: lax.ppermute(value, "col", [(0, 1), (1, 0)])
    in_order = lambda mine, sibling, axis: jnp.where(
        depth == 0,
        jnp.concatenate([mine, sibling], axis=axis),
        jnp.concatenate([sibling, mine], axis=axis),
    )

    env_own, env_sib, mpo_mine = split_inputs(environment, mpo)
    envs = [env_own, env_sib]
    for _ in range(row_count - 1):
        envs += [shift(envs[-2]), shift(envs[-1])]

    planar = jnp.transpose(after(site_tensor, env_sib), (0, 2, 1, 3))
    rows = planar.shape[2]
    half = rows // 2
    mine = lax.dynamic_slice_in_dim(planar, depth * half, half, 2)
    other = turn(mine)
    other = in_order(other, swap(after(other, envs[4])), 2)
    site = jnp.where(col == 0, jnp.stack([planar, other]), jnp.stack([other, planar]))

    parts = [mine[:, :, : half // 2], mine[:, :, half // 2 :]]
    travelling = [[shift(after(part, env, site)) for part, env in zip(parts, envs[-2:])]]
    for _ in range(row_count - 2):
        travelling.append([shift(part) for part in travelling[-1]])

    blocks = jnp.stack([lax.rem(row - k + row_count, row_count) for k in range(row_count)])
    blocks = blocks.astype(jnp.int32)
    q = first_product(blocks, mpo_mine, site, envs, half, half)
    q_sib = swap(after(q, *travelling[0]))

    goals = [
        [((r - step) % row_count // 2, (r - step) % row_count % 2) for r in range(row_count)]
        for step in range(row_count)
    ]
    pick = depth.astype(jnp.int32).reshape(1)

    def second(sites, *earlier):
        return second_product(after(pick, *earlier), q, q_sib, sites)

    def turn_to_goal(value, goal):
        return lax.ppermute(
            value,
            axes,
            [(place(r, 1 - c, d), place(r, c, d)) for r, (c, _) in enumerate(goal) for d in range(2)],
        )

    def send(value, goal, turned, crossed):
        return lax.ppermute(
            value,
            axes,
            [
                (place(r, 1 - c if turned else c, 1 - d if crossed else d), place(r, c, d))
                for r, (c, d) in enumerate(goal)
            ],
        )

    step_of = lambda d: lax.rem(row - col * 2 - d + row_count, row_count)
    lows = [second(parts)]
    turned = [turn_to_goal(lows[0], goals[0])]
    lows.append(second(travelling[0], lows[0], travelling[1][0]))
    turned.append(turn_to_goal(lows[1], goals[1]))
    lows.append(second(travelling[1], lows[1], turned[0]))
    turned.append(turn_to_goal(lows[2], goals[2]))
    totals = [low.astype(F32) + came.astype(F32) for low, came in zip(lows, turned)]

    def total_at(step):
        return jnp.where(step == 0, totals[0], jnp.where(step == 1, totals[1], totals[2]))

    def last_part(number, *earlier):
        low = second([travelling[2][number]], *earlier)
        ways = ((True, False), (True, True), (False, True))
        return [low] + [send(low, goals[3], *way) for way in ways]

    last = [last_part(0, lows[2])]
    mine, siblings = total_at(step_of(depth)), total_at(step_of(1 - depth)).astype(BF16)
    last.append(last_part(1, *last[0], mine, siblings))
    siblings = swap(siblings)
    came_last = (step_of(depth) == row_count - 1).astype(jnp.int32)
    pick = jnp.stack([came_last, depth.astype(jnp.int32)])
    out = finish(after(pick, last[1][0]), mine, siblings, last[0])
    return finish_last(pick, out, last[1])


def solution(mesh):
    placed = (
        P(("groups", "depth"), None, "row", "col"),
        P("groups", "row", None, "col"),
        P("groups", None, None, None),
    )
    fits = mesh.shape["col"] == 2 and mesh.shape["row"] == 2 * mesh.shape["col"]
    return jax.shard_map(
        ring if fits else any_line,
        mesh=mesh,
        in_specs=placed,
        out_specs=P("groups", None, "row", ("col", "depth")),
        check_vma=False,
    )
```

```python
import functools
import jax
import jax.numpy as jnp
from jax import lax
from jax.experimental import pallas as pl
from jax.experimental.pallas import tpu as pltpu
from jax.sharding import PartitionSpec as P

F32 = jnp.float32
BF16 = jnp.bfloat16
VMEM_BYTES = 40 * 1024 * 1024
LIGHT = pl.CostEstimate(flops=0, bytes_accessed=0, transcendentals=0)


def params(steps):
    return pltpu.CompilerParams(
        dimension_semantics=("arbitrary",) * steps, vmem_limit_bytes=VMEM_BYTES
    )


def mul(left, right):
    return jnp.dot(left, right, preferred_element_type=F32)


def mul_t(left, right):
    return lax.dot_general(left, right, (((1,), (1,)), ((), ())), preferred_element_type=F32)


def first_kernel(w_local, block_ref, mpo_ref, site_ref, *refs):
    q_ref, g_ref = refs[-2:]
    env_refs = refs[:-2]
    mpo_count, phys, _, rows, _ = q_ref.shape
    depth = env_refs[0].shape[2]
    per_col = site_ref.shape[-1] // depth
    for which in range(2):
        for w in range(w_local):
            with_real, with_imag = None, None
            for number in range(len(env_refs) // 2):
                block = block_ref[number]
                piece = pl.ds(pl.multiple_of((block % per_col) * depth, depth), depth)
                left = site_ref[block // per_col, :, :, :, piece].reshape(phys * 2 * rows, depth)
                env_ref = env_refs[number * 2 + which]
                more_real, more_imag = mul(left, env_ref[w, 0]), mul(left, env_ref[w, 1])
                with_real = more_real if with_real is None else with_real + more_real
                with_imag = more_imag if with_imag is None else with_imag + more_imag
            for s in range(phys):
                real, imag = (slice((2 * s + part) * rows, (2 * s + part + 1) * rows) for part in range(2))
                there = slice(s * rows, (s + 1) * rows)
                g_ref[which * w_local + w, 0, there] = with_real[real] + with_imag[imag]
                g_ref[which * w_local + w, 1, there] = with_imag[real] - with_real[imag]
    for part in range(2):
        for v in range(mpo_count):
            for t in range(phys):
                total = None
                for w in range(2 * w_local):
                    for s in range(phys):
                        term = mpo_ref[w, v, s, t] * g_ref[w, part, s * rows : (s + 1) * rows]
                        total = term if total is None else total + term
                q_ref[v, t, part] = total.astype(BF16)


def first_product(blocks, mpo, site, envs, row_tile, col_tile):
    col_count, phys, _, rows, wide = site.shape
    w_local, _, depth, cols = envs[0].shape
    mpo_count = mpo.shape[1]
    smem = pl.BlockSpec(memory_space=pltpu.SMEM)
    return pl.pallas_call(
        functools.partial(first_kernel, w_local),
        grid=(rows // row_tile, cols // col_tile),
        in_specs=[
            smem,
            smem,
            pl.BlockSpec((col_count, phys, 2, row_tile, wide), lambda i, j: (0, 0, 0, i, 0)),
        ]
        + [pl.BlockSpec((w_local, 2, depth, col_tile), lambda i, j: (0, 0, 0, j))] * len(envs),
        out_specs=pl.BlockSpec((mpo_count, phys, 2, row_tile, col_tile), lambda i, j: (0, 0, 0, i, j)),
        out_shape=jax.ShapeDtypeStruct((mpo_count, phys, 2, rows, cols), BF16),
        scratch_shapes=[pltpu.VMEM((2 * w_local, 2, phys * row_tile, col_tile), F32)],
        compiler_params=params(2),
        cost_estimate=LIGHT,
        name="first_product",
    )(blocks, mpo, site, *envs)


def second_kernel(pick_ref, own_ref, sib_ref, *refs):
    site_refs, out_ref = refs[:-1], refs[-1]
    phys, _, rows, cols = own_ref.shape[1:]
    total = None
    for q_ref, quarter in ((own_ref, pick_ref[0]), (sib_ref, 1 - pick_ref[0])):
        piece = pl.ds(pl.multiple_of(quarter * cols, cols), cols)
        for t in range(phys):
            right = [site_ref[t, part, :, piece] for part in range(2) for site_ref in site_refs]
            more = mul_t(q_ref[0, t].reshape(2 * rows, cols), jnp.concatenate(right, axis=0))
            total = more if total is None else total + more
    width = total.shape[1] // 2
    out_ref[0, 0] = (total[:rows, :width] - total[rows:, width:]).astype(BF16)
    out_ref[0, 1] = (total[:rows, width:] + total[rows:, :width]).astype(BF16)


def second_product(pick, own, sib, sites):
    mpo_count, phys, _, rows, cols = own.shape
    y_rows = sum(site.shape[2] for site in sites)
    q_spec = pl.BlockSpec((1, phys, 2, rows, cols), lambda v: (v, 0, 0, 0, 0))
    return pl.pallas_call(
        second_kernel,
        grid=(mpo_count,),
        in_specs=[pl.BlockSpec(memory_space=pltpu.SMEM), q_spec, q_spec]
        + [pl.BlockSpec(site.shape, lambda v: (0, 0, 0, 0)) for site in sites],
        out_specs=pl.BlockSpec((1, 2, rows, y_rows), lambda v: (v, 0, 0, 0)),
        out_shape=jax.ShapeDtypeStruct((mpo_count, 2, rows, y_rows), BF16),
        compiler_params=params(1),
        cost_estimate=LIGHT,
        name="second_product",
    )(pick, own, sib, *sites)


def finish_kernel(pick_ref, mine_ref, siblings_ref, *refs):
    out_ref = refs[-1]
    half = mine_ref.shape[3]
    halves = [pl.multiple_of(core * half, half) for core in (pick_ref[1], 1 - pick_ref[1])]

    @pl.when(pick_ref[0] == 0)
    def _():
        for ref, first in zip((mine_ref, siblings_ref), halves):
            out_ref[0, 0, :, pl.ds(first, half)] = ref[0, 0].astype(F32)

    @pl.when(pick_ref[0] != 0)
    def _():
        for side, first in enumerate(halves):
            one, two = refs[2 * side : 2 * side + 2]
            place = pl.ds(first, one.shape[3])
            out_ref[0, 0, :, place] = one[0, 0].astype(F32) + two[0, 0].astype(F32)


def finish(pick, mine, siblings, part):
    mpo_count, _, rows, half = mine.shape

    def spec(value, used):
        def index(v, p, pick):
            wanted = (pick[0] == used).astype(jnp.int32)
            return (v * wanted, p * wanted, 0, 0)

        return pl.BlockSpec((1, 1) + value.shape[2:], index)

    return pl.pallas_call(
        finish_kernel,
        grid_spec=pltpu.PrefetchScalarGridSpec(
            num_scalar_prefetch=1,
            grid=(mpo_count, 2),
            in_specs=[spec(mine, 0), spec(siblings, 0)] + [spec(value, 1) for value in part],
            out_specs=pl.BlockSpec((1, 1, rows, 2 * half), lambda v, p, pick: (v, p, 0, 0)),
        ),
        out_shape=jax.ShapeDtypeStruct((mpo_count, 2, rows, 2 * half), F32),
        compiler_params=params(2),
        cost_estimate=LIGHT,
        name="finish",
    )(pick, mine, siblings, *part)


def finish_last_kernel(pick_ref, *refs):
    part, (_, out_ref, sum_ref, sems) = refs[:4], refs[4:]
    mpo_count, _, _, width = part[0].shape
    half = out_ref.shape[3] // 2

    @pl.when(pick_ref[0] != 0)
    def _():
        copies = []
        for v in range(mpo_count):
            for p in range(2):
                for side, core in enumerate((pick_ref[1], 1 - pick_ref[1])):
                    one, two = part[2 * side : 2 * side + 2]
                    sum_ref[side, v, p] = one[v, p].astype(F32) + two[v, p].astype(F32)
                    place = pl.ds(pl.multiple_of(core * half + half - width, width), width)
                    copies.append(
                        pltpu.make_async_copy(
                            sum_ref.at[side, v, p], out_ref.at[v, p, :, place], sems.at[side, v, p]
                        )
                    )
                    copies[-1].start()
        for copy in copies:
            copy.wait()


def finish_last(pick, out, part):
    mpo_count, _, rows, width = part[0].shape
    anywhere = pl.BlockSpec(memory_space=pl.ANY)
    return pl.pallas_call(
        finish_last_kernel,
        in_specs=[pl.BlockSpec(memory_space=pltpu.SMEM)]
        + [pl.BlockSpec(memory_space=pltpu.VMEM)] * 4
        + [anywhere],
        out_specs=anywhere,
        out_shape=jax.ShapeDtypeStruct(out.shape, F32),
        input_output_aliases={5: 0},
        scratch_shapes=[
            pltpu.VMEM((2, mpo_count, 2, rows, width), F32),
            pltpu.SemaphoreType.DMA((2, mpo_count, 2)),
        ],
        compiler_params=pltpu.CompilerParams(vmem_limit_bytes=VMEM_BYTES),
        cost_estimate=LIGHT,
        name="finish_last",
    )(pick, *part, out)


def after(value, *earlier):
    return lax.optimization_barrier((value,) + earlier)[0]


def swap(value):
    return lax.ppermute(value, "depth", [(0, 1), (1, 0)])


def split_inputs(environment, mpo):
    depth = lax.axis_index("depth")
    w_local, half = environment.shape[0], environment.shape[3]
    cols = half // 2
    env_own = lax.dynamic_slice_in_dim(environment, depth * cols, cols, 3)
    env_sib = swap(lax.dynamic_slice_in_dim(environment, (1 - depth) * cols, cols, 3))
    mpo_mine = jnp.concatenate(
        [
            lax.dynamic_slice_in_dim(mpo, depth * w_local, w_local, 0),
            lax.dynamic_slice_in_dim(mpo, (1 - depth) * w_local, w_local, 0),
        ],
        axis=0,
    )
    return env_own, env_sib, mpo_mine


def one_product(left, right, dims):
    return jnp.einsum(dims, left, right, preferred_element_type=F32)


def any_line(environment, site_tensor, mpo):
    depth = lax.axis_index("depth")
    env_own, env_sib, mpo_mine = split_inputs(environment, mpo)
    env_own = lax.all_gather(env_own, "row", axis=2, tiled=True)
    env_sib = lax.all_gather(env_sib, "row", axis=2, tiled=True)
    env = jnp.concatenate([env_own, env_sib], axis=0)
    cols = env.shape[3]
    planar = jnp.transpose(site_tensor, (0, 2, 1, 3))
    site_own = lax.dynamic_slice_in_dim(planar, depth * cols, cols, 3)
    site = lax.all_gather(planar, "col", axis=3, tiled=True)
    first = functools.partial(one_product, dims="sxa,wac->wsxc")
    g = jnp.stack(
        [
            first(site[:, 0], env[:, 0]) + first(site[:, 1], env[:, 1]),
            first(site[:, 0], env[:, 1]) - first(site[:, 1], env[:, 0]),
        ],
        axis=2,
    )
    q = jnp.einsum("wvst,wspxc->vtpxc", mpo_mine, g, precision=lax.Precision.HIGHEST).astype(BF16)
    site = lax.all_gather(site_own, "row", axis=2, tiled=True)
    second = functools.partial(one_product, dims="vtxc,tyc->vxy")
    total = jnp.stack(
        [
            second(q[:, :, 0], site[:, 0]) - second(q[:, :, 1], site[:, 1]),
            second(q[:, :, 0], site[:, 1]) + second(q[:, :, 1], site[:, 0]),
        ],
        axis=1,
    )
    return lax.psum_scatter(total, ("col", "depth"), scatter_dimension=3, tiled=True)


def ring(environment, site_tensor, mpo):
    row_count, col_count = lax.axis_size("row"), lax.axis_size("col")
    row, col, depth = (lax.axis_index(axis) for axis in ("row", "col", "depth"))
    axes = ("row", "col", "depth")
    place = lambda r, c, d: (r * col_count + c) * 2 + d
    shift = lambda value: lax.ppermute(
        value, "row", [(r, (r + 1) % row_count) for r in range(row_count)]
    )
    turn = lambda value: lax.ppermute(value, "col", [(0, 1), (1, 0)])
    in_order = lambda mine, sibling, axis: jnp.where(
        depth == 0,
        jnp.concatenate([mine, sibling], axis=axis),
        jnp.concatenate([sibling, mine], axis=axis),
    )

    env_own, env_sib, mpo_mine = split_inputs(environment, mpo)
    envs = [env_own, env_sib]
    for _ in range(row_count - 1):
        envs += [shift(envs[-2]), shift(envs[-1])]

    planar = jnp.transpose(after(site_tensor, env_sib), (0, 2, 1, 3))
    rows = planar.shape[2]
    half = rows // 2
    mine = lax.dynamic_slice_in_dim(planar, depth * half, half, 2)
    other = turn(mine)
    other = in_order(other, swap(after(other, envs[3], envs[4])), 2)
    site = jnp.where(col == 0, jnp.stack([planar, other]), jnp.stack([other, planar]))

    parts = [mine[:, :, : half // 2], mine[:, :, half // 2 :]]
    travelling = [[shift(after(part, env, site)) for part, env in zip(parts, envs[-2:])]]
    for _ in range(row_count - 2):
        travelling.append([shift(part) for part in travelling[-1]])

    blocks = jnp.stack([lax.rem(row - k + row_count, row_count) for k in range(row_count)])
    blocks = blocks.astype(jnp.int32)
    q = first_product(blocks, mpo_mine, site, envs, half, half)
    q_sib = swap(after(q, *travelling[0]))

    goals = [
        [((r - step) % row_count // 2, (r - step) % row_count % 2) for r in range(row_count)]
        for step in range(row_count)
    ]
    pick = depth.astype(jnp.int32).reshape(1)

    def second(sites, *earlier):
        return second_product(after(pick, *earlier), q, q_sib, sites)

    def turn_to_goal(value, goal):
        return lax.ppermute(
            value,
            axes,
            [(place(r, 1 - c, d), place(r, c, d)) for r, (c, _) in enumerate(goal) for d in range(2)],
        )

    def send(value, goal, turned, crossed):
        return lax.ppermute(
            value,
            axes,
            [
                (place(r, 1 - c if turned else c, 1 - d if crossed else d), place(r, c, d))
                for r, (c, d) in enumerate(goal)
            ],
        )

    step_of = lambda d: lax.rem(row - col * 2 - d + row_count, row_count)
    lows = [second(parts)]
    turned = [turn_to_goal(lows[0], goals[0])]
    lows.append(second(travelling[0], lows[0], travelling[1][0]))
    turned.append(turn_to_goal(lows[1], goals[1]))
    lows.append(second(travelling[1], lows[1], turned[0]))
    turned.append(turn_to_goal(lows[2], goals[2]))
    totals = [low.astype(F32) + came.astype(F32) for low, came in zip(lows, turned)]

    def total_at(step):
        return jnp.where(step == 0, totals[0], jnp.where(step == 1, totals[1], totals[2]))

    def last_part(number, *earlier):
        low = second([travelling[2][number]], *earlier)
        ways = ((True, False), (True, True), (False, True))
        return [low] + [send(low, goals[3], *way) for way in ways]

    last = [last_part(0, lows[2])]
    mine, siblings = total_at(step_of(depth)), total_at(step_of(1 - depth)).astype(BF16)
    last.append(last_part(1, *last[0], mine, siblings))
    siblings = swap(siblings)
    came_last = (step_of(depth) == row_count - 1).astype(jnp.int32)
    pick = jnp.stack([came_last, depth.astype(jnp.int32)])
    out = finish(after(pick, last[1][0]), mine, siblings, last[0])
    return finish_last(pick, out, last[1])


def solution(mesh):
    placed = (
        P(("groups", "depth"), None, "row", "col"),
        P("groups", "row", None, "col"),
        P("groups", None, None, None),
    )
    fits = mesh.shape["col"] == 2 and mesh.shape["row"] == 2 * mesh.shape["col"]
    return jax.shard_map(
        ring if fits else any_line,
        mesh=mesh,
        in_specs=placed,
        out_specs=P("groups", None, "row", ("col", "depth")),
        check_vma=False,
    )
```

```python
import functools
import jax
import jax.numpy as jnp
from jax import lax
from jax.experimental import pallas as pl
from jax.experimental.pallas import tpu as pltpu
from jax.sharding import PartitionSpec as P

F32 = jnp.float32
BF16 = jnp.bfloat16
VMEM_BYTES = 26 * 1024 * 1024
LIGHT = pl.CostEstimate(flops=0, bytes_accessed=0, transcendentals=0)


def params(steps):
    return pltpu.CompilerParams(
        dimension_semantics=("arbitrary",) * steps, vmem_limit_bytes=VMEM_BYTES
    )


def mul(left, right):
    return jnp.dot(left, right, preferred_element_type=F32)


def mul_t(left, right):
    return lax.dot_general(left, right, (((1,), (1,)), ((), ())), preferred_element_type=F32)


def first_kernel(w_local, block_ref, mpo_ref, site_ref, *refs):
    q_ref, g_ref = refs[-2:]
    env_refs = refs[:-2]
    mpo_count, phys, _, rows, _ = q_ref.shape
    depth = env_refs[0].shape[2]
    per_col = site_ref.shape[-1] // depth
    for which in range(2):
        for w in range(w_local):
            with_real, with_imag = None, None
            for number in range(len(env_refs) // 2):
                block = block_ref[number]
                piece = pl.ds(pl.multiple_of((block % per_col) * depth, depth), depth)
                left = site_ref[block // per_col, :, :, :, piece].reshape(phys * 2 * rows, depth)
                env_ref = env_refs[number * 2 + which]
                more_real, more_imag = mul(left, env_ref[w, 0]), mul(left, env_ref[w, 1])
                with_real = more_real if with_real is None else with_real + more_real
                with_imag = more_imag if with_imag is None else with_imag + more_imag
            for s in range(phys):
                real, imag = (slice((2 * s + part) * rows, (2 * s + part + 1) * rows) for part in range(2))
                there = slice(s * rows, (s + 1) * rows)
                g_ref[which * w_local + w, 0, there] = with_real[real] + with_imag[imag]
                g_ref[which * w_local + w, 1, there] = with_imag[real] - with_real[imag]
    for part in range(2):
        for v in range(mpo_count):
            for t in range(phys):
                total = None
                for w in range(2 * w_local):
                    for s in range(phys):
                        term = mpo_ref[w, v, s, t] * g_ref[w, part, s * rows : (s + 1) * rows]
                        total = term if total is None else total + term
                q_ref[v, t, part] = total.astype(BF16)


def first_product(blocks, mpo, site, envs, row_tile, col_tile):
    col_count, phys, _, rows, wide = site.shape
    w_local, _, depth, cols = envs[0].shape
    mpo_count = mpo.shape[1]
    smem = pl.BlockSpec(memory_space=pltpu.SMEM)
    return pl.pallas_call(
        functools.partial(first_kernel, w_local),
        grid=(rows // row_tile, cols // col_tile),
        in_specs=[
            smem,
            smem,
            pl.BlockSpec((col_count, phys, 2, row_tile, wide), lambda i, j: (0, 0, 0, i, 0)),
        ]
        + [pl.BlockSpec((w_local, 2, depth, col_tile), lambda i, j: (0, 0, 0, j))] * len(envs),
        out_specs=pl.BlockSpec((mpo_count, phys, 2, row_tile, col_tile), lambda i, j: (0, 0, 0, i, j)),
        out_shape=jax.ShapeDtypeStruct((mpo_count, phys, 2, rows, cols), BF16),
        scratch_shapes=[pltpu.VMEM((2 * w_local, 2, phys * row_tile, col_tile), F32)],
        compiler_params=params(2),
        cost_estimate=LIGHT,
        name="first_product",
    )(blocks, mpo, site, *envs)


def second_kernel(pick_ref, own_ref, sib_ref, *refs):
    site_refs, out_ref = refs[:-1], refs[-1]
    phys, _, rows, cols = own_ref.shape[1:]
    total = None
    for q_ref, quarter in ((own_ref, pick_ref[0]), (sib_ref, 1 - pick_ref[0])):
        piece = pl.ds(pl.multiple_of(quarter * cols, cols), cols)
        for t in range(phys):
            right = [site_ref[t, part, :, piece] for part in range(2) for site_ref in site_refs]
            more = mul_t(q_ref[0, t].reshape(2 * rows, cols), jnp.concatenate(right, axis=0))
            total = more if total is None else total + more
    width = total.shape[1] // 2
    out_ref[0, 0] = (total[:rows, :width] - total[rows:, width:]).astype(BF16)
    out_ref[0, 1] = (total[:rows, width:] + total[rows:, :width]).astype(BF16)


def second_product(pick, own, sib, sites):
    mpo_count, phys, _, rows, cols = own.shape
    y_rows = sum(site.shape[2] for site in sites)
    q_spec = pl.BlockSpec((1, phys, 2, rows, cols), lambda v: (v, 0, 0, 0, 0))
    return pl.pallas_call(
        second_kernel,
        grid=(mpo_count,),
        in_specs=[pl.BlockSpec(memory_space=pltpu.SMEM), q_spec, q_spec]
        + [pl.BlockSpec(site.shape, lambda v: (0, 0, 0, 0)) for site in sites],
        out_specs=pl.BlockSpec((1, 2, rows, y_rows), lambda v: (v, 0, 0, 0)),
        out_shape=jax.ShapeDtypeStruct((mpo_count, 2, rows, y_rows), BF16),
        compiler_params=params(1),
        cost_estimate=LIGHT,
        name="second_product",
    )(pick, own, sib, *sites)


def finish_kernel(pick_ref, mine_ref, siblings_ref, *refs):
    out_ref = refs[-1]
    half = mine_ref.shape[3]
    halves = [pl.multiple_of(core * half, half) for core in (pick_ref[1], 1 - pick_ref[1])]

    @pl.when(pick_ref[0] == 0)
    def _():
        for ref, first in zip((mine_ref, siblings_ref), halves):
            out_ref[0, 0, :, pl.ds(first, half)] = ref[0, 0].astype(F32)

    @pl.when(pick_ref[0] != 0)
    def _():
        for side, first in enumerate(halves):
            one, two = refs[2 * side : 2 * side + 2]
            place = pl.ds(first, one.shape[3])
            out_ref[0, 0, :, place] = one[0, 0].astype(F32) + two[0, 0].astype(F32)


def finish(pick, mine, siblings, part):
    mpo_count, _, rows, half = mine.shape

    def spec(value, used):
        def index(v, p, pick):
            wanted = (pick[0] == used).astype(jnp.int32)
            return (v * wanted, p * wanted, 0, 0)

        return pl.BlockSpec((1, 1) + value.shape[2:], index)

    return pl.pallas_call(
        finish_kernel,
        grid_spec=pltpu.PrefetchScalarGridSpec(
            num_scalar_prefetch=1,
            grid=(mpo_count, 2),
            in_specs=[spec(mine, 0), spec(siblings, 0)] + [spec(value, 1) for value in part],
            out_specs=pl.BlockSpec((1, 1, rows, 2 * half), lambda v, p, pick: (v, p, 0, 0)),
        ),
        out_shape=jax.ShapeDtypeStruct((mpo_count, 2, rows, 2 * half), F32),
        compiler_params=params(2),
        cost_estimate=LIGHT,
        name="finish",
    )(pick, mine, siblings, *part)


def finish_last_kernel(pick_ref, *refs):
    part, (_, out_ref, sum_ref, sems) = refs[:4], refs[4:]
    mpo_count, _, _, width = part[0].shape
    half = out_ref.shape[3] // 2

    @pl.when(pick_ref[0] != 0)
    def _():
        copies = []
        for v in range(mpo_count):
            for p in range(2):
                for side, core in enumerate((pick_ref[1], 1 - pick_ref[1])):
                    one, two = part[2 * side : 2 * side + 2]
                    sum_ref[side, v, p] = one[v, p].astype(F32) + two[v, p].astype(F32)
                    place = pl.ds(pl.multiple_of(core * half + half - width, width), width)
                    copies.append(
                        pltpu.make_async_copy(
                            sum_ref.at[side, v, p], out_ref.at[v, p, :, place], sems.at[side, v, p]
                        )
                    )
                    copies[-1].start()
        for copy in copies:
            copy.wait()


def finish_last(pick, out, part):
    mpo_count, _, rows, width = part[0].shape
    anywhere = pl.BlockSpec(memory_space=pl.ANY)
    return pl.pallas_call(
        finish_last_kernel,
        in_specs=[pl.BlockSpec(memory_space=pltpu.SMEM)]
        + [pl.BlockSpec(memory_space=pltpu.VMEM)] * 4
        + [anywhere],
        out_specs=anywhere,
        out_shape=jax.ShapeDtypeStruct(out.shape, F32),
        input_output_aliases={5: 0},
        scratch_shapes=[
            pltpu.VMEM((2, mpo_count, 2, rows, width), F32),
            pltpu.SemaphoreType.DMA((2, mpo_count, 2)),
        ],
        compiler_params=pltpu.CompilerParams(vmem_limit_bytes=VMEM_BYTES),
        cost_estimate=LIGHT,
        name="finish_last",
    )(pick, *part, out)


def after(value, *earlier):
    return lax.optimization_barrier((value,) + earlier)[0]


def swap(value):
    return lax.ppermute(value, "depth", [(0, 1), (1, 0)])


def split_inputs(environment, mpo):
    depth = lax.axis_index("depth")
    w_local, half = environment.shape[0], environment.shape[3]
    cols = half // 2
    env_own = lax.dynamic_slice_in_dim(environment, depth * cols, cols, 3)
    env_sib = swap(lax.dynamic_slice_in_dim(environment, (1 - depth) * cols, cols, 3))
    mpo_mine = jnp.concatenate(
        [
            lax.dynamic_slice_in_dim(mpo, depth * w_local, w_local, 0),
            lax.dynamic_slice_in_dim(mpo, (1 - depth) * w_local, w_local, 0),
        ],
        axis=0,
    )
    return env_own, env_sib, mpo_mine


def one_product(left, right, dims):
    return jnp.einsum(dims, left, right, preferred_element_type=F32)


def any_line(environment, site_tensor, mpo):
    depth = lax.axis_index("depth")
    env_own, env_sib, mpo_mine = split_inputs(environment, mpo)
    env_own = lax.all_gather(env_own, "row", axis=2, tiled=True)
    env_sib = lax.all_gather(env_sib, "row", axis=2, tiled=True)
    env = jnp.concatenate([env_own, env_sib], axis=0)
    cols = env.shape[3]
    planar = jnp.transpose(site_tensor, (0, 2, 1, 3))
    site_own = lax.dynamic_slice_in_dim(planar, depth * cols, cols, 3)
    site = lax.all_gather(planar, "col", axis=3, tiled=True)
    first = functools.partial(one_product, dims="sxa,wac->wsxc")
    g = jnp.stack(
        [
            first(site[:, 0], env[:, 0]) + first(site[:, 1], env[:, 1]),
            first(site[:, 0], env[:, 1]) - first(site[:, 1], env[:, 0]),
        ],
        axis=2,
    )
    q = jnp.einsum("wvst,wspxc->vtpxc", mpo_mine, g, precision=lax.Precision.HIGHEST).astype(BF16)
    site = lax.all_gather(site_own, "row", axis=2, tiled=True)
    second = functools.partial(one_product, dims="vtxc,tyc->vxy")
    total = jnp.stack(
        [
            second(q[:, :, 0], site[:, 0]) - second(q[:, :, 1], site[:, 1]),
            second(q[:, :, 0], site[:, 1]) + second(q[:, :, 1], site[:, 0]),
        ],
        axis=1,
    )
    return lax.psum_scatter(total, ("col", "depth"), scatter_dimension=3, tiled=True)


def ring(environment, site_tensor, mpo):
    row_count, col_count = lax.axis_size("row"), lax.axis_size("col")
    row, col, depth = (lax.axis_index(axis) for axis in ("row", "col", "depth"))
    axes = ("row", "col", "depth")
    place = lambda r, c, d: (r * col_count + c) * 2 + d
    shift = lambda value: lax.ppermute(
        value, "row", [(r, (r + 1) % row_count) for r in range(row_count)]
    )
    turn = lambda value: lax.ppermute(value, "col", [(0, 1), (1, 0)])
    in_order = lambda mine, sibling, axis: jnp.where(
        depth == 0,
        jnp.concatenate([mine, sibling], axis=axis),
        jnp.concatenate([sibling, mine], axis=axis),
    )

    env_own, env_sib, mpo_mine = split_inputs(environment, mpo)
    envs = [env_own, env_sib]
    for _ in range(row_count - 1):
        envs += [shift(envs[-2]), shift(envs[-1])]

    planar = jnp.transpose(after(site_tensor, env_sib), (0, 2, 1, 3))
    rows = planar.shape[2]
    half = rows // 2
    mine = lax.dynamic_slice_in_dim(planar, depth * half, half, 2)
    other = turn(mine)
    other = in_order(other, swap(after(other, envs[3], envs[4])), 2)
    site = jnp.where(col == 0, jnp.stack([planar, other]), jnp.stack([other, planar]))

    parts = [mine[:, :, : half // 2], mine[:, :, half // 2 :]]
    travelling = [[shift(after(part, env, site)) for part, env in zip(parts, envs[-2:])]]
    for _ in range(row_count - 2):
        travelling.append([shift(part) for part in travelling[-1]])

    blocks = jnp.stack([lax.rem(row - k + row_count, row_count) for k in range(row_count)])
    blocks = blocks.astype(jnp.int32)
    q = first_product(blocks, mpo_mine, site, envs, half, half)
    q_sib = swap(after(q, *travelling[0]))

    goals = [
        [((r - step) % row_count // 2, (r - step) % row_count % 2) for r in range(row_count)]
        for step in range(row_count)
    ]
    pick = depth.astype(jnp.int32).reshape(1)

    def second(sites, *earlier):
        return second_product(after(pick, *earlier), q, q_sib, sites)

    def turn_to_goal(value, goal):
        return lax.ppermute(
            value,
            axes,
            [(place(r, 1 - c, d), place(r, c, d)) for r, (c, _) in enumerate(goal) for d in range(2)],
        )

    def send(value, goal, turned, crossed):
        return lax.ppermute(
            value,
            axes,
            [
                (place(r, 1 - c if turned else c, 1 - d if crossed else d), place(r, c, d))
                for r, (c, d) in enumerate(goal)
            ],
        )

    step_of = lambda d: lax.rem(row - col * 2 - d + row_count, row_count)
    lows = [second(parts)]
    turned = [turn_to_goal(lows[0], goals[0])]
    lows.append(second(travelling[0], lows[0], travelling[1][0]))
    turned.append(turn_to_goal(lows[1], goals[1]))
    lows.append(second(travelling[1], lows[1], turned[0]))
    turned.append(turn_to_goal(lows[2], goals[2]))
    totals = [low.astype(F32) + came.astype(F32) for low, came in zip(lows, turned)]

    def total_at(step):
        return jnp.where(step == 0, totals[0], jnp.where(step == 1, totals[1], totals[2]))

    def last_part(number, *earlier):
        low = second([travelling[2][number]], *earlier)
        ways = ((True, False), (True, True), (False, True))
        return [low] + [send(low, goals[3], *way) for way in ways]

    last = [last_part(0, lows[2])]
    mine, siblings = total_at(step_of(depth)), total_at(step_of(1 - depth)).astype(BF16)
    last.append(last_part(1, *last[0], mine, siblings))
    siblings = swap(siblings)
    came_last = (step_of(depth) == row_count - 1).astype(jnp.int32)
    pick = jnp.stack([came_last, depth.astype(jnp.int32)])
    out = finish(after(pick, last[1][0]), mine, siblings, last[0])
    return finish_last(pick, out, last[1])


def solution(mesh):
    placed = (
        P(("groups", "depth"), None, "row", "col"),
        P("groups", "row", None, "col"),
        P("groups", None, None, None),
    )
    fits = mesh.shape["col"] == 2 and mesh.shape["row"] == 2 * mesh.shape["col"]
    return jax.shard_map(
        ring if fits else any_line,
        mesh=mesh,
        in_specs=placed,
        out_specs=P("groups", None, "row", ("col", "depth")),
        check_vma=False,
    )
```

```python
import functools
import jax
import jax.numpy as jnp
from jax import lax
from jax.experimental import pallas as pl
from jax.experimental.pallas import tpu as pltpu
from jax.sharding import PartitionSpec as P

F32 = jnp.float32
BF16 = jnp.bfloat16
VMEM_BYTES = 40 * 1024 * 1024
LIGHT = pl.CostEstimate(flops=0, bytes_accessed=0, transcendentals=0)


def params(steps):
    return pltpu.CompilerParams(
        dimension_semantics=("arbitrary",) * steps, vmem_limit_bytes=VMEM_BYTES
    )


def mul(left, right):
    return jnp.dot(left, right, preferred_element_type=F32)


def mul_t(left, right):
    return lax.dot_general(left, right, (((1,), (1,)), ((), ())), preferred_element_type=F32)


def first_kernel(w_local, block_ref, mpo_ref, site_ref, *refs):
    q_ref, g_ref = refs[-2:]
    env_refs = refs[:-2]
    mpo_count, phys, _, rows, _ = q_ref.shape
    depth = env_refs[0].shape[2]
    per_col = site_ref.shape[-1] // depth
    for which in range(2):
        for w in range(w_local):
            with_real, with_imag = None, None
            for number in range(len(env_refs) // 2):
                block = block_ref[number]
                piece = pl.ds(pl.multiple_of((block % per_col) * depth, depth), depth)
                left = site_ref[block // per_col, 0, :, :, :, piece].reshape(phys * 2 * rows, depth)
                env_ref = env_refs[number * 2 + which]
                more_real, more_imag = mul(left, env_ref[w, 0]), mul(left, env_ref[w, 1])
                with_real = more_real if with_real is None else with_real + more_real
                with_imag = more_imag if with_imag is None else with_imag + more_imag
            for s in range(phys):
                real, imag = (slice((2 * s + part) * rows, (2 * s + part + 1) * rows) for part in range(2))
                there = slice(s * rows, (s + 1) * rows)
                g_ref[which * w_local + w, 0, there] = with_real[real] + with_imag[imag]
                g_ref[which * w_local + w, 1, there] = with_imag[real] - with_real[imag]
    for part in range(2):
        for v in range(mpo_count):
            for t in range(phys):
                total = None
                for w in range(2 * w_local):
                    for s in range(phys):
                        term = mpo_ref[w, v, s, t] * g_ref[w, part, s * rows : (s + 1) * rows]
                        total = term if total is None else total + term
                q_ref[v, t, part] = total.astype(BF16)


def first_product(blocks, mpo, site, envs, col_tile):
    col_count, tiles, phys, _, rows, wide = site.shape
    w_local, _, depth, cols = envs[0].shape
    mpo_count = mpo.shape[1]
    smem = pl.BlockSpec(memory_space=pltpu.SMEM)
    return pl.pallas_call(
        functools.partial(first_kernel, w_local),
        grid=(tiles, cols // col_tile),
        in_specs=[
            smem,
            smem,
            pl.BlockSpec((col_count, 1, phys, 2, rows, wide), lambda i, j: (0, i, 0, 0, 0, 0)),
        ]
        + [pl.BlockSpec((w_local, 2, depth, col_tile), lambda i, j: (0, 0, 0, j))] * len(envs),
        out_specs=pl.BlockSpec((mpo_count, phys, 2, rows, col_tile), lambda i, j: (0, 0, 0, i, j)),
        out_shape=jax.ShapeDtypeStruct((mpo_count, phys, 2, tiles * rows, cols), BF16),
        scratch_shapes=[pltpu.VMEM((2 * w_local, 2, phys * rows, col_tile), F32)],
        compiler_params=params(2),
        cost_estimate=LIGHT,
        name="first_product",
    )(blocks, mpo, site, *envs)


def second_kernel(pick_ref, own_ref, sib_ref, *refs):
    site_refs, out_ref = refs[:-1], refs[-1]
    phys, _, rows, cols = own_ref.shape[1:]
    total = None
    for q_ref, quarter in ((own_ref, pick_ref[0]), (sib_ref, 1 - pick_ref[0])):
        piece = pl.ds(pl.multiple_of(quarter * cols, cols), cols)
        for t in range(phys):
            right = [site_ref[t, part, :, piece] for part in range(2) for site_ref in site_refs]
            more = mul_t(q_ref[0, t].reshape(2 * rows, cols), jnp.concatenate(right, axis=0))
            total = more if total is None else total + more
    width = total.shape[1] // 2
    out_ref[0, 0] = (total[:rows, :width] - total[rows:, width:]).astype(BF16)
    out_ref[0, 1] = (total[:rows, width:] + total[rows:, :width]).astype(BF16)


def second_product(pick, own, sib, sites):
    mpo_count, phys, _, rows, cols = own.shape
    y_rows = sum(site.shape[2] for site in sites)
    q_spec = pl.BlockSpec((1, phys, 2, rows, cols), lambda v: (v, 0, 0, 0, 0))
    return pl.pallas_call(
        second_kernel,
        grid=(mpo_count,),
        in_specs=[pl.BlockSpec(memory_space=pltpu.SMEM), q_spec, q_spec]
        + [pl.BlockSpec(site.shape, lambda v: (0, 0, 0, 0)) for site in sites],
        out_specs=pl.BlockSpec((1, 2, rows, y_rows), lambda v: (v, 0, 0, 0)),
        out_shape=jax.ShapeDtypeStruct((mpo_count, 2, rows, y_rows), BF16),
        compiler_params=params(1),
        cost_estimate=LIGHT,
        name="second_product",
    )(pick, own, sib, *sites)


def finish_kernel(pick_ref, mine_ref, siblings_ref, *refs):
    out_ref = refs[-1]
    half = mine_ref.shape[3]
    halves = [pl.multiple_of(core * half, half) for core in (pick_ref[1], 1 - pick_ref[1])]

    @pl.when(pick_ref[0] == 0)
    def _():
        for ref, first in zip((mine_ref, siblings_ref), halves):
            out_ref[0, 0, :, pl.ds(first, half)] = ref[0, 0].astype(F32)

    @pl.when(pick_ref[0] != 0)
    def _():
        for side, first in enumerate(halves):
            one, two = refs[2 * side : 2 * side + 2]
            place = pl.ds(first, one.shape[3])
            out_ref[0, 0, :, place] = one[0, 0].astype(F32) + two[0, 0].astype(F32)


def finish(pick, mine, siblings, part):
    mpo_count, _, rows, half = mine.shape

    def spec(value, used):
        def index(v, p, pick):
            wanted = (pick[0] == used).astype(jnp.int32)
            return (v * wanted, p * wanted, 0, 0)

        return pl.BlockSpec((1, 1) + value.shape[2:], index)

    return pl.pallas_call(
        finish_kernel,
        grid_spec=pltpu.PrefetchScalarGridSpec(
            num_scalar_prefetch=1,
            grid=(mpo_count, 2),
            in_specs=[spec(mine, 0), spec(siblings, 0)] + [spec(value, 1) for value in part],
            out_specs=pl.BlockSpec((1, 1, rows, 2 * half), lambda v, p, pick: (v, p, 0, 0)),
        ),
        out_shape=jax.ShapeDtypeStruct((mpo_count, 2, rows, 2 * half), F32),
        compiler_params=params(2),
        cost_estimate=LIGHT,
        name="finish",
    )(pick, mine, siblings, *part)


def finish_last_kernel(pick_ref, *refs):
    part, (_, out_ref, sum_ref, sems) = refs[:4], refs[4:]
    mpo_count, _, _, width = part[0].shape
    half = out_ref.shape[3] // 2

    @pl.when(pick_ref[0] != 0)
    def _():
        copies = []
        for v in range(mpo_count):
            for p in range(2):
                for side, core in enumerate((pick_ref[1], 1 - pick_ref[1])):
                    one, two = part[2 * side : 2 * side + 2]
                    sum_ref[side, v, p] = one[v, p].astype(F32) + two[v, p].astype(F32)
                    place = pl.ds(pl.multiple_of(core * half + half - width, width), width)
                    copies.append(
                        pltpu.make_async_copy(
                            sum_ref.at[side, v, p], out_ref.at[v, p, :, place], sems.at[side, v, p]
                        )
                    )
                    copies[-1].start()
        for copy in copies:
            copy.wait()


def finish_last(pick, out, part):
    mpo_count, _, rows, width = part[0].shape
    anywhere = pl.BlockSpec(memory_space=pl.ANY)
    return pl.pallas_call(
        finish_last_kernel,
        in_specs=[pl.BlockSpec(memory_space=pltpu.SMEM)]
        + [pl.BlockSpec(memory_space=pltpu.VMEM)] * 4
        + [anywhere],
        out_specs=anywhere,
        out_shape=jax.ShapeDtypeStruct(out.shape, F32),
        input_output_aliases={5: 0},
        scratch_shapes=[
            pltpu.VMEM((2, mpo_count, 2, rows, width), F32),
            pltpu.SemaphoreType.DMA((2, mpo_count, 2)),
        ],
        compiler_params=pltpu.CompilerParams(vmem_limit_bytes=VMEM_BYTES),
        cost_estimate=LIGHT,
        name="finish_last",
    )(pick, *part, out)


def after(value, *earlier):
    return lax.optimization_barrier((value,) + earlier)[0]


def swap(value):
    return lax.ppermute(value, "depth", [(0, 1), (1, 0)])


def split_inputs(environment, mpo):
    depth = lax.axis_index("depth")
    w_local, half = environment.shape[0], environment.shape[3]
    cols = half // 2
    env_own = lax.dynamic_slice_in_dim(environment, depth * cols, cols, 3)
    env_sib = swap(lax.dynamic_slice_in_dim(environment, (1 - depth) * cols, cols, 3))
    mpo_mine = jnp.concatenate(
        [
            lax.dynamic_slice_in_dim(mpo, depth * w_local, w_local, 0),
            lax.dynamic_slice_in_dim(mpo, (1 - depth) * w_local, w_local, 0),
        ],
        axis=0,
    )
    return env_own, env_sib, mpo_mine


def one_product(left, right, dims):
    return jnp.einsum(dims, left, right, preferred_element_type=F32)


def any_line(environment, site_tensor, mpo):
    depth = lax.axis_index("depth")
    env_own, env_sib, mpo_mine = split_inputs(environment, mpo)
    env_own = lax.all_gather(env_own, "row", axis=2, tiled=True)
    env_sib = lax.all_gather(env_sib, "row", axis=2, tiled=True)
    env = jnp.concatenate([env_own, env_sib], axis=0)
    cols = env.shape[3]
    planar = jnp.transpose(site_tensor, (0, 2, 1, 3))
    site_own = lax.dynamic_slice_in_dim(planar, depth * cols, cols, 3)
    site = lax.all_gather(planar, "col", axis=3, tiled=True)
    first = functools.partial(one_product, dims="sxa,wac->wsxc")
    g = jnp.stack(
        [
            first(site[:, 0], env[:, 0]) + first(site[:, 1], env[:, 1]),
            first(site[:, 0], env[:, 1]) - first(site[:, 1], env[:, 0]),
        ],
        axis=2,
    )
    q = jnp.einsum("wvst,wspxc->vtpxc", mpo_mine, g, precision=lax.Precision.HIGHEST).astype(BF16)
    site = lax.all_gather(site_own, "row", axis=2, tiled=True)
    second = functools.partial(one_product, dims="vtxc,tyc->vxy")
    total = jnp.stack(
        [
            second(q[:, :, 0], site[:, 0]) - second(q[:, :, 1], site[:, 1]),
            second(q[:, :, 0], site[:, 1]) + second(q[:, :, 1], site[:, 0]),
        ],
        axis=1,
    )
    return lax.psum_scatter(total, ("col", "depth"), scatter_dimension=3, tiled=True)


def ring(environment, site_tensor, mpo):
    row_count, col_count = lax.axis_size("row"), lax.axis_size("col")
    row, col, depth = (lax.axis_index(axis) for axis in ("row", "col", "depth"))
    axes = ("row", "col", "depth")
    place = lambda r, c, d: (r * col_count + c) * 2 + d
    shift = lambda value: lax.ppermute(
        value, "row", [(r, (r + 1) % row_count) for r in range(row_count)]
    )
    env_own, env_sib, mpo_mine = split_inputs(environment, mpo)
    envs = [env_own, env_sib]
    for _ in range(row_count - 1):
        envs += [shift(envs[-2]), shift(envs[-1])]

    planar = jnp.transpose(after(site_tensor, env_sib), (0, 2, 1, 3))
    rows = planar.shape[2]
    half = rows // 2
    mine = lax.dynamic_slice_in_dim(planar, depth * half, half, 2)
    site = lax.all_gather(after(mine, envs[2]), ("col", "depth"), axis=0).reshape((col_count, 2) + mine.shape)

    parts = [mine[:, :, : half // 2], mine[:, :, half // 2 :]]
    travelling = [[shift(after(part, env)) for part, env in zip(parts, envs[-2:])]]
    for _ in range(row_count - 2):
        travelling.append([shift(part) for part in travelling[-1]])

    blocks = jnp.stack([lax.rem(row - k + row_count, row_count) for k in range(row_count)])
    blocks = blocks.astype(jnp.int32)
    q = first_product(blocks, mpo_mine, site, envs, half)
    q_sib = swap(after(q, *travelling[0]))

    goals = [
        [((r - step) % row_count // 2, (r - step) % row_count % 2) for r in range(row_count)]
        for step in range(row_count)
    ]
    pick = depth.astype(jnp.int32).reshape(1)

    def second(sites, *earlier):
        return second_product(after(pick, *earlier), q, q_sib, sites)

    def turn_to_goal(value, goal):
        return lax.ppermute(
            value,
            axes,
            [(place(r, 1 - c, d), place(r, c, d)) for r, (c, _) in enumerate(goal) for d in range(2)],
        )

    def send(value, goal, turned, crossed):
        return lax.ppermute(
            value,
            axes,
            [
                (place(r, 1 - c if turned else c, 1 - d if crossed else d), place(r, c, d))
                for r, (c, d) in enumerate(goal)
            ],
        )

    step_of = lambda d: lax.rem(row - col * 2 - d + row_count, row_count)
    lows = [second(parts)]
    turned = [turn_to_goal(lows[0], goals[0])]
    lows.append(second(travelling[0], lows[0], travelling[1][0]))
    turned.append(turn_to_goal(lows[1], goals[1]))
    lows.append(second(travelling[1], lows[1], turned[0]))
    turned.append(turn_to_goal(lows[2], goals[2]))
    totals = [low.astype(F32) + came.astype(F32) for low, came in zip(lows, turned)]

    def total_at(step):
        return jnp.where(step == 0, totals[0], jnp.where(step == 1, totals[1], totals[2]))

    def last_part(number, *earlier):
        low = second([travelling[2][number]], *earlier)
        ways = ((True, False), (True, True), (False, True))
        return [low] + [send(low, goals[3], *way) for way in ways]

    last = [last_part(0, lows[2])]
    mine, siblings = total_at(step_of(depth)), total_at(step_of(1 - depth)).astype(BF16)
    last.append(last_part(1, *last[0], mine, siblings))
    siblings = swap(siblings)
    came_last = (step_of(depth) == row_count - 1).astype(jnp.int32)
    pick = jnp.stack([came_last, depth.astype(jnp.int32)])
    out = finish(after(pick, last[1][0]), mine, siblings, last[0])
    return finish_last(pick, out, last[1])


def solution(mesh):
    placed = (
        P(("groups", "depth"), None, "row", "col"),
        P("groups", "row", None, "col"),
        P("groups", None, None, None),
    )
    fits = mesh.shape["col"] == 2 and mesh.shape["row"] == 2 * mesh.shape["col"]
    return jax.shard_map(
        ring if fits else any_line,
        mesh=mesh,
        in_specs=placed,
        out_specs=P("groups", None, "row", ("col", "depth")),
        check_vma=False,
    )
```

```python
import functools
import jax
import jax.numpy as jnp
from jax import lax
from jax.experimental import pallas as pl
from jax.experimental.pallas import tpu as pltpu
from jax.sharding import PartitionSpec as P

F32 = jnp.float32
BF16 = jnp.bfloat16
MIB = 1024 * 1024
LIGHT = pl.CostEstimate(flops=0, bytes_accessed=0, transcendentals=0)


def params(steps, mib):
    return pltpu.CompilerParams(
        dimension_semantics=("arbitrary",) * steps, vmem_limit_bytes=mib * MIB
    )


def mul(left, right):
    return jnp.dot(left, right, preferred_element_type=F32)


def mul_t(left, right):
    return lax.dot_general(left, right, (((1,), (1,)), ((), ())), preferred_element_type=F32)


def first_kernel(w_local, block_ref, mpo_ref, site_ref, *refs):
    q_ref, g_ref = refs[-2:]
    env_refs = refs[:-2]
    mpo_count, phys, _, rows, _ = q_ref.shape
    depth = env_refs[0].shape[2]
    per_col = site_ref.shape[-1] // depth
    for which in range(2):
        for w in range(w_local):
            with_real, with_imag = None, None
            for number in range(len(env_refs) // 2):
                block = block_ref[number]
                piece = pl.ds(pl.multiple_of((block % per_col) * depth, depth), depth)
                left = site_ref[block // per_col, :, :, :, piece].reshape(phys * 2 * rows, depth)
                env_ref = env_refs[number * 2 + which]
                more_real, more_imag = mul(left, env_ref[w, 0]), mul(left, env_ref[w, 1])
                with_real = more_real if with_real is None else with_real + more_real
                with_imag = more_imag if with_imag is None else with_imag + more_imag
            for s in range(phys):
                real, imag = (slice((2 * s + part) * rows, (2 * s + part + 1) * rows) for part in range(2))
                there = slice(s * rows, (s + 1) * rows)
                g_ref[which * w_local + w, 0, there] = with_real[real] + with_imag[imag]
                g_ref[which * w_local + w, 1, there] = with_imag[real] - with_real[imag]
    for part in range(2):
        for v in range(mpo_count):
            for t in range(phys):
                total = None
                for w in range(2 * w_local):
                    for s in range(phys):
                        term = mpo_ref[w, v, s, t] * g_ref[w, part, s * rows : (s + 1) * rows]
                        total = term if total is None else total + term
                q_ref[v, t, part] = total.astype(BF16)


def first_product(blocks, mpo, site, envs, row_tile, col_tile):
    col_count, phys, _, rows, wide = site.shape
    w_local, _, depth, cols = envs[0].shape
    mpo_count = mpo.shape[1]
    smem = pl.BlockSpec(memory_space=pltpu.SMEM)
    return pl.pallas_call(
        functools.partial(first_kernel, w_local),
        grid=(rows // row_tile, cols // col_tile),
        in_specs=[
            smem,
            smem,
            pl.BlockSpec((col_count, phys, 2, row_tile, wide), lambda i, j: (0, 0, 0, i, 0)),
        ]
        + [pl.BlockSpec((w_local, 2, depth, col_tile), lambda i, j: (0, 0, 0, j))] * len(envs),
        out_specs=pl.BlockSpec((mpo_count, phys, 2, row_tile, col_tile), lambda i, j: (0, 0, 0, i, j)),
        out_shape=jax.ShapeDtypeStruct((mpo_count, phys, 2, rows, cols), BF16),
        scratch_shapes=[pltpu.VMEM((2 * w_local, 2, phys * row_tile, col_tile), F32)],
        compiler_params=params(2, 28),
        cost_estimate=LIGHT,
        name="first_product",
    )(blocks, mpo, site, *envs)


def second_kernel(pick_ref, own_ref, sib_ref, *refs):
    site_refs, out_ref = refs[:-1], refs[-1]
    phys, _, rows, cols = own_ref.shape[1:]
    total = None
    for q_ref, quarter in ((own_ref, pick_ref[0]), (sib_ref, 1 - pick_ref[0])):
        piece = pl.ds(pl.multiple_of(quarter * cols, cols), cols)
        for t in range(phys):
            right = [site_ref[t, part, :, piece] for part in range(2) for site_ref in site_refs]
            more = mul_t(q_ref[0, t].reshape(2 * rows, cols), jnp.concatenate(right, axis=0))
            total = more if total is None else total + more
    width = total.shape[1] // 2
    out_ref[0, 0] = (total[:rows, :width] - total[rows:, width:]).astype(BF16)
    out_ref[0, 1] = (total[:rows, width:] + total[rows:, :width]).astype(BF16)


def second_product(pick, own, sib, sites):
    mpo_count, phys, _, rows, cols = own.shape
    y_rows = sum(site.shape[2] for site in sites)
    q_spec = pl.BlockSpec((1, phys, 2, rows, cols), lambda v: (v, 0, 0, 0, 0))
    return pl.pallas_call(
        second_kernel,
        grid=(mpo_count,),
        in_specs=[pl.BlockSpec(memory_space=pltpu.SMEM), q_spec, q_spec]
        + [pl.BlockSpec(site.shape, lambda v: (0, 0, 0, 0)) for site in sites],
        out_specs=pl.BlockSpec((1, 2, rows, y_rows), lambda v: (v, 0, 0, 0)),
        out_shape=jax.ShapeDtypeStruct((mpo_count, 2, rows, y_rows), BF16),
        compiler_params=params(1, 20),
        cost_estimate=LIGHT,
        name="second_product",
    )(pick, own, sib, *sites)


def finish_kernel(pick_ref, mine_ref, siblings_ref, *refs):
    out_ref = refs[-1]
    half = mine_ref.shape[3]
    halves = [pl.multiple_of(core * half, half) for core in (pick_ref[1], 1 - pick_ref[1])]

    @pl.when(pick_ref[0] == 0)
    def _():
        for ref, first in zip((mine_ref, siblings_ref), halves):
            out_ref[0, 0, :, pl.ds(first, half)] = ref[0, 0].astype(F32)

    @pl.when(pick_ref[0] != 0)
    def _():
        for side, first in enumerate(halves):
            one, two = refs[2 * side : 2 * side + 2]
            place = pl.ds(first, one.shape[3])
            out_ref[0, 0, :, place] = one[0, 0].astype(F32) + two[0, 0].astype(F32)


def finish(pick, mine, siblings, part):
    mpo_count, _, rows, half = mine.shape

    def spec(value, used):
        def index(v, p, pick):
            wanted = (pick[0] == used).astype(jnp.int32)
            return (v * wanted, p * wanted, 0, 0)

        return pl.BlockSpec((1, 1) + value.shape[2:], index)

    return pl.pallas_call(
        finish_kernel,
        grid_spec=pltpu.PrefetchScalarGridSpec(
            num_scalar_prefetch=1,
            grid=(mpo_count, 2),
            in_specs=[spec(mine, 0), spec(siblings, 0)] + [spec(value, 1) for value in part],
            out_specs=pl.BlockSpec((1, 1, rows, 2 * half), lambda v, p, pick: (v, p, 0, 0)),
        ),
        out_shape=jax.ShapeDtypeStruct((mpo_count, 2, rows, 2 * half), F32),
        compiler_params=params(2, 16),
        cost_estimate=LIGHT,
        name="finish",
    )(pick, mine, siblings, *part)


def finish_last_kernel(pick_ref, *refs):
    part, (_, out_ref, sum_ref, sems) = refs[:4], refs[4:]
    mpo_count, _, _, width = part[0].shape
    half = out_ref.shape[3] // 2

    @pl.when(pick_ref[0] != 0)
    def _():
        copies = []
        for v in range(mpo_count):
            for p in range(2):
                for side, core in enumerate((pick_ref[1], 1 - pick_ref[1])):
                    one, two = part[2 * side : 2 * side + 2]
                    sum_ref[side, v, p] = one[v, p].astype(F32) + two[v, p].astype(F32)
                    place = pl.ds(pl.multiple_of(core * half + half - width, width), width)
                    copies.append(
                        pltpu.make_async_copy(
                            sum_ref.at[side, v, p], out_ref.at[v, p, :, place], sems.at[side, v, p]
                        )
                    )
                    copies[-1].start()
        for copy in copies:
            copy.wait()


def finish_last(pick, out, part):
    mpo_count, _, rows, width = part[0].shape
    anywhere = pl.BlockSpec(memory_space=pl.ANY)
    return pl.pallas_call(
        finish_last_kernel,
        in_specs=[pl.BlockSpec(memory_space=pltpu.SMEM)]
        + [pl.BlockSpec(memory_space=pltpu.VMEM)] * 4
        + [anywhere],
        out_specs=anywhere,
        out_shape=jax.ShapeDtypeStruct(out.shape, F32),
        input_output_aliases={5: 0},
        scratch_shapes=[
            pltpu.VMEM((2, mpo_count, 2, rows, width), F32),
            pltpu.SemaphoreType.DMA((2, mpo_count, 2)),
        ],
        compiler_params=pltpu.CompilerParams(vmem_limit_bytes=12 * MIB),
        cost_estimate=LIGHT,
        name="finish_last",
    )(pick, *part, out)


def after(value, *earlier):
    return lax.optimization_barrier((value,) + earlier)[0]


def swap(value):
    return lax.ppermute(value, "depth", [(0, 1), (1, 0)])


def split_inputs(environment, mpo):
    depth = lax.axis_index("depth")
    w_local, half = environment.shape[0], environment.shape[3]
    cols = half // 2
    env_own = lax.dynamic_slice_in_dim(environment, depth * cols, cols, 3)
    env_sib = swap(lax.dynamic_slice_in_dim(environment, (1 - depth) * cols, cols, 3))
    mpo_mine = jnp.concatenate(
        [
            lax.dynamic_slice_in_dim(mpo, depth * w_local, w_local, 0),
            lax.dynamic_slice_in_dim(mpo, (1 - depth) * w_local, w_local, 0),
        ],
        axis=0,
    )
    return env_own, env_sib, mpo_mine


def one_product(left, right, dims):
    return jnp.einsum(dims, left, right, preferred_element_type=F32)


def any_line(environment, site_tensor, mpo):
    depth = lax.axis_index("depth")
    env_own, env_sib, mpo_mine = split_inputs(environment, mpo)
    env_own = lax.all_gather(env_own, "row", axis=2, tiled=True)
    env_sib = lax.all_gather(env_sib, "row", axis=2, tiled=True)
    env = jnp.concatenate([env_own, env_sib], axis=0)
    cols = env.shape[3]
    planar = jnp.transpose(site_tensor, (0, 2, 1, 3))
    site_own = lax.dynamic_slice_in_dim(planar, depth * cols, cols, 3)
    site = lax.all_gather(planar, "col", axis=3, tiled=True)
    first = functools.partial(one_product, dims="sxa,wac->wsxc")
    g = jnp.stack(
        [
            first(site[:, 0], env[:, 0]) + first(site[:, 1], env[:, 1]),
            first(site[:, 0], env[:, 1]) - first(site[:, 1], env[:, 0]),
        ],
        axis=2,
    )
    q = jnp.einsum("wvst,wspxc->vtpxc", mpo_mine, g, precision=lax.Precision.HIGHEST).astype(BF16)
    site = lax.all_gather(site_own, "row", axis=2, tiled=True)
    second = functools.partial(one_product, dims="vtxc,tyc->vxy")
    total = jnp.stack(
        [
            second(q[:, :, 0], site[:, 0]) - second(q[:, :, 1], site[:, 1]),
            second(q[:, :, 0], site[:, 1]) + second(q[:, :, 1], site[:, 0]),
        ],
        axis=1,
    )
    return lax.psum_scatter(total, ("col", "depth"), scatter_dimension=3, tiled=True)


def ring(environment, site_tensor, mpo):
    row_count, col_count = lax.axis_size("row"), lax.axis_size("col")
    row, col, depth = (lax.axis_index(axis) for axis in ("row", "col", "depth"))
    axes = ("row", "col", "depth")
    place = lambda r, c, d: (r * col_count + c) * 2 + d
    shift = lambda value: lax.ppermute(
        value, "row", [(r, (r + 1) % row_count) for r in range(row_count)]
    )
    turn = lambda value: lax.ppermute(value, "col", [(0, 1), (1, 0)])
    in_order = lambda mine, sibling, axis: jnp.where(
        depth == 0,
        jnp.concatenate([mine, sibling], axis=axis),
        jnp.concatenate([sibling, mine], axis=axis),
    )

    env_own, env_sib, mpo_mine = split_inputs(environment, mpo)
    envs = [env_own, env_sib]
    for _ in range(row_count - 1):
        envs += [shift(envs[-2]), shift(envs[-1])]

    planar = jnp.transpose(after(site_tensor, env_sib), (0, 2, 1, 3))
    rows = planar.shape[2]
    half = rows // 2
    mine = lax.dynamic_slice_in_dim(planar, depth * half, half, 2)
    other = turn(mine)
    other = in_order(other, swap(after(other, envs[3], envs[4])), 2)
    site = jnp.where(col == 0, jnp.stack([planar, other]), jnp.stack([other, planar]))

    parts = [mine[:, :, : half // 2], mine[:, :, half // 2 :]]
    travelling = [[shift(after(part, env, site)) for part, env in zip(parts, envs[-2:])]]
    for _ in range(row_count - 2):
        travelling.append([shift(part) for part in travelling[-1]])

    blocks = jnp.stack([lax.rem(row - k + row_count, row_count) for k in range(row_count)])
    blocks = blocks.astype(jnp.int32)
    q = first_product(blocks, mpo_mine, site, envs, half, half)
    q_sib = swap(after(q, *travelling[0]))

    goals = [
        [((r - step) % row_count // 2, (r - step) % row_count % 2) for r in range(row_count)]
        for step in range(row_count)
    ]
    pick = depth.astype(jnp.int32).reshape(1)

    def second(sites, *earlier):
        return second_product(after(pick, *earlier), q, q_sib, sites)

    def turn_to_goal(value, goal):
        return lax.ppermute(
            value,
            axes,
            [(place(r, 1 - c, d), place(r, c, d)) for r, (c, _) in enumerate(goal) for d in range(2)],
        )

    def send(value, goal, turned, crossed):
        return lax.ppermute(
            value,
            axes,
            [
                (place(r, 1 - c if turned else c, 1 - d if crossed else d), place(r, c, d))
                for r, (c, d) in enumerate(goal)
            ],
        )

    step_of = lambda d: lax.rem(row - col * 2 - d + row_count, row_count)
    lows = [second(parts)]
    turned = [turn_to_goal(lows[0], goals[0])]
    lows.append(second(travelling[0], lows[0], travelling[1][0]))
    turned.append(turn_to_goal(lows[1], goals[1]))
    lows.append(second(travelling[1], lows[1], turned[0]))
    turned.append(turn_to_goal(lows[2], goals[2]))
    totals = [low.astype(F32) + came.astype(F32) for low, came in zip(lows, turned)]

    def total_at(step):
        return jnp.where(step == 0, totals[0], jnp.where(step == 1, totals[1], totals[2]))

    def last_part(number, *earlier):
        low = second([travelling[2][number]], *earlier)
        ways = ((True, False), (True, True), (False, True))
        return [low] + [send(low, goals[3], *way) for way in ways]

    last = [last_part(0, lows[2])]
    mine, siblings = total_at(step_of(depth)), total_at(step_of(1 - depth)).astype(BF16)
    last.append(last_part(1, *last[0], mine, siblings))
    siblings = swap(siblings)
    came_last = (step_of(depth) == row_count - 1).astype(jnp.int32)
    pick = jnp.stack([came_last, depth.astype(jnp.int32)])
    out = finish(after(pick, last[1][0]), mine, siblings, last[0])
    return finish_last(pick, out, last[1])


def solution(mesh):
    placed = (
        P(("groups", "depth"), None, "row", "col"),
        P("groups", "row", None, "col"),
        P("groups", None, None, None),
    )
    fits = mesh.shape["col"] == 2 and mesh.shape["row"] == 2 * mesh.shape["col"]
    return jax.shard_map(
        ring if fits else any_line,
        mesh=mesh,
        in_specs=placed,
        out_specs=P("groups", None, "row", ("col", "depth")),
        check_vma=False,
    )
```

```python
import functools
import jax
import jax.numpy as jnp
from jax import lax
from jax.experimental import pallas as pl
from jax.experimental.pallas import tpu as pltpu
from jax.sharding import PartitionSpec as P

F32 = jnp.float32
BF16 = jnp.bfloat16
VMEM_BYTES = 40 * 1024 * 1024
ALL_VMEM_BYTES = 64 * 1024 * 1024
LIGHT = pl.CostEstimate(flops=0, bytes_accessed=0, transcendentals=0)


def params(steps, vmem_bytes=VMEM_BYTES):
    return pltpu.CompilerParams(
        dimension_semantics=("arbitrary",) * steps, vmem_limit_bytes=vmem_bytes
    )


def mul(left, right):
    return jnp.dot(left, right, preferred_element_type=F32)


def mul_t(left, right):
    return lax.dot_general(left, right, (((1,), (1,)), ((), ())), preferred_element_type=F32)


def first_kernel(w_local, block_ref, mpo_ref, site_ref, *refs):
    q_ref, g_ref = refs[-2:]
    env_refs = refs[:-2]
    mpo_count, phys, _, rows, _ = q_ref.shape
    depth = env_refs[0].shape[2]
    per_col = site_ref.shape[-1] // depth
    for which in range(2):
        for w in range(w_local):
            with_real, with_imag = None, None
            for number in range(len(env_refs) // 2):
                block = block_ref[number]
                piece = pl.ds(pl.multiple_of((block % per_col) * depth, depth), depth)
                left = site_ref[block // per_col, :, :, :, piece].reshape(phys * 2 * rows, depth)
                env_ref = env_refs[number * 2 + which]
                more_real, more_imag = mul(left, env_ref[w, 0]), mul(left, env_ref[w, 1])
                with_real = more_real if with_real is None else with_real + more_real
                with_imag = more_imag if with_imag is None else with_imag + more_imag
            for s in range(phys):
                real, imag = (slice((2 * s + part) * rows, (2 * s + part + 1) * rows) for part in range(2))
                there = slice(s * rows, (s + 1) * rows)
                g_ref[which * w_local + w, 0, there] = with_real[real] + with_imag[imag]
                g_ref[which * w_local + w, 1, there] = with_imag[real] - with_real[imag]
    for part in range(2):
        for v in range(mpo_count):
            for t in range(phys):
                total = None
                for w in range(2 * w_local):
                    for s in range(phys):
                        term = mpo_ref[w, v, s, t] * g_ref[w, part, s * rows : (s + 1) * rows]
                        total = term if total is None else total + term
                q_ref[v, t, part] = total.astype(BF16)


def first_product(blocks, mpo, site, envs, row_tile, col_tile):
    col_count, phys, _, rows, wide = site.shape
    w_local, _, depth, cols = envs[0].shape
    mpo_count = mpo.shape[1]
    smem = pl.BlockSpec(memory_space=pltpu.SMEM)
    return pl.pallas_call(
        functools.partial(first_kernel, w_local),
        grid=(rows // row_tile, cols // col_tile),
        in_specs=[
            smem,
            smem,
            pl.BlockSpec((col_count, phys, 2, row_tile, wide), lambda i, j: (0, 0, 0, i, 0)),
        ]
        + [pl.BlockSpec((w_local, 2, depth, col_tile), lambda i, j: (0, 0, 0, j))] * len(envs),
        out_specs=pl.BlockSpec((mpo_count, phys, 2, row_tile, col_tile), lambda i, j: (0, 0, 0, i, j)),
        out_shape=jax.ShapeDtypeStruct((mpo_count, phys, 2, rows, cols), BF16),
        scratch_shapes=[pltpu.VMEM((2 * w_local, 2, phys * row_tile, col_tile), F32)],
        compiler_params=params(2),
        cost_estimate=LIGHT,
        name="first_product",
    )(blocks, mpo, site, *envs)


def second_kernel(pick_ref, own_ref, sib_ref, *refs):
    site_refs, out_ref = refs[:-1], refs[-1]
    phys, _, rows, cols = own_ref.shape[1:]
    total = None
    for q_ref, quarter in ((own_ref, pick_ref[0]), (sib_ref, 1 - pick_ref[0])):
        piece = pl.ds(pl.multiple_of(quarter * cols, cols), cols)
        for t in range(phys):
            right = [site_ref[t, part, :, piece] for part in range(2) for site_ref in site_refs]
            more = mul_t(q_ref[0, t].reshape(2 * rows, cols), jnp.concatenate(right, axis=0))
            total = more if total is None else total + more
    width = total.shape[1] // 2
    out_ref[0, 0] = (total[:rows, :width] - total[rows:, width:]).astype(BF16)
    out_ref[0, 1] = (total[:rows, width:] + total[rows:, :width]).astype(BF16)


def second_product(pick, own, sib, sites, vmem_bytes):
    mpo_count, phys, _, rows, cols = own.shape
    y_rows = sum(site.shape[2] for site in sites)
    q_spec = pl.BlockSpec((1, phys, 2, rows, cols), lambda v: (v, 0, 0, 0, 0))
    return pl.pallas_call(
        second_kernel,
        grid=(mpo_count,),
        in_specs=[pl.BlockSpec(memory_space=pltpu.SMEM), q_spec, q_spec]
        + [pl.BlockSpec(site.shape, lambda v: (0, 0, 0, 0)) for site in sites],
        out_specs=pl.BlockSpec((1, 2, rows, y_rows), lambda v: (v, 0, 0, 0)),
        out_shape=jax.ShapeDtypeStruct((mpo_count, 2, rows, y_rows), BF16),
        compiler_params=params(1, vmem_bytes),
        cost_estimate=LIGHT,
        name="second_product",
    )(pick, own, sib, *sites)


def finish_kernel(pick_ref, mine_ref, siblings_ref, *refs):
    out_ref = refs[-1]
    half = mine_ref.shape[3]
    halves = [pl.multiple_of(core * half, half) for core in (pick_ref[1], 1 - pick_ref[1])]

    @pl.when(pick_ref[0] == 0)
    def _():
        for ref, first in zip((mine_ref, siblings_ref), halves):
            out_ref[0, 0, :, pl.ds(first, half)] = ref[0, 0].astype(F32)

    @pl.when(pick_ref[0] != 0)
    def _():
        for side, first in enumerate(halves):
            one, two = refs[2 * side : 2 * side + 2]
            place = pl.ds(first, one.shape[3])
            out_ref[0, 0, :, place] = one[0, 0].astype(F32) + two[0, 0].astype(F32)


def finish(pick, mine, siblings, part):
    mpo_count, _, rows, half = mine.shape

    def spec(value, used):
        def index(v, p, pick):
            wanted = (pick[0] == used).astype(jnp.int32)
            return (v * wanted, p * wanted, 0, 0)

        return pl.BlockSpec((1, 1) + value.shape[2:], index)

    return pl.pallas_call(
        finish_kernel,
        grid_spec=pltpu.PrefetchScalarGridSpec(
            num_scalar_prefetch=1,
            grid=(mpo_count, 2),
            in_specs=[spec(mine, 0), spec(siblings, 0)] + [spec(value, 1) for value in part],
            out_specs=pl.BlockSpec((1, 1, rows, 2 * half), lambda v, p, pick: (v, p, 0, 0)),
        ),
        out_shape=jax.ShapeDtypeStruct((mpo_count, 2, rows, 2 * half), F32),
        compiler_params=params(2),
        cost_estimate=LIGHT,
        name="finish",
    )(pick, mine, siblings, *part)


def finish_last_kernel(pick_ref, *refs):
    part, (_, out_ref, sum_ref, sems) = refs[:4], refs[4:]
    mpo_count, _, _, width = part[0].shape
    half = out_ref.shape[3] // 2

    @pl.when(pick_ref[0] != 0)
    def _():
        copies = []
        for v in range(mpo_count):
            for p in range(2):
                for side, core in enumerate((pick_ref[1], 1 - pick_ref[1])):
                    one, two = part[2 * side : 2 * side + 2]
                    sum_ref[side, v, p] = one[v, p].astype(F32) + two[v, p].astype(F32)
                    place = pl.ds(pl.multiple_of(core * half + half - width, width), width)
                    copies.append(
                        pltpu.make_async_copy(
                            sum_ref.at[side, v, p], out_ref.at[v, p, :, place], sems.at[side, v, p]
                        )
                    )
                    copies[-1].start()
        for copy in copies:
            copy.wait()


def finish_last(pick, out, part):
    mpo_count, _, rows, width = part[0].shape
    anywhere = pl.BlockSpec(memory_space=pl.ANY)
    return pl.pallas_call(
        finish_last_kernel,
        in_specs=[pl.BlockSpec(memory_space=pltpu.SMEM)]
        + [pl.BlockSpec(memory_space=pltpu.VMEM)] * 4
        + [anywhere],
        out_specs=anywhere,
        out_shape=jax.ShapeDtypeStruct(out.shape, F32),
        input_output_aliases={5: 0},
        scratch_shapes=[
            pltpu.VMEM((2, mpo_count, 2, rows, width), F32),
            pltpu.SemaphoreType.DMA((2, mpo_count, 2)),
        ],
        compiler_params=pltpu.CompilerParams(vmem_limit_bytes=VMEM_BYTES),
        cost_estimate=LIGHT,
        name="finish_last",
    )(pick, *part, out)


def after(value, *earlier):
    return lax.optimization_barrier((value,) + earlier)[0]


def swap(value):
    return lax.ppermute(value, "depth", [(0, 1), (1, 0)])


def split_inputs(environment, mpo):
    depth = lax.axis_index("depth")
    w_local, half = environment.shape[0], environment.shape[3]
    cols = half // 2
    env_own = lax.dynamic_slice_in_dim(environment, depth * cols, cols, 3)
    env_sib = swap(lax.dynamic_slice_in_dim(environment, (1 - depth) * cols, cols, 3))
    mpo_mine = jnp.concatenate(
        [
            lax.dynamic_slice_in_dim(mpo, depth * w_local, w_local, 0),
            lax.dynamic_slice_in_dim(mpo, (1 - depth) * w_local, w_local, 0),
        ],
        axis=0,
    )
    return env_own, env_sib, mpo_mine


def one_product(left, right, dims):
    return jnp.einsum(dims, left, right, preferred_element_type=F32)


def any_line(environment, site_tensor, mpo):
    depth = lax.axis_index("depth")
    env_own, env_sib, mpo_mine = split_inputs(environment, mpo)
    env_own = lax.all_gather(env_own, "row", axis=2, tiled=True)
    env_sib = lax.all_gather(env_sib, "row", axis=2, tiled=True)
    env = jnp.concatenate([env_own, env_sib], axis=0)
    cols = env.shape[3]
    planar = jnp.transpose(site_tensor, (0, 2, 1, 3))
    site_own = lax.dynamic_slice_in_dim(planar, depth * cols, cols, 3)
    site = lax.all_gather(planar, "col", axis=3, tiled=True)
    first = functools.partial(one_product, dims="sxa,wac->wsxc")
    g = jnp.stack(
        [
            first(site[:, 0], env[:, 0]) + first(site[:, 1], env[:, 1]),
            first(site[:, 0], env[:, 1]) - first(site[:, 1], env[:, 0]),
        ],
        axis=2,
    )
    q = jnp.einsum("wvst,wspxc->vtpxc", mpo_mine, g, precision=lax.Precision.HIGHEST).astype(BF16)
    site = lax.all_gather(site_own, "row", axis=2, tiled=True)
    second = functools.partial(one_product, dims="vtxc,tyc->vxy")
    total = jnp.stack(
        [
            second(q[:, :, 0], site[:, 0]) - second(q[:, :, 1], site[:, 1]),
            second(q[:, :, 0], site[:, 1]) + second(q[:, :, 1], site[:, 0]),
        ],
        axis=1,
    )
    return lax.psum_scatter(total, ("col", "depth"), scatter_dimension=3, tiled=True)


def ring(environment, site_tensor, mpo):
    row_count, col_count = lax.axis_size("row"), lax.axis_size("col")
    row, col, depth = (lax.axis_index(axis) for axis in ("row", "col", "depth"))
    axes = ("row", "col", "depth")
    place = lambda r, c, d: (r * col_count + c) * 2 + d
    shift = lambda value: lax.ppermute(
        value, "row", [(r, (r + 1) % row_count) for r in range(row_count)]
    )
    turn = lambda value: lax.ppermute(value, "col", [(0, 1), (1, 0)])
    in_order = lambda mine, sibling, axis: jnp.where(
        depth == 0,
        jnp.concatenate([mine, sibling], axis=axis),
        jnp.concatenate([sibling, mine], axis=axis),
    )

    env_own, env_sib, mpo_mine = split_inputs(environment, mpo)
    envs = [env_own, env_sib]
    for _ in range(row_count - 1):
        envs += [shift(envs[-2]), shift(envs[-1])]

    planar = jnp.transpose(after(site_tensor, env_sib), (0, 2, 1, 3))
    rows = planar.shape[2]
    half = rows // 2
    mine = lax.dynamic_slice_in_dim(planar, depth * half, half, 2)
    other = turn(mine)
    other = in_order(other, swap(after(other, envs[3], envs[4])), 2)
    site = jnp.where(col == 0, jnp.stack([planar, other]), jnp.stack([other, planar]))

    parts = [mine[:, :, : half // 2], mine[:, :, half // 2 :]]
    travelling = [[shift(after(part, env, site)) for part, env in zip(parts, envs[-2:])]]
    for _ in range(row_count - 2):
        travelling.append([shift(part) for part in travelling[-1]])

    blocks = jnp.stack([lax.rem(row - k + row_count, row_count) for k in range(row_count)])
    blocks = blocks.astype(jnp.int32)
    q = first_product(blocks, mpo_mine, site, envs, half, half)
    q_sib = swap(after(q, *travelling[0]))

    goals = [
        [((r - step) % row_count // 2, (r - step) % row_count % 2) for r in range(row_count)]
        for step in range(row_count)
    ]
    pick = depth.astype(jnp.int32).reshape(1)

    def second(sites, *earlier, vmem_bytes=VMEM_BYTES):
        return second_product(after(pick, *earlier), q, q_sib, sites, vmem_bytes)

    def turn_to_goal(value, goal):
        return lax.ppermute(
            value,
            axes,
            [(place(r, 1 - c, d), place(r, c, d)) for r, (c, _) in enumerate(goal) for d in range(2)],
        )

    def send(value, goal, turned, crossed):
        return lax.ppermute(
            value,
            axes,
            [
                (place(r, 1 - c if turned else c, 1 - d if crossed else d), place(r, c, d))
                for r, (c, d) in enumerate(goal)
            ],
        )

    step_of = lambda d: lax.rem(row - col * 2 - d + row_count, row_count)
    lows = [second(parts)]
    turned = [turn_to_goal(lows[0], goals[0])]
    lows.append(second(travelling[0], lows[0], travelling[1][0]))
    turned.append(turn_to_goal(lows[1], goals[1]))
    lows.append(second(travelling[1], lows[1], turned[0]))
    turned.append(turn_to_goal(lows[2], goals[2]))
    totals = [low.astype(F32) + came.astype(F32) for low, came in zip(lows, turned)]

    def total_at(step):
        return jnp.where(step == 0, totals[0], jnp.where(step == 1, totals[1], totals[2]))

    def last_part(number, *earlier):
        vmem_bytes = VMEM_BYTES if number else ALL_VMEM_BYTES
        low = second([travelling[2][number]], *earlier, vmem_bytes=vmem_bytes)
        ways = ((True, False), (True, True), (False, True))
        return [low] + [send(low, goals[3], *way) for way in ways]

    last = [last_part(0, lows[2])]
    mine, siblings = total_at(step_of(depth)), total_at(step_of(1 - depth)).astype(BF16)
    last.append(last_part(1, *last[0], mine, siblings))
    siblings = swap(siblings)
    came_last = (step_of(depth) == row_count - 1).astype(jnp.int32)
    pick = jnp.stack([came_last, depth.astype(jnp.int32)])
    out = finish(after(pick, last[1][0]), mine, siblings, last[0])
    return finish_last(pick, out, last[1])


def solution(mesh):
    placed = (
        P(("groups", "depth"), None, "row", "col"),
        P("groups", "row", None, "col"),
        P("groups", None, None, None),
    )
    fits = mesh.shape["col"] == 2 and mesh.shape["row"] == 2 * mesh.shape["col"]
    return jax.shard_map(
        ring if fits else any_line,
        mesh=mesh,
        in_specs=placed,
        out_specs=P("groups", None, "row", ("col", "depth")),
        check_vma=False,
    )
```

```python
import functools
import jax
import jax.numpy as jnp
from jax import lax
from jax.experimental import pallas as pl
from jax.experimental.pallas import tpu as pltpu
from jax.sharding import PartitionSpec as P

F32 = jnp.float32
BF16 = jnp.bfloat16
VMEM_BYTES = 40 * 1024 * 1024
LIGHT = pl.CostEstimate(flops=0, bytes_accessed=0, transcendentals=0)


def params(steps):
    return pltpu.CompilerParams(
        dimension_semantics=("arbitrary",) * steps, vmem_limit_bytes=VMEM_BYTES
    )


def mul(left, right):
    return jnp.dot(left, right, preferred_element_type=F32)


def mul_t(left, right):
    return lax.dot_general(left, right, (((1,), (1,)), ((), ())), preferred_element_type=F32)


def first_kernel(w_local, block_ref, mpo_ref, site_ref, *refs):
    q_ref, g_ref = refs[-2:]
    env_refs = refs[:-2]
    mpo_count, phys, _, rows, _ = q_ref.shape
    depth = env_refs[0].shape[2]
    per_col = site_ref.shape[-1] // depth
    for which in range(2):
        for w in range(w_local):
            with_real, with_imag = None, None
            for number in range(len(env_refs) // 2):
                block = block_ref[number]
                piece = pl.ds(pl.multiple_of((block % per_col) * depth, depth), depth)
                left = site_ref[block // per_col, :, :, :, piece].reshape(phys * 2 * rows, depth)
                env_ref = env_refs[number * 2 + which]
                more_real, more_imag = mul(left, env_ref[w, 0]), mul(left, env_ref[w, 1])
                with_real = more_real if with_real is None else with_real + more_real
                with_imag = more_imag if with_imag is None else with_imag + more_imag
            for s in range(phys):
                real, imag = (slice((2 * s + part) * rows, (2 * s + part + 1) * rows) for part in range(2))
                there = slice(s * rows, (s + 1) * rows)
                g_ref[which * w_local + w, 0, there] = with_real[real] + with_imag[imag]
                g_ref[which * w_local + w, 1, there] = with_imag[real] - with_real[imag]
    for part in range(2):
        for v in range(mpo_count):
            for t in range(phys):
                total = None
                for w in range(2 * w_local):
                    for s in range(phys):
                        term = mpo_ref[w, v, s, t] * g_ref[w, part, s * rows : (s + 1) * rows]
                        total = term if total is None else total + term
                q_ref[v, t, part] = total.astype(BF16)


def first_product(blocks, mpo, site, envs, row_tile, col_tile):
    col_count, phys, _, rows, wide = site.shape
    w_local, _, depth, cols = envs[0].shape
    mpo_count = mpo.shape[1]
    smem = pl.BlockSpec(memory_space=pltpu.SMEM)
    return pl.pallas_call(
        functools.partial(first_kernel, w_local),
        grid=(rows // row_tile, cols // col_tile),
        in_specs=[
            smem,
            smem,
            pl.BlockSpec((col_count, phys, 2, row_tile, wide), lambda i, j: (0, 0, 0, i, 0)),
        ]
        + [pl.BlockSpec((w_local, 2, depth, col_tile), lambda i, j: (0, 0, 0, j))] * len(envs),
        out_specs=pl.BlockSpec((mpo_count, phys, 2, row_tile, col_tile), lambda i, j: (0, 0, 0, i, j)),
        out_shape=jax.ShapeDtypeStruct((mpo_count, phys, 2, rows, cols), BF16),
        scratch_shapes=[pltpu.VMEM((2 * w_local, 2, phys * row_tile, col_tile), F32)],
        compiler_params=params(2),
        cost_estimate=LIGHT,
        name="first_product",
    )(blocks, mpo, site, *envs)


def second_kernel(pick_ref, own_ref, sib_ref, *refs):
    site_refs, out_ref = refs[:-1], refs[-1]
    phys, _, rows, cols = own_ref.shape[1:]
    total = None
    for q_ref, quarter in ((own_ref, pick_ref[0]), (sib_ref, 1 - pick_ref[0])):
        piece = pl.ds(pl.multiple_of(quarter * cols, cols), cols)
        for t in range(phys):
            right = [site_ref[t, part, :, piece] for part in range(2) for site_ref in site_refs]
            more = mul_t(q_ref[0, t].reshape(2 * rows, cols), jnp.concatenate(right, axis=0))
            total = more if total is None else total + more
    width = total.shape[1] // 2
    out_ref[0, 0] = (total[:rows, :width] - total[rows:, width:]).astype(BF16)
    out_ref[0, 1] = (total[:rows, width:] + total[rows:, :width]).astype(BF16)


def second_product(pick, own, sib, sites):
    mpo_count, phys, _, rows, cols = own.shape
    y_rows = sum(site.shape[2] for site in sites)
    q_spec = pl.BlockSpec((1, phys, 2, rows, cols), lambda v: (v, 0, 0, 0, 0))
    return pl.pallas_call(
        second_kernel,
        grid=(mpo_count,),
        in_specs=[pl.BlockSpec(memory_space=pltpu.SMEM), q_spec, q_spec]
        + [pl.BlockSpec(site.shape, lambda v: (0, 0, 0, 0)) for site in sites],
        out_specs=pl.BlockSpec((1, 2, rows, y_rows), lambda v: (v, 0, 0, 0)),
        out_shape=jax.ShapeDtypeStruct((mpo_count, 2, rows, y_rows), BF16),
        compiler_params=params(1),
        cost_estimate=LIGHT,
        name="second_product",
    )(pick, own, sib, *sites)


def finish_kernel(pick_ref, mine_ref, siblings_ref, *refs):
    out_ref = refs[-1]
    half = mine_ref.shape[3]
    halves = [pl.multiple_of(core * half, half) for core in (pick_ref[1], 1 - pick_ref[1])]

    @pl.when(pick_ref[0] == 0)
    def _():
        for ref, first in zip((mine_ref, siblings_ref), halves):
            out_ref[0, 0, :, pl.ds(first, half)] = ref[0, 0].astype(F32)

    @pl.when(pick_ref[0] != 0)
    def _():
        for side, first in enumerate(halves):
            one, two = refs[2 * side : 2 * side + 2]
            place = pl.ds(first, one.shape[3])
            out_ref[0, 0, :, place] = one[0, 0].astype(F32) + two[0, 0].astype(F32)


def finish(pick, mine, siblings, part):
    mpo_count, _, rows, half = mine.shape

    def spec(value, used):
        def index(v, p, pick):
            wanted = (pick[0] == used).astype(jnp.int32)
            return (v * wanted, p * wanted, 0, 0)

        return pl.BlockSpec((1, 1) + value.shape[2:], index)

    return pl.pallas_call(
        finish_kernel,
        grid_spec=pltpu.PrefetchScalarGridSpec(
            num_scalar_prefetch=1,
            grid=(mpo_count, 2),
            in_specs=[spec(mine, 0), spec(siblings, 0)] + [spec(value, 1) for value in part],
            out_specs=pl.BlockSpec((1, 1, rows, 2 * half), lambda v, p, pick: (v, p, 0, 0)),
        ),
        out_shape=jax.ShapeDtypeStruct((mpo_count, 2, rows, 2 * half), F32),
        compiler_params=params(2),
        cost_estimate=LIGHT,
        name="finish",
    )(pick, mine, siblings, *part)


def finish_last_kernel(pick_ref, *refs):
    part, (_, out_ref, sum_ref, sems) = refs[:4], refs[4:]
    mpo_count, _, _, width = part[0].shape
    half = out_ref.shape[3] // 2

    @pl.when(pick_ref[0] != 0)
    def _():
        copies = []
        for v in range(mpo_count):
            for p in range(2):
                for side, core in enumerate((pick_ref[1], 1 - pick_ref[1])):
                    one, two = part[2 * side : 2 * side + 2]
                    sum_ref[side, v, p] = one[v, p].astype(F32) + two[v, p].astype(F32)
                    place = pl.ds(pl.multiple_of(core * half + half - width, width), width)
                    copies.append(
                        pltpu.make_async_copy(
                            sum_ref.at[side, v, p], out_ref.at[v, p, :, place], sems.at[side, v, p]
                        )
                    )
                    copies[-1].start()
        for copy in copies:
            copy.wait()


def finish_last(pick, out, part):
    mpo_count, _, rows, width = part[0].shape
    anywhere = pl.BlockSpec(memory_space=pl.ANY)
    return pl.pallas_call(
        finish_last_kernel,
        in_specs=[pl.BlockSpec(memory_space=pltpu.SMEM)]
        + [pl.BlockSpec(memory_space=pltpu.VMEM)] * 4
        + [anywhere],
        out_specs=anywhere,
        out_shape=jax.ShapeDtypeStruct(out.shape, F32),
        input_output_aliases={5: 0},
        scratch_shapes=[
            pltpu.VMEM((2, mpo_count, 2, rows, width), F32),
            pltpu.SemaphoreType.DMA((2, mpo_count, 2)),
        ],
        compiler_params=pltpu.CompilerParams(vmem_limit_bytes=VMEM_BYTES),
        cost_estimate=LIGHT,
        name="finish_last",
    )(pick, *part, out)


def after(value, *earlier):
    return lax.optimization_barrier((value,) + earlier)[0]


def swap(value):
    return lax.ppermute(value, "depth", [(0, 1), (1, 0)])


def split_inputs(environment, mpo):
    depth = lax.axis_index("depth")
    w_local, half = environment.shape[0], environment.shape[3]
    cols = half // 2
    env_own = lax.dynamic_slice_in_dim(environment, depth * cols, cols, 3)
    env_sib = swap(lax.dynamic_slice_in_dim(environment, (1 - depth) * cols, cols, 3))
    mpo_mine = jnp.concatenate(
        [
            lax.dynamic_slice_in_dim(mpo, depth * w_local, w_local, 0),
            lax.dynamic_slice_in_dim(mpo, (1 - depth) * w_local, w_local, 0),
        ],
        axis=0,
    )
    return env_own, env_sib, mpo_mine


def one_product(left, right, dims):
    return jnp.einsum(dims, left, right, preferred_element_type=F32)


def any_line(environment, site_tensor, mpo):
    depth = lax.axis_index("depth")
    env_own, env_sib, mpo_mine = split_inputs(environment, mpo)
    env_own = lax.all_gather(env_own, "row", axis=2, tiled=True)
    env_sib = lax.all_gather(env_sib, "row", axis=2, tiled=True)
    env = jnp.concatenate([env_own, env_sib], axis=0)
    cols = env.shape[3]
    planar = jnp.transpose(site_tensor, (0, 2, 1, 3))
    site_own = lax.dynamic_slice_in_dim(planar, depth * cols, cols, 3)
    site = lax.all_gather(planar, "col", axis=3, tiled=True)
    first = functools.partial(one_product, dims="sxa,wac->wsxc")
    g = jnp.stack(
        [
            first(site[:, 0], env[:, 0]) + first(site[:, 1], env[:, 1]),
            first(site[:, 0], env[:, 1]) - first(site[:, 1], env[:, 0]),
        ],
        axis=2,
    )
    q = jnp.einsum("wvst,wspxc->vtpxc", mpo_mine, g, precision=lax.Precision.HIGHEST).astype(BF16)
    site = lax.all_gather(site_own, "row", axis=2, tiled=True)
    second = functools.partial(one_product, dims="vtxc,tyc->vxy")
    total = jnp.stack(
        [
            second(q[:, :, 0], site[:, 0]) - second(q[:, :, 1], site[:, 1]),
            second(q[:, :, 0], site[:, 1]) + second(q[:, :, 1], site[:, 0]),
        ],
        axis=1,
    )
    return lax.psum_scatter(total, ("col", "depth"), scatter_dimension=3, tiled=True)


def ring(environment, site_tensor, mpo):
    row_count, col_count = lax.axis_size("row"), lax.axis_size("col")
    row, col, depth = (lax.axis_index(axis) for axis in ("row", "col", "depth"))
    axes = ("row", "col", "depth")
    place = lambda r, c, d: (r * col_count + c) * 2 + d
    shift = lambda value: lax.ppermute(
        value, "row", [(r, (r + 1) % row_count) for r in range(row_count)]
    )
    turn = lambda value: lax.ppermute(value, "col", [(0, 1), (1, 0)])
    in_order = lambda mine, sibling, axis: jnp.where(
        depth == 0,
        jnp.concatenate([mine, sibling], axis=axis),
        jnp.concatenate([sibling, mine], axis=axis),
    )

    env_own, env_sib, mpo_mine = split_inputs(environment, mpo)
    envs = [env_own, env_sib]
    for _ in range(row_count - 1):
        envs += [shift(envs[-2]), shift(envs[-1])]

    planar = jnp.transpose(after(site_tensor, env_sib), (0, 2, 1, 3))
    rows = planar.shape[2]
    half = rows // 2
    mine = lax.dynamic_slice_in_dim(planar, depth * half, half, 2)
    other = turn(mine)
    other = in_order(other, swap(after(other, envs[6], envs[7])), 2)
    site = jnp.where(col == 0, jnp.stack([planar, other]), jnp.stack([other, planar]))

    parts = [mine[:, :, : half // 2], mine[:, :, half // 2 :]]
    travelling = [[shift(after(part, env)) for part, env in zip(parts, envs[-2:])]]
    for _ in range(row_count - 2):
        travelling.append([shift(part) for part in travelling[-1]])

    blocks = jnp.stack([lax.rem(row - k + row_count, row_count) for k in range(row_count)])
    blocks = blocks.astype(jnp.int32)
    q = first_product(blocks, mpo_mine, site, envs, half, half)
    q_sib = swap(after(q, *travelling[0]))

    goals = [
        [((r - step) % row_count // 2, (r - step) % row_count % 2) for r in range(row_count)]
        for step in range(row_count)
    ]
    pick = depth.astype(jnp.int32).reshape(1)

    def second(sites, *earlier):
        return second_product(after(pick, *earlier), q, q_sib, sites)

    def turn_to_goal(value, goal):
        return lax.ppermute(
            value,
            axes,
            [(place(r, 1 - c, d), place(r, c, d)) for r, (c, _) in enumerate(goal) for d in range(2)],
        )

    def send(value, goal, turned, crossed):
        return lax.ppermute(
            value,
            axes,
            [
                (place(r, 1 - c if turned else c, 1 - d if crossed else d), place(r, c, d))
                for r, (c, d) in enumerate(goal)
            ],
        )

    step_of = lambda d: lax.rem(row - col * 2 - d + row_count, row_count)
    lows = [second(parts)]
    turned = [turn_to_goal(lows[0], goals[0])]
    lows.append(second(travelling[0], lows[0], travelling[1][0]))
    turned.append(turn_to_goal(lows[1], goals[1]))
    lows.append(second(travelling[1], lows[1], turned[0]))
    turned.append(turn_to_goal(lows[2], goals[2]))
    totals = [low.astype(F32) + came.astype(F32) for low, came in zip(lows, turned)]

    def total_at(step):
        return jnp.where(step == 0, totals[0], jnp.where(step == 1, totals[1], totals[2]))

    def last_part(number, *earlier):
        low = second([travelling[2][number]], *earlier)
        ways = ((True, False), (True, True), (False, True))
        return [low] + [send(low, goals[3], *way) for way in ways]

    last = [last_part(0, lows[2])]
    mine, siblings = total_at(step_of(depth)), total_at(step_of(1 - depth)).astype(BF16)
    last.append(last_part(1, *last[0], mine, siblings))
    siblings = swap(siblings)
    came_last = (step_of(depth) == row_count - 1).astype(jnp.int32)
    pick = jnp.stack([came_last, depth.astype(jnp.int32)])
    out = finish(after(pick, last[1][0]), mine, siblings, last[0])
    return finish_last(pick, out, last[1])


def solution(mesh):
    placed = (
        P(("groups", "depth"), None, "row", "col"),
        P("groups", "row", None, "col"),
        P("groups", None, None, None),
    )
    fits = mesh.shape["col"] == 2 and mesh.shape["row"] == 2 * mesh.shape["col"]
    return jax.shard_map(
        ring if fits else any_line,
        mesh=mesh,
        in_specs=placed,
        out_specs=P("groups", None, "row", ("col", "depth")),
        check_vma=False,
    )
```

```python
import functools
import jax
import jax.numpy as jnp
from jax import lax
from jax.experimental import pallas as pl
from jax.experimental.pallas import tpu as pltpu
from jax.sharding import PartitionSpec as P

F32 = jnp.float32
BF16 = jnp.bfloat16
VMEM_BYTES = 40 * 1024 * 1024
LIGHT = pl.CostEstimate(flops=0, bytes_accessed=0, transcendentals=0)


def params(steps):
    return pltpu.CompilerParams(
        dimension_semantics=("arbitrary",) * steps, vmem_limit_bytes=VMEM_BYTES
    )


def mul(left, right):
    return jnp.dot(left, right, preferred_element_type=F32)


def mul_t(left, right):
    return lax.dot_general(left, right, (((1,), (1,)), ((), ())), preferred_element_type=F32)


def first_kernel(w_local, block_ref, mpo_ref, site_ref, *refs):
    q_ref, g_ref = refs[-2:]
    env_refs = refs[:-2]
    mpo_count, phys, _, rows, _ = q_ref.shape
    depth = env_refs[0].shape[2]
    per_col = site_ref.shape[-1] // depth
    for which in range(2):
        for w in range(w_local):
            with_real, with_imag = None, None
            for number in range(len(env_refs) // 2):
                block = block_ref[number]
                piece = pl.ds(pl.multiple_of((block % per_col) * depth, depth), depth)
                left = site_ref[block // per_col, :, :, :, piece].reshape(phys * 2 * rows, depth)
                env_ref = env_refs[number * 2 + which]
                more_real, more_imag = mul(left, env_ref[w, 0]), mul(left, env_ref[w, 1])
                with_real = more_real if with_real is None else with_real + more_real
                with_imag = more_imag if with_imag is None else with_imag + more_imag
            for s in range(phys):
                real, imag = (slice((2 * s + part) * rows, (2 * s + part + 1) * rows) for part in range(2))
                there = slice(s * rows, (s + 1) * rows)
                g_ref[which * w_local + w, 0, there] = with_real[real] + with_imag[imag]
                g_ref[which * w_local + w, 1, there] = with_imag[real] - with_real[imag]
    for part in range(2):
        for v in range(mpo_count):
            for t in range(phys):
                total = None
                for w in range(2 * w_local):
                    for s in range(phys):
                        term = mpo_ref[w, v, s, t] * g_ref[w, part, s * rows : (s + 1) * rows]
                        total = term if total is None else total + term
                q_ref[v, t, part] = total.astype(BF16)


def first_product(blocks, mpo, site, envs, row_tile, col_tile):
    col_count, phys, _, rows, wide = site.shape
    w_local, _, depth, cols = envs[0].shape
    mpo_count = mpo.shape[1]
    smem = pl.BlockSpec(memory_space=pltpu.SMEM)
    return pl.pallas_call(
        functools.partial(first_kernel, w_local),
        grid=(rows // row_tile, cols // col_tile),
        in_specs=[
            smem,
            smem,
            pl.BlockSpec((col_count, phys, 2, row_tile, wide), lambda i, j: (0, 0, 0, i, 0)),
        ]
        + [pl.BlockSpec((w_local, 2, depth, col_tile), lambda i, j: (0, 0, 0, j))] * len(envs),
        out_specs=pl.BlockSpec((mpo_count, phys, 2, row_tile, col_tile), lambda i, j: (0, 0, 0, i, j)),
        out_shape=jax.ShapeDtypeStruct((mpo_count, phys, 2, rows, cols), BF16),
        scratch_shapes=[pltpu.VMEM((2 * w_local, 2, phys * row_tile, col_tile), F32)],
        compiler_params=params(2),
        cost_estimate=LIGHT,
        name="first_product",
    )(blocks, mpo, site, *envs)


def second_kernel(pick_ref, own_ref, sib_ref, *refs):
    site_refs, out_ref = refs[:-1], refs[-1]
    phys, _, rows, cols = own_ref.shape[1:]
    total = None
    for q_ref, quarter in ((own_ref, pick_ref[0]), (sib_ref, 1 - pick_ref[0])):
        piece = pl.ds(pl.multiple_of(quarter * cols, cols), cols)
        for t in range(phys):
            right = [site_ref[t, part, :, piece] for part in range(2) for site_ref in site_refs]
            more = mul_t(q_ref[0, t].reshape(2 * rows, cols), jnp.concatenate(right, axis=0))
            total = more if total is None else total + more
    width = total.shape[1] // 2
    out_ref[0, 0] = (total[:rows, :width] - total[rows:, width:]).astype(BF16)
    out_ref[0, 1] = (total[:rows, width:] + total[rows:, :width]).astype(BF16)


def second_product(pick, own, sib, sites):
    mpo_count, phys, _, rows, cols = own.shape
    y_rows = sum(site.shape[2] for site in sites)
    q_spec = pl.BlockSpec((1, phys, 2, rows, cols), lambda v: (v, 0, 0, 0, 0))
    return pl.pallas_call(
        second_kernel,
        grid=(mpo_count,),
        in_specs=[pl.BlockSpec(memory_space=pltpu.SMEM), q_spec, q_spec]
        + [pl.BlockSpec(site.shape, lambda v: (0, 0, 0, 0)) for site in sites],
        out_specs=pl.BlockSpec((1, 2, rows, y_rows), lambda v: (v, 0, 0, 0)),
        out_shape=jax.ShapeDtypeStruct((mpo_count, 2, rows, y_rows), BF16),
        compiler_params=params(1),
        cost_estimate=LIGHT,
        name="second_product",
    )(pick, own, sib, *sites)


def finish_kernel(pick_ref, mine_ref, siblings_ref, *refs):
    out_ref = refs[-1]
    half = mine_ref.shape[3]
    halves = [pl.multiple_of(core * half, half) for core in (pick_ref[1], 1 - pick_ref[1])]

    @pl.when(pick_ref[0] == 0)
    def _():
        for ref, first in zip((mine_ref, siblings_ref), halves):
            out_ref[0, 0, :, pl.ds(first, half)] = ref[0, 0].astype(F32)

    @pl.when(pick_ref[0] != 0)
    def _():
        for side, first in enumerate(halves):
            one, two = refs[2 * side : 2 * side + 2]
            place = pl.ds(first, one.shape[3])
            out_ref[0, 0, :, place] = one[0, 0].astype(F32) + two[0, 0].astype(F32)


def finish(pick, mine, siblings, part):
    mpo_count, _, rows, half = mine.shape

    def spec(value, used):
        def index(v, p, pick):
            wanted = (pick[0] == used).astype(jnp.int32)
            return (v * wanted, p * wanted, 0, 0)

        return pl.BlockSpec((1, 1) + value.shape[2:], index)

    return pl.pallas_call(
        finish_kernel,
        grid_spec=pltpu.PrefetchScalarGridSpec(
            num_scalar_prefetch=1,
            grid=(mpo_count, 2),
            in_specs=[spec(mine, 0), spec(siblings, 0)] + [spec(value, 1) for value in part],
            out_specs=pl.BlockSpec((1, 1, rows, 2 * half), lambda v, p, pick: (v, p, 0, 0)),
        ),
        out_shape=jax.ShapeDtypeStruct((mpo_count, 2, rows, 2 * half), F32),
        compiler_params=params(2),
        cost_estimate=LIGHT,
        name="finish",
    )(pick, mine, siblings, *part)


def finish_last_kernel(pick_ref, *refs):
    part, (_, out_ref, sum_ref, sems) = refs[:4], refs[4:]
    mpo_count, _, _, width = part[0].shape
    half = out_ref.shape[3] // 2

    @pl.when(pick_ref[0] != 0)
    def _():
        copies = []
        for v in range(mpo_count):
            for p in range(2):
                for side, core in enumerate((pick_ref[1], 1 - pick_ref[1])):
                    one, two = part[2 * side : 2 * side + 2]
                    sum_ref[side, v, p] = one[v, p].astype(F32) + two[v, p].astype(F32)
                    place = pl.ds(pl.multiple_of(core * half + half - width, width), width)
                    copies.append(
                        pltpu.make_async_copy(
                            sum_ref.at[side, v, p], out_ref.at[v, p, :, place], sems.at[side, v, p]
                        )
                    )
                    copies[-1].start()
        for copy in copies:
            copy.wait()


def finish_last(pick, out, part):
    mpo_count, _, rows, width = part[0].shape
    anywhere = pl.BlockSpec(memory_space=pl.ANY)
    return pl.pallas_call(
        finish_last_kernel,
        in_specs=[pl.BlockSpec(memory_space=pltpu.SMEM)]
        + [pl.BlockSpec(memory_space=pltpu.VMEM)] * 4
        + [anywhere],
        out_specs=anywhere,
        out_shape=jax.ShapeDtypeStruct(out.shape, F32),
        input_output_aliases={5: 0},
        scratch_shapes=[
            pltpu.VMEM((2, mpo_count, 2, rows, width), F32),
            pltpu.SemaphoreType.DMA((2, mpo_count, 2)),
        ],
        compiler_params=pltpu.CompilerParams(vmem_limit_bytes=VMEM_BYTES),
        cost_estimate=LIGHT,
        name="finish_last",
    )(pick, *part, out)


def after(value, *earlier):
    return lax.optimization_barrier((value,) + earlier)[0]


def swap(value):
    return lax.ppermute(value, "depth", [(0, 1), (1, 0)])


def split_inputs(environment, mpo):
    depth = lax.axis_index("depth")
    w_local, half = environment.shape[0], environment.shape[3]
    cols = half // 2
    env_own = lax.dynamic_slice_in_dim(environment, depth * cols, cols, 3)
    env_sib = swap(lax.dynamic_slice_in_dim(environment, (1 - depth) * cols, cols, 3))
    mpo_mine = jnp.concatenate(
        [
            lax.dynamic_slice_in_dim(mpo, depth * w_local, w_local, 0),
            lax.dynamic_slice_in_dim(mpo, (1 - depth) * w_local, w_local, 0),
        ],
        axis=0,
    )
    return env_own, env_sib, mpo_mine


def one_product(left, right, dims):
    return jnp.einsum(dims, left, right, preferred_element_type=F32)


def any_line(environment, site_tensor, mpo):
    depth = lax.axis_index("depth")
    env_own, env_sib, mpo_mine = split_inputs(environment, mpo)
    env_own = lax.all_gather(env_own, "row", axis=2, tiled=True)
    env_sib = lax.all_gather(env_sib, "row", axis=2, tiled=True)
    env = jnp.concatenate([env_own, env_sib], axis=0)
    cols = env.shape[3]
    planar = jnp.transpose(site_tensor, (0, 2, 1, 3))
    site_own = lax.dynamic_slice_in_dim(planar, depth * cols, cols, 3)
    site = lax.all_gather(planar, "col", axis=3, tiled=True)
    first = functools.partial(one_product, dims="sxa,wac->wsxc")
    g = jnp.stack(
        [
            first(site[:, 0], env[:, 0]) + first(site[:, 1], env[:, 1]),
            first(site[:, 0], env[:, 1]) - first(site[:, 1], env[:, 0]),
        ],
        axis=2,
    )
    q = jnp.einsum("wvst,wspxc->vtpxc", mpo_mine, g, precision=lax.Precision.HIGHEST).astype(BF16)
    site = lax.all_gather(site_own, "row", axis=2, tiled=True)
    second = functools.partial(one_product, dims="vtxc,tyc->vxy")
    total = jnp.stack(
        [
            second(q[:, :, 0], site[:, 0]) - second(q[:, :, 1], site[:, 1]),
            second(q[:, :, 0], site[:, 1]) + second(q[:, :, 1], site[:, 0]),
        ],
        axis=1,
    )
    return lax.psum_scatter(total, ("col", "depth"), scatter_dimension=3, tiled=True)


def ring(environment, site_tensor, mpo):
    row_count, col_count = lax.axis_size("row"), lax.axis_size("col")
    row, col, depth = (lax.axis_index(axis) for axis in ("row", "col", "depth"))
    axes = ("row", "col", "depth")
    place = lambda r, c, d: (r * col_count + c) * 2 + d
    shift = lambda value: lax.ppermute(
        value, "row", [(r, (r + 1) % row_count) for r in range(row_count)]
    )
    turn = lambda value: lax.ppermute(value, "col", [(0, 1), (1, 0)])
    in_order = lambda mine, sibling, axis: jnp.where(
        depth == 0,
        jnp.concatenate([mine, sibling], axis=axis),
        jnp.concatenate([sibling, mine], axis=axis),
    )

    env_own, env_sib, mpo_mine = split_inputs(environment, mpo)
    envs = [env_own, env_sib]
    for _ in range(row_count - 1):
        envs += [shift(envs[-2]), shift(envs[-1])]

    planar = jnp.transpose(after(site_tensor, env_sib), (0, 2, 1, 3))
    rows = planar.shape[2]
    half = rows // 2
    mine = lax.dynamic_slice_in_dim(planar, depth * half, half, 2)
    other = turn(mine)
    other = in_order(other, swap(after(other, envs[5], envs[6])), 2)
    site = jnp.where(col == 0, jnp.stack([planar, other]), jnp.stack([other, planar]))

    parts = [mine[:, :, : half // 2], mine[:, :, half // 2 :]]
    travelling = [[shift(after(part, env)) for part, env in zip(parts, envs[-2:])]]
    for _ in range(row_count - 2):
        travelling.append([shift(part) for part in travelling[-1]])

    blocks = jnp.stack([lax.rem(row - k + row_count, row_count) for k in range(row_count)])
    blocks = blocks.astype(jnp.int32)
    q = first_product(blocks, mpo_mine, site, envs, half, half)
    q_sib = swap(after(q, *travelling[0]))

    goals = [
        [((r - step) % row_count // 2, (r - step) % row_count % 2) for r in range(row_count)]
        for step in range(row_count)
    ]
    pick = depth.astype(jnp.int32).reshape(1)

    def second(sites, *earlier):
        return second_product(after(pick, *earlier), q, q_sib, sites)

    def turn_to_goal(value, goal):
        return lax.ppermute(
            value,
            axes,
            [(place(r, 1 - c, d), place(r, c, d)) for r, (c, _) in enumerate(goal) for d in range(2)],
        )

    def send(value, goal, turned, crossed):
        return lax.ppermute(
            value,
            axes,
            [
                (place(r, 1 - c if turned else c, 1 - d if crossed else d), place(r, c, d))
                for r, (c, d) in enumerate(goal)
            ],
        )

    step_of = lambda d: lax.rem(row - col * 2 - d + row_count, row_count)
    lows = [second(parts)]
    turned = [turn_to_goal(lows[0], goals[0])]
    lows.append(second(travelling[0], lows[0], travelling[1][0]))
    turned.append(turn_to_goal(lows[1], goals[1]))
    lows.append(second(travelling[1], lows[1], turned[0]))
    turned.append(turn_to_goal(lows[2], goals[2]))
    totals = [low.astype(F32) + came.astype(F32) for low, came in zip(lows, turned)]

    def total_at(step):
        return jnp.where(step == 0, totals[0], jnp.where(step == 1, totals[1], totals[2]))

    def last_part(number, *earlier):
        low = second([travelling[2][number]], *earlier)
        ways = ((True, False), (True, True), (False, True))
        return [low] + [send(low, goals[3], *way) for way in ways]

    last = [last_part(0, lows[2])]
    mine, siblings = total_at(step_of(depth)), total_at(step_of(1 - depth)).astype(BF16)
    last.append(last_part(1, *last[0], mine, siblings))
    siblings = swap(siblings)
    came_last = (step_of(depth) == row_count - 1).astype(jnp.int32)
    pick = jnp.stack([came_last, depth.astype(jnp.int32)])
    out = finish(after(pick, last[1][0]), mine, siblings, last[0])
    return finish_last(pick, out, last[1])


def solution(mesh):
    placed = (
        P(("groups", "depth"), None, "row", "col"),
        P("groups", "row", None, "col"),
        P("groups", None, None, None),
    )
    fits = mesh.shape["col"] == 2 and mesh.shape["row"] == 2 * mesh.shape["col"]
    return jax.shard_map(
        ring if fits else any_line,
        mesh=mesh,
        in_specs=placed,
        out_specs=P("groups", None, "row", ("col", "depth")),
        check_vma=False,
    )
```
